32 devices in a mesh: dp: 2 (over x), expert: 4 (over y, core), shard: 4 (over z).
Axes of the slice: x: 2, y: 2, z: 4, core: 2. Of those that a mesh axis runs over, the one named last changes fastest.
Arguments:
- tokens: bfloat16 [16, 1024, 1536], P(('expert', 'shard'), 'dp'), may hold values from -6 to 6
- cotangent: bfloat16 [16, 1024, 1536], P(('expert', 'shard'), 'dp'), may hold values from -6 to 6
- gain_attn: float32 [1536], replicated, may hold values from 0.1 to 1.9
- w_query: bfloat16 [1536, 1536], P('shard')
- key_weight: bfloat16 [1536, 512], P('shard'), may hold values from -0.15625 to 0.15625
- value_weight: bfloat16 [1536, 512], P('shard'), may hold values from -0.15625 to 0.15625
- w_output: bfloat16 [1536, 1536], P('shard'), may hold values from -2 to 2
- gain_ffn: float32 [1536], replicated, may hold values from 0.1 to 1.9
- w_router: bfloat16 [1536, 32], replicated, may hold values from -0.076171875 to 0.076171875
- expert_in: bfloat16 [32, 1536, 1024], P(('expert', 'shard')), may hold values from -0.15625 to 0.15625
- expert_out: bfloat16 [32, 512, 1536], P(('expert', 'shard')), may hold values from -1 to 1
- routes: int32 [16, 1024, 8], P(('expert', 'shard'), 'dp'), may hold values from 0 to 31, all different within a row; in each aligned block of 512 rows (0 to 511, 512 to 1023, ..., all dimensions but the last counted through in order) at most 256 rows name the same one
- doc_ids: int32 [16, 1024], P(('expert', 'shard'), 'dp'), may hold values from 0 to 2, as said below
- threshold: int32 [1], replicated, may hold values from 1 to 3
Outputs:
- out: bfloat16 [16, 1024, 1536], P(('expert', 'shard'), 'dp')
- grad_tokens: bfloat16 [16, 1024, 1536], P(('expert', 'shard'), 'dp')
- grad_gain_attn: float32 [1536], P(('dp', 'expert', 'shard'))
- grad_query: float32 [1536, 1536], P(('dp', 'expert', 'shard'))
- grad_key: float32 [1536, 512], P(('dp', 'expert', 'shard'))
- grad_value: float32 [1536, 512], P(('dp', 'expert', 'shard'))
- grad_output: float32 [1536, 1536], P(('dp', 'expert', 'shard'))
- grad_gain_ffn: float32 [1536], P(('dp', 'expert', 'shard'))
- grad_router: float32 [1536, 32], P(('dp', 'expert', 'shard'))
- grad_expert_in: float32 [32, 1536, 1024], P(('expert', 'shard'), 'dp')
- grad_expert_out: float32 [32, 512, 1536], P(('expert', 'shard'), 'dp')
- largest_logits: float32 [24], replicated
- clipped_query: bfloat16 [1536, 1536], P('shard')
- clipped_key: bfloat16 [1536, 512], P('shard')
The draws below stay inside these ranges and needn't reach their ends.
Inputs may be any that keep to these rules, and one draw needn't show every extreme that they name: `routes`: on the rows of one device no expert is named more than 256 times; the 8 ids of a token differ. `doc_ids`: each sequence holds three documents, numbered 0, 1, 2 in order of position; document 1 starts after position 0 and within the first 256 positions, document 2 starts within the last 256 positions and after the first of them.
All inputs are finite; a program needn't handle non-finite values.
Results may differ from the reference program's by a relative error of at most 0.018.
The reference program's roundings to bfloat16 on the way count: a program that leaves them out, or rounds other values in their place, can miss the bound.
Values may be sent and summed in bfloat16 or wider, within the bound.
A program may use at most 320 MiB of HBM per device.

```python
import math
import jax
import jax.numpy as jnp
import numpy as np
from jax import lax

MODEL_DIM = 1536
QUERY_HEADS = 24
KEY_VALUE_HEADS = 8
HEAD_DIM = 64
FFE = 512
TOP = 8
SEQUENCE_TOKENS = 1024
TOK_DEV = 512
SEQS = 16
EXPERTS = 32
CAP = 256


def draw_w_query(key, part):
    key = jax.random.fold_in(key, 11)
    scale_key, value_key = jax.random.split(key)
    head_scale = jnp.exp(jax.random.uniform(scale_key, (QUERY_HEADS,), jnp.float32, 0.0, 0.9162907))
    base = jax.random.normal(value_key, (MODEL_DIM, QUERY_HEADS, HEAD_DIM), jnp.float32)
    return (base * head_scale[None, :, None] * MODEL_DIM ** (-0.5)).reshape(MODEL_DIM, QUERY_HEADS * HEAD_DIM).astype(jnp.bfloat16)


def draw_doc_ids(key, part):
    key = jax.random.fold_in(key, 23)
    start_key, end_key = jax.random.split(key)
    half_rows = max(TOK_DEV // 2, 2)
    first_start = jax.random.randint(start_key, (SEQS, 1), 1, half_rows)
    last_start = jax.random.randint(end_key, (SEQS, 1), SEQUENCE_TOKENS - half_rows + 1, SEQUENCE_TOKENS)
    positions = jnp.arange(SEQUENCE_TOKENS)[None, :]
    after_first = (positions >= first_start).astype(jnp.int32)
    after_last = (positions >= last_start).astype(jnp.int32)
    return after_first + after_last


def block_levels(key, dims, pieces, least, top_value):
    factor_of = 1.0
    for axis_at, shards_of in pieces:
        heights = jax.random.uniform(jax.random.fold_in(jax.random.fold_in(key, 6), axis_at), (shards_of,), jnp.float32, least / len(pieces), top_value / len(pieces))
        factor_of = factor_of * jnp.repeat(jnp.exp(heights), dims[axis_at] // shards_of).reshape((-1,) + (1,) * (len(dims) - 1 - axis_at))
    return factor_of


def routed_block(stream_key, own, number, rows, count, top, limit, slope):
    order = jax.random.permutation(stream_key, count)
    packed, ordinary = load_shares(count, rows * top, limit, slope, True), load_shares(count, rows * top, limit, slope, False)
    places = jnp.arange(count)

    def named(lengths, rotation):
        used = int((lengths > 0).sum())
        fixed = max(1, used // 4)
        moved = fixed + (places - fixed + rotation * (used - fixed)) % max(1, count - fixed)
        return jnp.zeros((count,), jnp.int32).at[order[jnp.where(places < fixed, places, moved)]].set(jnp.asarray(lengths, jnp.int32))

    lengths = jnp.where(number % 4 == 0, named(packed, number // 4), named(ordinary, number - number // 4 - 1))
    mixed = jax.random.permutation(jax.random.fold_in(own, 3), count)
    source_of, receiver = mixed[0:count // 2 * 2:2], mixed[1:count // 2 * 2:2]
    slack = jnp.minimum(lengths[source_of] - 1, limit - lengths[receiver]) // 2
    slack = jnp.where((source_of == order[0]) | (receiver == order[0]) | (lengths[receiver] == 0), 0, jnp.maximum(slack, 0))
    moved = jax.random.randint(jax.random.fold_in(own, 4), (count // 2,), 0, 1 << 20) % (slack + 1)
    lengths = lengths.at[source_of].add(-moved).at[receiver].add(moved)
    members = jnp.searchsorted(jnp.cumsum(lengths), jnp.arange(rows * top), side="right").astype(jnp.int32)
    table = members.reshape(top, rows).T
    table = table[jax.random.permutation(jax.random.fold_in(own, 1), rows)]
    rotation = jax.random.randint(jax.random.fold_in(own, 2), (rows, 1), 0, top)
    return jnp.take_along_axis(table, (jnp.arange(top)[None, :] + rotation) % top, axis=1)


def load_shares(number_of, total, reach, skew, full):
    weights = [(1 << 20) // math.isqrt(grade ** skew) + 1 for grade in range(1, number_of + 1)]
    largest = reach if full else min(reach, max(-(-total // number_of), total * weights[0] // sum(weights)))
    least = 1 if total - largest >= number_of - 1 else 0
    counts, spare = [largest] + [least] * (number_of - 1), total - largest - least * (number_of - 1)
    while spare > 0:
        free = [i for i in range(1, number_of) if counts[i] < largest] or [i for i in range(1, number_of) if counts[i] < reach]
        mass, budget = sum([weights[i] for i in free]), spare
        for i in free:
            more = min(reach - counts[i], max(1, budget * weights[i] // mass), spare)
            counts[i] = counts[i] + more
            spare = spare - more
    return np.array(counts)


def noise(stream_key, shape, width, limit, shards=(), kind=jnp.bfloat16):
    factor_of = block_levels(stream_key, shape, shards, -0.22, 0.18) if shards else 1.0
    values = jax.random.normal(stream_key, shape, jnp.float32) * width * factor_of
    return jnp.minimum(jnp.maximum(values, -limit), limit).astype(kind)


def setup_inputs(seed: int = 0) -> dict:
    seeds = jax.random.split(jax.random.key(seed), 15)
    tokens = noise(seeds[0], (SEQS, SEQUENCE_TOKENS, MODEL_DIM), 1.0, 6.0, ((0, 16), (1, 2)))
    cotangent = noise(seeds[1], (SEQS, SEQUENCE_TOKENS, MODEL_DIM), 1.0, 6.0, ((0, 16), (1, 2)))
    gain_attn = jnp.clip(1.0 + 0.18 * jax.random.normal(seeds[2], (MODEL_DIM,), jnp.float32), 0.1, 1.9)
    w_query = draw_w_query(jax.random.fold_in(seeds[14], 71), 0)
    key_weight = noise(seeds[4], (MODEL_DIM, KEY_VALUE_HEADS * HEAD_DIM), MODEL_DIM ** -0.5, 0.15625, ((0, 4),))
    value_weight = noise(seeds[5], (MODEL_DIM, KEY_VALUE_HEADS * HEAD_DIM), MODEL_DIM ** -0.5, 0.15625, ((0, 4),))
    w_output = noise(seeds[6], (MODEL_DIM, QUERY_HEADS * HEAD_DIM), (max(QUERY_HEADS // 3, 1)) ** -0.5, 2.0, ((0, 4),))
    gain_ffn = jnp.clip(1.0 + 0.18 * jax.random.normal(seeds[7], (MODEL_DIM,), jnp.float32), 0.1, 1.9)
    w_router = noise(seeds[8], (MODEL_DIM, EXPERTS), (0.5 * MODEL_DIM ** -0.5), 0.076171875)
    expert_in = noise(seeds[9], (EXPERTS, MODEL_DIM, 2 * FFE), MODEL_DIM ** -0.5, 0.15625, ((0, 16),))
    expert_out = noise(seeds[10], (EXPERTS, FFE, MODEL_DIM), (max(FFE // 16, 1)) ** -0.5, 1.0, ((0, 16),))
    routes_keys = jax.random.split(jax.random.fold_in(seeds[11], 1), SEQS * SEQUENCE_TOKENS // TOK_DEV)
    routes_turns = jax.random.permutation(jax.random.fold_in(seeds[11], 3), SEQS * SEQUENCE_TOKENS // TOK_DEV)
    routes = jax.vmap(lambda own, number: routed_block(jax.random.fold_in(seeds[11], 2), own, number, TOK_DEV, EXPERTS, TOP, CAP, 2))(routes_keys, routes_turns).reshape((SEQS, SEQUENCE_TOKENS, TOP))
    doc_ids = draw_doc_ids(jax.random.fold_in(seeds[14], 71), 0)
    threshold = jax.random.randint(seeds[13], (1,), 1, 4).astype(jnp.int32)
    return dict(tokens=tokens, cotangent=cotangent, gain_attn=gain_attn, w_query=w_query, key_weight=key_weight, value_weight=value_weight, w_output=w_output, gain_ffn=gain_ffn, w_router=w_router, expert_in=expert_in, expert_out=expert_out, routes=routes, doc_ids=doc_ids, threshold=threshold)


EPSILON = 1e-06
EXCLUDED = -1e+30
HIGH = lax.Precision.HIGHEST

@jax.custom_vjp
def reduced_precision(v):
    return lax.optimization_barrier(v.astype(jnp.bfloat16)).astype(jnp.float32)

@jax.custom_vjp
def low_back(v):
    return v

def low_keep(v):
    return (reduced_precision(v), None)

def low_pass(kept, grad):
    return (grad,)

def back_keep(v):
    return (v, None)

def back_low(kept, grad):
    return (reduced_precision(grad),)
reduced_precision.defvjp(low_keep, low_pass)
low_back.defvjp(back_keep, back_low)

def rope_tables(positions, head_size):
    half_size = head_size // 2
    frequency = jnp.exp(jnp.arange(half_size).astype(jnp.float32) * (-2.0 * math.log(10000.0) / head_size))
    angles = positions.astype(jnp.float32)[:, None] * frequency[None, :]
    return (jnp.cos(angles), jnp.sin(angles))

def apply_rotary(values, cosine_lookup, sine_lookup):
    half_size = values.shape[-1] // 2
    first_half = values[..., :half_size]
    second = values[..., half_size:]
    cosine_b = cosine_lookup[:, None, :]
    sine_b = sine_lookup[:, None, :]
    return jnp.concatenate([first_half * cosine_b - second * sine_b, second * cosine_b + first_half * sine_b], axis=-1)

def rms_scale(values):
    return lax.rsqrt(lax.optimization_barrier(jnp.mean(values * values, axis=-1, keepdims=True)) + EPSILON)

def attention_sequence(hidden_attn, w_query, key_weight, value_weight, docs):
    positions = jnp.arange(SEQUENCE_TOKENS)
    cosine_lookup, sine_lookup = rope_tables(positions, HEAD_DIM)
    query_proj = low_back(jnp.dot(hidden_attn, w_query, precision=HIGH))
    key_projected = low_back(jnp.dot(hidden_attn, key_weight, precision=HIGH))
    value_selected = low_back(reduced_precision(jnp.dot(hidden_attn, value_weight, precision=HIGH)))
    query_rotated = reduced_precision(apply_rotary(query_proj.reshape(SEQUENCE_TOKENS, QUERY_HEADS, HEAD_DIM), cosine_lookup, sine_lookup) * 0.125)
    key_rotated = reduced_precision(apply_rotary(key_projected.reshape(SEQUENCE_TOKENS, KEY_VALUE_HEADS, HEAD_DIM), cosine_lookup, sine_lookup))
    allowed = (positions[None, :] <= positions[:, None]) & (docs[None, :] == docs[:, None])
    query_per_key = QUERY_HEADS // KEY_VALUE_HEADS
    heads_of_query = query_rotated.reshape(SEQUENCE_TOKENS, KEY_VALUE_HEADS, query_per_key, HEAD_DIM).transpose(1, 2, 0, 3)
    heads_of_key = key_rotated.transpose(1, 0, 2)
    heads_of_value = value_selected.reshape(SEQUENCE_TOKENS, KEY_VALUE_HEADS, HEAD_DIM).transpose(1, 0, 2)

    def one_head(operands):
        query_group, key_group, value_group = operands
        scores = low_back(jnp.einsum('gtd,sd->gts', query_group, key_group, precision=HIGH))
        scores = jnp.where(allowed[None], scores, EXCLUDED)
        row_max = lax.optimization_barrier(jnp.max(scores, axis=-1, keepdims=True))
        exponent = jnp.exp(scores - row_max)
        attn_probs = reduced_precision(exponent / lax.optimization_barrier(jnp.sum(exponent, axis=-1, keepdims=True)))
        head_mix = jnp.einsum('gts,sd->gtd', attn_probs, value_group, precision=HIGH)
        return (head_mix, lax.optimization_barrier(jnp.max(row_max[..., 0], axis=-1)))
    head_mix, head_max = lax.map(jax.checkpoint(one_head), (heads_of_query, heads_of_key, heads_of_value))
    return (head_mix.transpose(2, 0, 1, 3).reshape(SEQUENCE_TOKENS, QUERY_HEADS * HEAD_DIM), head_max.reshape(QUERY_HEADS))

def layer_sequence(weights, inputs, route_ids, docs):
    gain_attn, w_query, key_weight, value_weight, w_output, gain_ffn, w_router, expert_in, expert_out = weights
    hidden_attn = reduced_precision(inputs * rms_scale(inputs) * gain_attn)
    attn_mix, head_max = attention_sequence(hidden_attn, w_query, key_weight, value_weight, docs)
    attn_used = low_back(reduced_precision(attn_mix))
    branch_attn = low_back(jnp.dot(attn_used, w_output.T, precision=HIGH))
    residual = inputs + branch_attn
    hidden_ffn = reduced_precision(residual * rms_scale(residual) * gain_ffn)
    router_logits = low_back(jnp.dot(hidden_ffn, w_router, precision=HIGH))
    chosen = jnp.take_along_axis(router_logits, route_ids, axis=1)
    chosen_exp = jnp.exp(chosen - lax.optimization_barrier(jnp.max(chosen, axis=-1, keepdims=True)))
    gate_weights = chosen_exp / lax.optimization_barrier(jnp.sum(chosen_exp, axis=-1, keepdims=True))
    expert_ids = jnp.arange(EXPERTS)
    picked = (route_ids[:, :, None] == expert_ids[None, None, :]).astype(jnp.float32)
    combine = lax.optimization_barrier(jnp.sum(picked * gate_weights[:, :, None], axis=1))

    def one_expert(running, operands):
        weight_in, weight_out, column = operands
        rows_in = low_back(hidden_ffn)
        gate_up = low_back(jnp.dot(rows_in, weight_in, precision=HIGH))
        gate_part = gate_up[:, :FFE]
        up_part = gate_up[:, FFE:]
        hidden_low = reduced_precision(gate_part * jax.nn.sigmoid(gate_part) * up_part)
        results = low_back(reduced_precision(jnp.dot(hidden_low, weight_out, precision=HIGH)))
        return (running + column[:, None] * results, None)
    branch_ffn, unused = lax.scan(jax.checkpoint(one_expert), jnp.zeros((SEQUENCE_TOKENS, MODEL_DIM), jnp.float32), (expert_in, expert_out, combine.T))
    return (residual + branch_ffn, head_max)

def reference(tokens, cotangent, gain_attn, w_query, key_weight, value_weight, w_output, gain_ffn, w_router, expert_in, expert_out, routes, doc_ids, threshold):
    weights = (gain_attn.astype(jnp.float32), w_query.astype(jnp.float32), key_weight.astype(jnp.float32), value_weight.astype(jnp.float32), w_output.astype(jnp.float32), gain_ffn.astype(jnp.float32), w_router.astype(jnp.float32), expert_in.astype(jnp.float32), expert_out.astype(jnp.float32))
    inputs = tokens.astype(jnp.float32)

    def forward(inputs_all, weight_set):

        def per_sequence(operands):
            return layer_sequence(weight_set, operands[0], operands[1], operands[2])
        outputs, head_max = lax.map(jax.checkpoint(per_sequence), (inputs_all, routes, doc_ids))
        return (outputs, head_max)
    outputs, pullback, head_max = jax.vjp(forward, inputs, weights, has_aux=True)
    grad_inputs, grad_weights = pullback(cotangent.astype(jnp.float32))
    largest = lax.optimization_barrier(jnp.max(head_max, axis=0))
    clip_limit = threshold[0].astype(jnp.float32)
    shrink_factor = clip_limit / jnp.maximum(largest, clip_limit)
    query_scale = jnp.repeat(jnp.sqrt(shrink_factor), HEAD_DIM)
    key_shrink = jnp.repeat(jnp.sqrt(lax.optimization_barrier(jnp.min(shrink_factor.reshape(KEY_VALUE_HEADS, QUERY_HEADS // KEY_VALUE_HEADS), axis=1))), HEAD_DIM)
    clipped_query = (w_query.astype(jnp.float32) * query_scale[None, :]).astype(jnp.bfloat16)
    clipped_key = (key_weight.astype(jnp.float32) * key_shrink[None, :]).astype(jnp.bfloat16)
    return (outputs.astype(jnp.bfloat16), grad_inputs.astype(jnp.bfloat16), grad_weights[0], grad_weights[1], grad_weights[2], grad_weights[3], grad_weights[4], grad_weights[5], grad_weights[6], grad_weights[7], grad_weights[8], largest, clipped_query, clipped_key)
```

```python
import math

import jax
import jax.numpy as jnp
from jax import lax
from jax.experimental import pallas as pl
from jax.experimental.pallas import tpu as pltpu
from jax.sharding import PartitionSpec as P

QUERY_HEADS = 24
KEY_VALUE_HEADS = 8
HEAD_DIM = 64
TOP = 8
GROUP = ("expert", "shard")
EVERY = ("dp", "expert", "shard")

EPSILON = 1e-06
EXCLUDED = -1e30


def rope_tables(positions, head_size):
    half_size = head_size // 2
    frequency = jnp.exp(
        jnp.arange(half_size).astype(jnp.float32) * (-2.0 * math.log(10000.0) / head_size)
    )
    angles = positions.astype(jnp.float32)[:, None] * frequency[None, :]
    return (jnp.cos(angles), jnp.sin(angles))


def apply_rotary(values, cosine_lookup, sine_lookup):
    half_size = values.shape[-1] // 2
    first_half = values[..., :half_size]
    second = values[..., half_size:]
    cosine_b = cosine_lookup[:, None, :]
    sine_b = sine_lookup[:, None, :]
    return jnp.concatenate(
        [first_half * cosine_b - second * sine_b, second * cosine_b + first_half * sine_b], axis=-1
    )


def rms_scale(values):
    return lax.rsqrt(jnp.mean(values * values, axis=-1, keepdims=True) + EPSILON)


def norm_back(grad_normed, normed, inv_rms, gain_vector):
    scaled = grad_normed * gain_vector
    return inv_rms * (scaled - normed * jnp.mean(scaled * normed, axis=-1, keepdims=True))


def contract_rows(left_side, right_side):
    return lax.dot_general(
        left_side, right_side, (((0,), (0,)), ((), ())), preferred_element_type=jnp.float32
    )


def contract_cols(left_side, right_side):
    return lax.dot_general(
        left_side, right_side, (((1,), (1,)), ((), ())), preferred_element_type=jnp.float32
    )


def as_column(vector, before=0):
    return jnp.pad(vector[:, None], ((0, 0), (0, 127 - before)))


def masked_softmax(logits, picked):
    kept = jnp.where(picked, logits, EXCLUDED)
    exponent = jnp.exp(kept - jnp.max(kept, axis=-1, keepdims=True))
    return exponent / jnp.sum(exponent, axis=-1, keepdims=True)


def experts_kernel(
    at_ref, routes_ref, router_ref, rows_ref, cot_ref, win_ref, wout_ref,
    out_ref, grad_ref, gates_ref, dwin_ref, dwout_ref, acc_in, acc_out,
):
    step, steps = pl.program_id(0), pl.num_programs(0)
    own_count, width = wout_ref.shape[0], wout_ref.shape[1]

    @pl.when(step == 0)
    def _():
        acc_in[...] = jnp.zeros_like(acc_in)
        acc_out[...] = jnp.zeros_like(acc_out)

    rows, cot = rows_ref[...], cot_ref[...]
    logits = jnp.dot(rows, router_ref[...], preferred_element_type=jnp.float32)
    lanes = lax.broadcasted_iota(jnp.int32, logits.shape, 1)
    picked = lanes == routes_ref[:, 0:1]
    for k in range(1, TOP):
        picked = picked | (lanes == routes_ref[:, k : k + 1])
    gates = masked_softmax(logits, picked)
    first = at_ref[0] * own_count
    out_sum = grad_sum = None
    gate_lanes = lax.broadcasted_iota(jnp.int32, gates_ref.shape, 1)
    gate_grads = jnp.zeros(gates_ref.shape, jnp.float32)
    for e in range(own_count):
        gate = jnp.sum(jnp.where(lanes == first + e, gates, 0.0), axis=1, keepdims=True)
        both = jnp.dot(rows, win_ref[e], preferred_element_type=jnp.float32)
        gate_part, up_part = both[:, :width], both[:, width:]
        sig = jax.nn.sigmoid(gate_part)
        activated = gate_part * sig
        hidden = (activated * up_part).astype(jnp.bfloat16).astype(jnp.float32)
        gated = (gate * hidden).astype(jnp.bfloat16)
        term = jnp.dot(gated, wout_ref[e], preferred_element_type=jnp.float32)
        out_sum = term if out_sum is None else out_sum + term
        plain = contract_cols(cot, wout_ref[e])
        own_grad = jnp.sum(plain * hidden, axis=1, keepdims=True)
        gate_grads = jnp.where(gate_lanes == e, own_grad, gate_grads)
        back = gate * plain
        d_gate = back * up_part * sig * (1.0 + gate_part * (1.0 - sig))
        d_up = back * activated
        d_both = jnp.concatenate([d_gate, d_up], axis=1).astype(jnp.bfloat16)
        term = contract_cols(d_both, win_ref[e])
        grad_sum = term if grad_sum is None else grad_sum + term
        acc_in[e] += contract_rows(rows, d_both)
        acc_out[e] += contract_rows(gated, cot)
    out_ref[...] = out_sum.astype(jnp.bfloat16)
    grad_ref[...] = grad_sum.astype(jnp.bfloat16)
    gates_ref[...] = gate_grads

    @pl.when(step == steps - 1)
    def _():
        dwin_ref[...] = acc_in[...].astype(jnp.bfloat16)
        dwout_ref[...] = acc_out[...].astype(jnp.bfloat16)


def experts_pass(group_at, routes, w_router, rows, cotangent, expert_in, expert_out):
    total, model = rows.shape
    tile = 256
    by_row = lambda width: pl.BlockSpec((tile, width), lambda i: (i, 0))
    whole = lambda shape: pl.BlockSpec(
        shape, lambda i: (0,) * len(shape), pipeline_mode=pl.Buffered(1)
    )
    return pl.pallas_call(
        experts_kernel,
        grid=(total // tile,),
        out_shape=(
            jax.ShapeDtypeStruct((total, model), jnp.bfloat16),
            jax.ShapeDtypeStruct((total, model), jnp.bfloat16),
            jax.ShapeDtypeStruct((total, expert_in.shape[0]), jnp.float32),
            jax.ShapeDtypeStruct(expert_in.shape, jnp.bfloat16),
            jax.ShapeDtypeStruct(expert_out.shape, jnp.bfloat16),
        ),
        in_specs=[
            pl.BlockSpec(memory_space=pltpu.SMEM),
            by_row(routes.shape[1]),
            whole(w_router.shape),
            by_row(model),
            by_row(model),
            whole(expert_in.shape),
            whole(expert_out.shape),
        ],
        out_specs=(
            by_row(model),
            by_row(model),
            by_row(expert_in.shape[0]),
            whole(expert_in.shape),
            whole(expert_out.shape),
        ),
        scratch_shapes=[
            pltpu.VMEM(expert_in.shape, jnp.float32),
            pltpu.VMEM(expert_out.shape, jnp.float32),
        ],
        compiler_params=pltpu.CompilerParams(vmem_limit_bytes=60 * 2**20),
    )(group_at[None].astype(jnp.int32), routes, w_router, rows, cotangent, expert_in, expert_out)


def on_device(
    tokens,
    cotangent,
    gain_attn,
    w_query,
    key_weight,
    value_weight,
    w_output,
    gain_ffn,
    w_router,
    expert_in,
    expert_out,
    routes,
    doc_ids,
    threshold,
):
    inputs = tokens[0].astype(jnp.float32)
    token_matrix, model_width = inputs.shape
    query_per_key = QUERY_HEADS // KEY_VALUE_HEADS
    query_width, key_width = w_query.shape[1], key_weight.shape[1]
    all_cotangent = lax.all_gather(cotangent[0], GROUP, axis=0, tiled=True)
    all_routes = lax.all_gather(routes[0], GROUP, axis=0, tiled=True)
    scale_attn = rms_scale(inputs)
    normed_attn = inputs * scale_attn
    hidden_attn = (normed_attn * gain_attn).astype(jnp.bfloat16)
    full_query, full_key, full_value, full_output = (
        lax.all_gather(w_query, "shard", axis=0, tiled=True),
        lax.all_gather(key_weight, "shard", axis=0, tiled=True),
        lax.all_gather(value_weight, "shard", axis=0, tiled=True),
        lax.all_gather(w_output, "shard", axis=0, tiled=True),
    )
    own_positions = lax.axis_index("dp") * token_matrix + jnp.arange(token_matrix)
    local_cosine, local_sine = rope_tables(own_positions, HEAD_DIM)
    query_proj = jnp.dot(hidden_attn, full_query, preferred_element_type=jnp.float32)
    key_projected = jnp.dot(hidden_attn, full_key, preferred_element_type=jnp.float32)
    value_proj = jnp.dot(hidden_attn, full_value, preferred_element_type=jnp.float32)
    query_rotated = (
        apply_rotary(
            query_proj.reshape(token_matrix, QUERY_HEADS, HEAD_DIM), local_cosine, local_sine
        )
        * 0.125
    ).astype(jnp.bfloat16)
    key_rotated = (
        apply_rotary(
            key_projected.reshape(token_matrix, KEY_VALUE_HEADS, HEAD_DIM), local_cosine, local_sine
        )
        .astype(jnp.bfloat16)
        .reshape(token_matrix, KEY_VALUE_HEADS * HEAD_DIM)
    )
    value_low = value_proj.astype(jnp.bfloat16)
    own_docs = doc_ids[0]
    gathered_keys, gathered_values, docs_all = (
        lax.all_gather(key_rotated, "dp", axis=0, tiled=True),
        lax.all_gather(value_low, "dp", axis=0, tiled=True),
        lax.all_gather(own_docs, "dp", axis=0, tiled=True),
    )
    total_keys = gathered_keys.shape[0]
    allowed = (jnp.arange(total_keys)[None, :] <= own_positions[:, None]) & (
        docs_all[None, :] == own_docs[:, None]
    )
    heads_of_query = query_rotated.reshape(
        token_matrix, KEY_VALUE_HEADS, query_per_key, HEAD_DIM
    ).transpose(1, 2, 0, 3)
    heads_of_key = gathered_keys.reshape(total_keys, KEY_VALUE_HEADS, HEAD_DIM).transpose(1, 0, 2)
    heads_of_value = gathered_values.reshape(total_keys, KEY_VALUE_HEADS, HEAD_DIM).transpose(
        1, 0, 2
    )

    def attend(operands):
        query_group, key_group, value_group = operands
        scores = jnp.einsum(
            "gtd,sd->gts", query_group, key_group, preferred_element_type=jnp.float32
        )
        scores = jnp.where(allowed[None], scores, EXCLUDED)
        row_max = jnp.max(scores, axis=-1, keepdims=True)
        exponent = jnp.exp(scores - row_max)
        totals = jnp.sum(exponent, axis=-1, keepdims=True)
        attn_probs = (exponent / totals).astype(jnp.bfloat16)
        head_mix = jnp.einsum(
            "gts,sd->gtd", attn_probs, value_group, preferred_element_type=jnp.float32
        )
        return (head_mix, (row_max + jnp.log(totals))[..., 0], jnp.max(row_max[..., 0], axis=-1))

    head_mix, log_totals, head_max = lax.map(attend, (heads_of_query, heads_of_key, heads_of_value))
    largest = lax.pmax(head_max.reshape(QUERY_HEADS), ("dp", "expert", "shard"))
    attn_low = (
        head_mix.transpose(2, 0, 1, 3)
        .reshape(token_matrix, QUERY_HEADS * HEAD_DIM)
        .astype(jnp.bfloat16)
    )
    branch_attn = contract_cols(attn_low, full_output)
    residual = inputs + branch_attn
    scale_ffn = rms_scale(residual)
    normed_ffn = residual * scale_ffn
    hidden_ffn = (normed_ffn * gain_ffn).astype(jnp.bfloat16)
    expert_count = w_router.shape[1]
    router_logits = jnp.dot(hidden_ffn, w_router, preferred_element_type=jnp.float32)
    route_ids = routes[0]
    picked = (route_ids[:, :, None] == jnp.arange(expert_count)[None, None, :]).any(axis=1)
    gate_weights = masked_softmax(router_logits, picked)
    grad_out = cotangent[0].astype(jnp.float32)
    all_hidden = lax.all_gather(hidden_ffn, GROUP, axis=0, tiled=True)
    group_at = lax.axis_index("expert") * lax.axis_size("shard") + lax.axis_index("shard")
    partial_out, partial_grad, grad_gates_own, weight_in_grad, weight_out_grad = experts_pass(
        group_at, all_routes, w_router, all_hidden, all_cotangent, expert_in, expert_out
    )
    grad_gates = (
        lax.all_to_all(
            grad_gates_own.reshape(-1, token_matrix, expert_in.shape[0]), GROUP, 0, 0, tiled=True
        )
        .transpose(1, 0, 2)
        .reshape(token_matrix, expert_count)
    )
    grad_hidden_ffn = lax.psum_scatter(
        partial_grad, GROUP, scatter_dimension=0, tiled=True
    ).astype(jnp.float32)
    branch_ffn = lax.psum_scatter(partial_out, GROUP, scatter_dimension=0, tiled=True)
    out = (residual + branch_ffn.astype(jnp.float32)).astype(jnp.bfloat16)
    grad_in_shard, grad_out_shard = (
        lax.psum_scatter(weight_in_grad, "dp", scatter_dimension=1, tiled=True).astype(jnp.float32),
        lax.psum_scatter(weight_out_grad, "dp", scatter_dimension=1, tiled=True).astype(
            jnp.float32
        ),
    )
    weighted = gate_weights * jnp.where(picked, grad_gates, 0.0)
    grad_logits = (
        weighted - gate_weights * jnp.sum(weighted, axis=-1, keepdims=True)
    ).astype(jnp.bfloat16)
    router_grad = contract_rows(hidden_ffn, grad_logits)
    grad_hidden_ffn = grad_hidden_ffn + contract_cols(grad_logits, w_router)
    gain_ffn_grad = jnp.sum(grad_hidden_ffn * normed_ffn, axis=0)
    grad_residual = grad_out + norm_back(grad_hidden_ffn, normed_ffn, scale_ffn, gain_ffn)
    grad_branch = grad_residual.astype(jnp.bfloat16)
    output_grad = contract_rows(grad_branch, attn_low)
    late_sums = lax.psum_scatter(
        jnp.concatenate(
            [output_grad, router_grad, as_column(gain_ffn_grad, expert_count)], axis=1
        ).astype(jnp.bfloat16),
        EVERY,
        scatter_dimension=0,
        tiled=True,
    ).astype(jnp.float32)
    attention_gradient = jnp.dot(
        grad_branch, full_output, preferred_element_type=jnp.float32
    ).astype(jnp.bfloat16)
    head_gradient = attention_gradient.reshape(
        token_matrix, KEY_VALUE_HEADS, query_per_key, HEAD_DIM
    ).transpose(1, 2, 0, 3)

    def attend_back(operands):
        query_group, key_group, value_group, grad_group, log_group = operands
        scores = jnp.einsum(
            "gtd,sd->gts", query_group, key_group, preferred_element_type=jnp.float32
        )
        attn_probs = jnp.where(allowed[None], jnp.exp(scores - log_group[..., None]), 0.0)
        grad_probs = jnp.einsum(
            "gtd,sd->gts", grad_group, value_group, preferred_element_type=jnp.float32
        )
        centre = jnp.sum(attn_probs * grad_probs, axis=-1, keepdims=True)
        grad_scores = (attn_probs * (grad_probs - centre)).astype(jnp.bfloat16)
        grad_query_group = jnp.einsum(
            "gts,sd->gtd", grad_scores, key_group, preferred_element_type=jnp.float32
        )
        grad_key_group = jnp.einsum(
            "gts,gtd->sd", grad_scores, query_group, preferred_element_type=jnp.float32
        )
        grad_value_group = jnp.einsum(
            "gts,gtd->sd",
            attn_probs.astype(jnp.bfloat16),
            grad_group,
            preferred_element_type=jnp.float32,
        )
        return (grad_query_group, grad_key_group, grad_value_group)

    grad_query_heads, key_head_gradient, value_head_gradient = lax.map(
        attend_back, (heads_of_query, heads_of_key, heads_of_value, head_gradient, log_totals)
    )
    complete_key_gradient = key_head_gradient.transpose(1, 0, 2).reshape(
        total_keys, KEY_VALUE_HEADS * HEAD_DIM
    )
    complete_value_gradient = value_head_gradient.transpose(1, 0, 2).reshape(
        total_keys, KEY_VALUE_HEADS * HEAD_DIM
    )
    local_key_gradient, value_grad_own = (
        lax.psum_scatter(
            complete_key_gradient.astype(jnp.bfloat16), "dp", scatter_dimension=0, tiled=True
        ).astype(jnp.float32),
        lax.psum_scatter(
            complete_value_gradient.astype(jnp.bfloat16), "dp", scatter_dimension=0, tiled=True
        ).astype(jnp.float32),
    )
    key_grad_low = (
        apply_rotary(
            local_key_gradient.reshape(token_matrix, KEY_VALUE_HEADS, HEAD_DIM),
            local_cosine,
            -local_sine,
        )
        .reshape(token_matrix, KEY_VALUE_HEADS * HEAD_DIM)
        .astype(jnp.bfloat16)
    )
    value_grad_low = value_grad_own.astype(jnp.bfloat16)
    query_grad_rows = grad_query_heads.transpose(2, 0, 1, 3).reshape(
        token_matrix, QUERY_HEADS, HEAD_DIM
    )
    query_grad_low = (
        (apply_rotary(query_grad_rows, local_cosine, -local_sine) * 0.125)
        .reshape(token_matrix, QUERY_HEADS * HEAD_DIM)
        .astype(jnp.bfloat16)
    )
    query_grad = contract_rows(hidden_attn, query_grad_low)
    key_grad = contract_rows(hidden_attn, key_grad_low)
    value_grad = contract_rows(hidden_attn, value_grad_low)
    grad_hidden_attn = (
        contract_cols(query_grad_low, full_query)
        + contract_cols(key_grad_low, full_key)
        + contract_cols(value_grad_low, full_value)
    )
    gain_attn_grad = jnp.sum(grad_hidden_attn * normed_attn, axis=0)
    grad_inputs = grad_residual + norm_back(grad_hidden_attn, normed_attn, scale_attn, gain_attn)
    attn_sums = lax.psum_scatter(
        jnp.concatenate(
            [query_grad, key_grad, value_grad, as_column(gain_attn_grad)], axis=1
        ).astype(jnp.bfloat16),
        EVERY,
        scatter_dimension=0,
        tiled=True,
    ).astype(jnp.float32)
    clip_limit = threshold[0].astype(jnp.float32)
    shrink_factor = clip_limit / jnp.maximum(largest, clip_limit)
    query_scale = jnp.repeat(jnp.sqrt(shrink_factor), HEAD_DIM)
    key_shrink = jnp.repeat(
        jnp.sqrt(jnp.min(shrink_factor.reshape(KEY_VALUE_HEADS, query_per_key), axis=1)), HEAD_DIM
    )
    clipped_query = (w_query.astype(jnp.float32) * query_scale[None, :]).astype(jnp.bfloat16)
    clipped_key = (key_weight.astype(jnp.float32) * key_shrink[None, :]).astype(jnp.bfloat16)
    return (
        out[None],
        grad_inputs.astype(jnp.bfloat16)[None],
        attn_sums[:, query_width + 2 * key_width],
        attn_sums[:, :query_width],
        attn_sums[:, query_width : query_width + key_width],
        attn_sums[:, query_width + key_width : query_width + 2 * key_width],
        late_sums[:, :query_width],
        late_sums[:, query_width + expert_count],
        late_sums[:, query_width : query_width + expert_count],
        grad_in_shard,
        grad_out_shard,
        largest,
        clipped_query,
        clipped_key,
    )


def solution(mesh):
    return jax.shard_map(
        on_device,
        mesh=mesh,
        in_specs=(
            P(("expert", "shard"), "dp", None),
            P(("expert", "shard"), "dp", None),
            P(),
            P("shard", None),
            P("shard", None),
            P("shard", None),
            P("shard", None),
            P(),
            P(),
            P(("expert", "shard"), None, None),
            P(("expert", "shard"), None, None),
            P(("expert", "shard"), "dp", None),
            P(("expert", "shard"), "dp"),
            P(),
        ),
        out_specs=(
            P(("expert", "shard"), "dp", None),
            P(("expert", "shard"), "dp", None),
            P(("dp", "expert", "shard")),
            P(("dp", "expert", "shard"), None),
            P(("dp", "expert", "shard"), None),
            P(("dp", "expert", "shard"), None),
            P(("dp", "expert", "shard"), None),
            P(("dp", "expert", "shard")),
            P(("dp", "expert", "shard"), None),
            P(("expert", "shard"), "dp", None),
            P(("expert", "shard"), "dp", None),
            P(),
            P("shard", None),
            P("shard", None),
        ),
        check_vma=False,
    )
```

```python
import math

import jax
import jax.numpy as jnp
from jax import lax
from jax.experimental import pallas as pl
from jax.experimental.pallas import tpu as pltpu
from jax.sharding import PartitionSpec as P

QUERY_HEADS = 24
KEY_VALUE_HEADS = 8
HEAD_DIM = 64
TOP = 8
GROUP = ("expert", "shard")
EVERY = ("dp", "expert", "shard")

EPSILON = 1e-06
EXCLUDED = -1e30


def rope_tables(positions, head_size):
    half_size = head_size // 2
    frequency = jnp.exp(
        jnp.arange(half_size).astype(jnp.float32) * (-2.0 * math.log(10000.0) / head_size)
    )
    angles = positions.astype(jnp.float32)[:, None] * frequency[None, :]
    return (jnp.cos(angles), jnp.sin(angles))


def apply_rotary(values, cosine_lookup, sine_lookup):
    half_size = values.shape[-1] // 2
    first_half = values[..., :half_size]
    second = values[..., half_size:]
    cosine_b = cosine_lookup[:, None, :]
    sine_b = sine_lookup[:, None, :]
    return jnp.concatenate(
        [first_half * cosine_b - second * sine_b, second * cosine_b + first_half * sine_b], axis=-1
    )


def rms_scale(values):
    return lax.rsqrt(jnp.mean(values * values, axis=-1, keepdims=True) + EPSILON)


def norm_back(grad_normed, normed, inv_rms, gain_vector):
    scaled = grad_normed * gain_vector
    return inv_rms * (scaled - normed * jnp.mean(scaled * normed, axis=-1, keepdims=True))


def contract_rows(left_side, right_side):
    return lax.dot_general(
        left_side, right_side, (((0,), (0,)), ((), ())), preferred_element_type=jnp.float32
    )


def contract_cols(left_side, right_side):
    return lax.dot_general(
        left_side, right_side, (((1,), (1,)), ((), ())), preferred_element_type=jnp.float32
    )


def as_column(vector, before=0):
    return jnp.pad(vector[:, None], ((0, 0), (0, 127 - before)))


def masked_softmax(logits, picked):
    kept = jnp.where(picked, logits, EXCLUDED)
    exponent = jnp.exp(kept - jnp.max(kept, axis=-1, keepdims=True))
    return exponent / jnp.sum(exponent, axis=-1, keepdims=True)


def experts_kernel(
    hidden_ref, cot_ref, routes_ref, router_ref, win_ref, wout_ref,
    rows_ref, kept_ref, core_ref, across_ref, line_ref, stage_ref, dwin_ref, dwout_ref,
    acc_in, acc_out, win, wout, router, row_tile, cot_tile, route_tile, made, parts,
    load_sem, tile_sem, row_recv, core_send, across_send, line_send,
    made_sem, part_sem, core_recv, across_recv, line_recv, stage_sem, stage_send, store_sem,
):
    own_count, width = wout_ref.shape[0], wout_ref.shape[1]
    rows_own, model = hidden_ref.shape
    tile = rows_own // 2
    expert, depth = lax.axis_index("expert"), lax.axis_index("shard")
    side, core = expert // 2, expert % 2
    sibling = {"expert": 2 * side + (core + 1) % 2}
    opposite = {"expert": 2 * ((side + 1) % 2) + core}

    def along(distance):
        return {"shard": (depth + distance) % 4}

    def remote(src, dst, send, recv, to):
        return pltpu.make_async_remote_copy(
            src_ref=src, dst_ref=dst, send_sem=send, recv_sem=recv, device_id=to,
            device_id_type=pl.DeviceIdType.MESH,
        )

    barrier = pltpu.get_barrier_semaphore()
    for peer in (sibling, opposite, along(1), along(2), along(3)):
        pl.semaphore_signal(barrier, inc=1, device_id=peer, device_id_type=pl.DeviceIdType.MESH)
    pl.semaphore_wait(barrier, 5)

    loads = [
        pltpu.make_async_copy(win_ref, win, load_sem.at[0]),
        pltpu.make_async_copy(wout_ref, wout, load_sem.at[1]),
        pltpu.make_async_copy(router_ref, router, load_sem.at[2]),
    ]

    def to_sibling(src, r):
        return remote(src, rows_ref.at[r + 1], core_send.at[r // 2], row_recv.at[r + 1], sibling)

    def to_opposite(src, r):
        return remote(src, rows_ref.at[r + 2], across_send.at[r // 4], row_recv.at[r + 2], opposite)

    def to_line(zi):
        return remote(
            hidden_ref, rows_ref.at[4 * zi], line_send.at[zi], row_recv.at[4 * zi], along(4 - zi)
        )

    def own_rows():
        return pltpu.make_async_copy(hidden_ref, rows_ref.at[0], row_recv.at[0])

    to_sibling(hidden_ref, 0).start()
    to_opposite(hidden_ref, 0).start()
    for zi in range(1, 4):
        to_line(zi).start()
    own_rows().start()
    for load in loads:
        load.start()

    def arrive(r):
        @pl.when(r == 0)
        def _():
            own_rows().wait()

        @pl.when(r > 0)
        def _():
            remote(
                rows_ref.at[r], rows_ref.at[r], core_send.at[0], row_recv.at[r], sibling
            ).wait_recv()

            @pl.when(r % 2 == 0)
            def _():
                to_sibling(rows_ref.at[r], r).start()

            @pl.when(r % 4 == 0)
            def _():
                to_opposite(rows_ref.at[r], r).start()

    def block_at(step):
        turn = (step // 2 + 1) // 2
        place = (turn + 7) % 8
        return 4 * ((place + place // 4) % 4) + 2 * (1 - place // 4) + (step // 2 + 1) % 2

    def tiles(step):
        r, sub, slot = block_at(step), step % 2, step % 2
        other = 2 * ((side + (r % 4) // 2) % 2) + (core + r) % 2
        start = (other * 4 + (depth + r // 4) % 4) * rows_own + sub * tile
        start = pl.multiple_of(start, tile)
        return (
            pltpu.make_async_copy(
                rows_ref.at[r, pl.ds(pl.multiple_of(sub * tile, tile), tile)],
                row_tile.at[slot], tile_sem.at[0, slot],
            ),
            pltpu.make_async_copy(
                cot_ref.at[pl.ds(start, tile)], cot_tile.at[slot], tile_sem.at[1, slot]
            ),
            pltpu.make_async_copy(
                routes_ref.at[pl.ds(start, tile)], route_tile.at[slot], tile_sem.at[2, slot]
            ),
        )

    acc_in[...] = jnp.zeros_like(acc_in)
    acc_out[...] = jnp.zeros_like(acc_out)
    arrive(1)
    for copy in tiles(0):
        copy.start()
    for load in loads:
        load.wait()

    def send_made(step):
        r, sub, slot = block_at(step), step % 2, step % 2
        return remote(
            made.at[slot], core_ref.at[r // 2, sub], made_sem.at[slot],
            core_recv.at[r // 2, sub], sibling,
        )

    def keep_made(step):
        r, sub, slot = block_at(step), step % 2, step % 2
        return pltpu.make_async_copy(made.at[slot], kept_ref.at[r // 2, sub], made_sem.at[slot])

    def made_done(step):
        away = (step // 2 + 1) % 2

        @pl.when(away == 1)
        def _():
            send_made(step).wait_send()

        @pl.when(away == 0)
        def _():
            keep_made(step).wait()

    def send_y(zi, sub):
        return remote(
            stage_ref.at[zi, sub], across_ref.at[zi, sub], stage_send.at[zi, sub],
            across_recv.at[zi, sub], opposite,
        )

    def send_z(zi, sub):
        return remote(
            stage_ref.at[3 + zi, sub], line_ref.at[zi, sub], stage_send.at[3 + zi, sub],
            line_recv.at[zi, sub], along(zi),
        )

    def staged(place, sub):
        return pltpu.make_async_copy(parts.at[0], stage_ref.at[place, sub], stage_sem.at[0])

    def load_kept(pair, sub):
        return pltpu.make_async_copy(kept_ref.at[pair, sub], parts.at[0], part_sem.at[0])

    def load_core(pair, sub):
        return pltpu.make_async_copy(core_ref.at[pair, sub], parts.at[1], part_sem.at[1])

    def load_across(zi, sub):
        return pltpu.make_async_copy(across_ref.at[zi, sub], parts.at[2], part_sem.at[2])

    def core_arrived(pair, sub):
        remote(
            made.at[0], core_ref.at[pair, sub], made_sem.at[0], core_recv.at[pair, sub], sibling
        ).wait_recv()

    def begin_y(zi, sub):
        core_arrived(2 * zi + 1, sub)
        load_kept(2 * zi + 1, sub).start()
        load_core(2 * zi + 1, sub).start()

    def end_y(zi, sub):
        load_kept(2 * zi + 1, sub).wait()
        load_core(2 * zi + 1, sub).wait()
        parts[0] = (parts[0].astype(jnp.float32) + parts[1].astype(jnp.float32)).astype(
            jnp.bfloat16
        )
        staged(zi, sub).start()

    def begin_z(zi, sub):
        core_arrived(2 * zi, sub)
        send_y(zi, sub).wait_recv()
        load_kept(2 * zi, sub).start()
        load_core(2 * zi, sub).start()
        load_across(zi, sub).start()

    def end_z(zi, sub):
        load_kept(2 * zi, sub).wait()
        load_core(2 * zi, sub).wait()
        load_across(zi, sub).wait()
        parts[0] = (
            parts[0].astype(jnp.float32) + parts[1].astype(jnp.float32) + parts[2].astype(jnp.float32)
        ).astype(jnp.bfloat16)
        staged(3 + zi, sub).start()

    first = (expert * 4 + depth) * own_count

    def body(step, carry):
        slot, sub = step % 2, step % 2
        stage_y = (step >= 10) & (step < 24) & (step % 4 >= 2)
        zi_y = (step // 4 - 1) % 4
        stage_z = (step == 24) | (step == 25) | (step >= 30)
        zi_z = 1 + (step - 24) // 6
        for copy in tiles(step):
            copy.wait()

        @pl.when(step < 31)
        def _():
            after = block_at(step + 1)

            @pl.when((step % 2 == 1) & ((after % 4 != 0) | (after == 0)))
            def _():
                arrive(after)

            for early, r in ((2, 4), (6, 8), (10, 12)):
                @pl.when(step == early)
                def _():
                    arrive(jnp.int32(r))

            for copy in tiles(step + 1):
                copy.start()

        before_y = (step >= 11) & (step < 25) & ((step - 1) % 4 >= 2)
        before_z = (step == 25) | (step == 26) | (step == 31)

        @pl.when(before_y)
        def _():
            zi = ((step - 1) // 4 - 1) % 4
            staged(zi, 1 - sub).wait()
            send_y(zi, 1 - sub).start()

        @pl.when(before_z)
        def _():
            zi = 1 + (step - 25) // 6
            staged(3 + zi, 1 - sub).wait()
            send_z(zi, 1 - sub).start()

        @pl.when(stage_y)
        def _():
            begin_y(zi_y, sub)

        @pl.when(stage_z)
        def _():
            begin_z(zi_z, sub)

        @pl.when(step >= 2)
        def _():
            made_done(step - 2)

        rows, cot = row_tile[slot], cot_tile[slot]
        logits = jnp.dot(rows, router[...], preferred_element_type=jnp.float32)
        lanes = lax.broadcasted_iota(jnp.int32, logits.shape, 1)
        routes = route_tile[slot]
        picked = lanes == routes[:, 0:1]
        for k in range(1, TOP):
            picked = picked | (lanes == routes[:, k : k + 1])
        gates = masked_softmax(logits, picked)
        out_sum = grad_sum = None
        gate_lanes = lax.broadcasted_iota(jnp.int32, (tile, 128), 1)
        gate_grads = jnp.zeros((tile, 128), jnp.float32)
        for e in range(own_count):
            gate = jnp.sum(jnp.where(lanes == first + e, gates, 0.0), axis=1, keepdims=True)
            both = jnp.dot(rows, win[e], preferred_element_type=jnp.float32)
            gate_part, up_part = both[:, :width], both[:, width:]
            sig = jax.nn.sigmoid(gate_part)
            activated = gate_part * sig
            hidden = (activated * up_part).astype(jnp.bfloat16).astype(jnp.float32)
            gated = (gate * hidden).astype(jnp.bfloat16)
            term = jnp.dot(gated, wout[e], preferred_element_type=jnp.float32)
            out_sum = term if out_sum is None else out_sum + term
            plain = contract_cols(cot, wout[e])
            own_grad = jnp.sum(plain * hidden, axis=1, keepdims=True)
            high = own_grad.astype(jnp.bfloat16).astype(jnp.float32)
            gate_grads = jnp.where(gate_lanes == first + e, high, gate_grads)
            gate_grads = jnp.where(gate_lanes == 64 + first + e, own_grad - high, gate_grads)
            back = gate * plain
            d_gate = back * up_part * sig * (1.0 + gate_part * (1.0 - sig))
            d_up = back * activated
            d_both = jnp.concatenate([d_gate, d_up], axis=1).astype(jnp.bfloat16)
            term = contract_cols(d_both, win[e])
            grad_sum = term if grad_sum is None else grad_sum + term
            acc_in[e] += contract_rows(rows, d_both)
            acc_out[e] += contract_rows(gated, cot)
        made[slot, :, :model] = grad_sum.astype(jnp.bfloat16)
        made[slot, :, model : 2 * model] = out_sum.astype(jnp.bfloat16)
        made[slot, :, 2 * model :] = gate_grads.astype(jnp.bfloat16)

        away = (step // 2 + 1) % 2

        @pl.when(away == 1)
        def _():
            send_made(step).start()

        @pl.when(away == 0)
        def _():
            keep_made(step).start()

        @pl.when(stage_y)
        def _():
            end_y(zi_y, sub)

        @pl.when(stage_z)
        def _():
            end_z(zi_z, sub)

        return carry

    lax.fori_loop(0, 32, body, 0)
    stores = [
        pltpu.make_async_copy(acc_in, dwin_ref, store_sem.at[0]),
        pltpu.make_async_copy(acc_out, dwout_ref, store_sem.at[1]),
    ]
    for store in stores:
        store.start()
    staged(5, 1).wait()
    send_z(2, 1).start()
    for sub in range(2):
        begin_z(3, sub)
        end_z(3, sub)
        staged(6, sub).wait()
        send_z(3, sub).start()
    made_done(30)
    made_done(31)
    for sub in range(2):
        core_arrived(0, sub)
        send_y(0, sub).wait_recv()
        for zi in range(4):
            send_y(zi, sub).wait_send()
        for zi in range(1, 4):
            send_z(zi, sub).wait_send()
            send_z(zi, sub).wait_recv()
    for r in range(0, 16, 2):
        to_sibling(hidden_ref, r).wait_send()
    for r in range(0, 16, 4):
        to_opposite(hidden_ref, r).wait_send()
    for zi in range(1, 4):
        to_line(zi).wait_send()
    for store in stores:
        store.wait()


def experts_pass(hidden, cotangent, routes, w_router, expert_in, expert_out):
    rows_own, model = hidden.shape
    tile = rows_own // 2
    wide = 2 * model + 128
    anywhere = pl.BlockSpec(memory_space=pl.ANY)
    low = jnp.bfloat16
    kept = jax.ShapeDtypeStruct((8, 2, tile, wide), low)
    quarter = jax.ShapeDtypeStruct((4, 2, tile, wide), low)
    dma = pltpu.SemaphoreType.DMA
    results = pl.pallas_call(
        experts_kernel,
        out_shape=(
            jax.ShapeDtypeStruct((16, rows_own, model), low),
            kept,
            kept,
            quarter,
            quarter,
            jax.ShapeDtypeStruct((7, 2, tile, wide), low),
            jax.ShapeDtypeStruct(expert_in.shape, jnp.float32),
            jax.ShapeDtypeStruct(expert_out.shape, jnp.float32),
        ),
        in_specs=[anywhere] * 6,
        out_specs=(anywhere,) * 8,
        scratch_shapes=[
            pltpu.VMEM(expert_in.shape, jnp.float32),
            pltpu.VMEM(expert_out.shape, jnp.float32),
            pltpu.VMEM(expert_in.shape, low),
            pltpu.VMEM(expert_out.shape, low),
            pltpu.VMEM(w_router.shape, low),
            pltpu.VMEM((2, tile, model), low),
            pltpu.VMEM((2, tile, model), low),
            pltpu.VMEM((2, tile, routes.shape[1]), jnp.int32),
            pltpu.VMEM((2, tile, wide), low),
            pltpu.VMEM((3, tile, wide), low),
            dma((3,)), dma((3, 2)), dma((16,)), dma((8,)), dma((4,)), dma((4,)),
            dma((2,)), dma((3,)), dma((8, 2)), dma((4, 2)), dma((4, 2)), dma((1,)), dma((7, 2)), dma((2,)),
        ],
        compiler_params=pltpu.CompilerParams(
            collective_id=0, has_side_effects=True, vmem_limit_bytes=60 * 2**20
        ),
    )(hidden, cotangent, routes, w_router, expert_in, expert_out)
    _, kept, core, across, line, _, weight_in_grad, weight_out_grad = results
    total = kept[0].astype(jnp.float32) + core[0].astype(jnp.float32)
    total = total + across[0].astype(jnp.float32)
    for zi in range(1, 4):
        total = total + line[zi].astype(jnp.float32)
    return total.reshape(rows_own, wide), weight_in_grad, weight_out_grad


def on_device(
    tokens,
    cotangent,
    gain_attn,
    w_query,
    key_weight,
    value_weight,
    w_output,
    gain_ffn,
    w_router,
    expert_in,
    expert_out,
    routes,
    doc_ids,
    threshold,
):
    inputs = tokens[0].astype(jnp.float32)
    token_matrix, model_width = inputs.shape
    query_per_key = QUERY_HEADS // KEY_VALUE_HEADS
    query_width, key_width = w_query.shape[1], key_weight.shape[1]
    all_cotangent = lax.all_gather(cotangent[0], GROUP, axis=0, tiled=True)
    all_routes = lax.all_gather(routes[0], GROUP, axis=0, tiled=True)
    scale_attn = rms_scale(inputs)
    normed_attn = inputs * scale_attn
    hidden_attn = (normed_attn * gain_attn).astype(jnp.bfloat16)
    full_query, full_key, full_value, full_output = (
        lax.all_gather(w_query, "shard", axis=0, tiled=True),
        lax.all_gather(key_weight, "shard", axis=0, tiled=True),
        lax.all_gather(value_weight, "shard", axis=0, tiled=True),
        lax.all_gather(w_output, "shard", axis=0, tiled=True),
    )
    own_positions = lax.axis_index("dp") * token_matrix + jnp.arange(token_matrix)
    local_cosine, local_sine = rope_tables(own_positions, HEAD_DIM)
    query_proj = jnp.dot(hidden_attn, full_query, preferred_element_type=jnp.float32)
    key_projected = jnp.dot(hidden_attn, full_key, preferred_element_type=jnp.float32)
    value_proj = jnp.dot(hidden_attn, full_value, preferred_element_type=jnp.float32)
    query_rotated = (
        apply_rotary(
            query_proj.reshape(token_matrix, QUERY_HEADS, HEAD_DIM), local_cosine, local_sine
        )
        * 0.125
    ).astype(jnp.bfloat16)
    key_rotated = (
        apply_rotary(
            key_projected.reshape(token_matrix, KEY_VALUE_HEADS, HEAD_DIM), local_cosine, local_sine
        )
        .astype(jnp.bfloat16)
        .reshape(token_matrix, KEY_VALUE_HEADS * HEAD_DIM)
    )
    value_low = value_proj.astype(jnp.bfloat16)
    own_docs = doc_ids[0]
    gathered_keys, gathered_values, docs_all = (
        lax.all_gather(key_rotated, "dp", axis=0, tiled=True),
        lax.all_gather(value_low, "dp", axis=0, tiled=True),
        lax.all_gather(own_docs, "dp", axis=0, tiled=True),
    )
    total_keys = gathered_keys.shape[0]
    allowed = (jnp.arange(total_keys)[None, :] <= own_positions[:, None]) & (
        docs_all[None, :] == own_docs[:, None]
    )
    heads_of_query = query_rotated.reshape(
        token_matrix, KEY_VALUE_HEADS, query_per_key, HEAD_DIM
    ).transpose(1, 2, 0, 3)
    heads_of_key = gathered_keys.reshape(total_keys, KEY_VALUE_HEADS, HEAD_DIM).transpose(1, 0, 2)
    heads_of_value = gathered_values.reshape(total_keys, KEY_VALUE_HEADS, HEAD_DIM).transpose(
        1, 0, 2
    )

    def attend(operands):
        query_group, key_group, value_group = operands
        scores = jnp.einsum(
            "gtd,sd->gts", query_group, key_group, preferred_element_type=jnp.float32
        )
        scores = jnp.where(allowed[None], scores, EXCLUDED)
        row_max = jnp.max(scores, axis=-1, keepdims=True)
        exponent = jnp.exp(scores - row_max)
        totals = jnp.sum(exponent, axis=-1, keepdims=True)
        attn_probs = (exponent / totals).astype(jnp.bfloat16)
        head_mix = jnp.einsum(
            "gts,sd->gtd", attn_probs, value_group, preferred_element_type=jnp.float32
        )
        return (head_mix, (row_max + jnp.log(totals))[..., 0], jnp.max(row_max[..., 0], axis=-1))

    head_mix, log_totals, head_max = lax.map(attend, (heads_of_query, heads_of_key, heads_of_value))
    largest = lax.pmax(head_max.reshape(QUERY_HEADS), ("dp", "expert", "shard"))
    attn_low = (
        head_mix.transpose(2, 0, 1, 3)
        .reshape(token_matrix, QUERY_HEADS * HEAD_DIM)
        .astype(jnp.bfloat16)
    )
    branch_attn = contract_cols(attn_low, full_output)
    residual = inputs + branch_attn
    scale_ffn = rms_scale(residual)
    normed_ffn = residual * scale_ffn
    hidden_ffn = (normed_ffn * gain_ffn).astype(jnp.bfloat16)
    expert_count = w_router.shape[1]
    router_logits = jnp.dot(hidden_ffn, w_router, preferred_element_type=jnp.float32)
    route_ids = routes[0]
    picked = (route_ids[:, :, None] == jnp.arange(expert_count)[None, None, :]).any(axis=1)
    gate_weights = masked_softmax(router_logits, picked)
    grad_out = cotangent[0].astype(jnp.float32)
    summed, weight_in_grad, weight_out_grad = experts_pass(
        hidden_ffn, all_cotangent, all_routes, w_router, expert_in, expert_out
    )
    model = hidden_ffn.shape[1]
    grad_hidden_ffn = summed[:, :model]
    out = (residual + summed[:, model : 2 * model]).astype(jnp.bfloat16)
    gate_cols = summed[:, 2 * model :]
    grad_gates = gate_cols[:, :expert_count] + gate_cols[:, 64 : 64 + expert_count]
    grad_in_shard, grad_out_shard = (
        lax.psum_scatter(
            weight_in_grad.astype(jnp.bfloat16), "dp", scatter_dimension=1, tiled=True
        ).astype(jnp.float32),
        lax.psum_scatter(
            weight_out_grad.astype(jnp.bfloat16), "dp", scatter_dimension=1, tiled=True
        ).astype(jnp.float32),
    )
    weighted = gate_weights * jnp.where(picked, grad_gates, 0.0)
    grad_logits = (
        weighted - gate_weights * jnp.sum(weighted, axis=-1, keepdims=True)
    ).astype(jnp.bfloat16)
    router_grad = contract_rows(hidden_ffn, grad_logits)
    grad_hidden_ffn = grad_hidden_ffn + contract_cols(grad_logits, w_router)
    gain_ffn_grad = jnp.sum(grad_hidden_ffn * normed_ffn, axis=0)
    grad_residual = grad_out + norm_back(grad_hidden_ffn, normed_ffn, scale_ffn, gain_ffn)
    grad_branch = grad_residual.astype(jnp.bfloat16)
    output_grad = contract_rows(grad_branch, attn_low)
    late_sums = lax.psum_scatter(
        jnp.concatenate(
            [output_grad, router_grad, as_column(gain_ffn_grad, expert_count)], axis=1
        ).astype(jnp.bfloat16),
        EVERY,
        scatter_dimension=0,
        tiled=True,
    ).astype(jnp.float32)
    attention_gradient = jnp.dot(
        grad_branch, full_output, preferred_element_type=jnp.float32
    ).astype(jnp.bfloat16)
    head_gradient = attention_gradient.reshape(
        token_matrix, KEY_VALUE_HEADS, query_per_key, HEAD_DIM
    ).transpose(1, 2, 0, 3)

    def attend_back(operands):
        query_group, key_group, value_group, grad_group, log_group = operands
        scores = jnp.einsum(
            "gtd,sd->gts", query_group, key_group, preferred_element_type=jnp.float32
        )
        attn_probs = jnp.where(allowed[None], jnp.exp(scores - log_group[..., None]), 0.0)
        grad_probs = jnp.einsum(
            "gtd,sd->gts", grad_group, value_group, preferred_element_type=jnp.float32
        )
        centre = jnp.sum(attn_probs * grad_probs, axis=-1, keepdims=True)
        grad_scores = (attn_probs * (grad_probs - centre)).astype(jnp.bfloat16)
        grad_query_group = jnp.einsum(
            "gts,sd->gtd", grad_scores, key_group, preferred_element_type=jnp.float32
        )
        grad_key_group = jnp.einsum(
            "gts,gtd->sd", grad_scores, query_group, preferred_element_type=jnp.float32
        )
        grad_value_group = jnp.einsum(
            "gts,gtd->sd",
            attn_probs.astype(jnp.bfloat16),
            grad_group,
            preferred_element_type=jnp.float32,
        )
        return (grad_query_group, grad_key_group, grad_value_group)

    grad_query_heads, key_head_gradient, value_head_gradient = lax.map(
        attend_back, (heads_of_query, heads_of_key, heads_of_value, head_gradient, log_totals)
    )
    complete_key_gradient = key_head_gradient.transpose(1, 0, 2).reshape(
        total_keys, KEY_VALUE_HEADS * HEAD_DIM
    )
    complete_value_gradient = value_head_gradient.transpose(1, 0, 2).reshape(
        total_keys, KEY_VALUE_HEADS * HEAD_DIM
    )
    local_key_gradient, value_grad_own = (
        lax.psum_scatter(
            complete_key_gradient.astype(jnp.bfloat16), "dp", scatter_dimension=0, tiled=True
        ).astype(jnp.float32),
        lax.psum_scatter(
            complete_value_gradient.astype(jnp.bfloat16), "dp", scatter_dimension=0, tiled=True
        ).astype(jnp.float32),
    )
    key_grad_low = (
        apply_rotary(
            local_key_gradient.reshape(token_matrix, KEY_VALUE_HEADS, HEAD_DIM),
            local_cosine,
            -local_sine,
        )
        .reshape(token_matrix, KEY_VALUE_HEADS * HEAD_DIM)
        .astype(jnp.bfloat16)
    )
    value_grad_low = value_grad_own.astype(jnp.bfloat16)
    query_grad_rows = grad_query_heads.transpose(2, 0, 1, 3).reshape(
        token_matrix, QUERY_HEADS, HEAD_DIM
    )
    query_grad_low = (
        (apply_rotary(query_grad_rows, local_cosine, -local_sine) * 0.125)
        .reshape(token_matrix, QUERY_HEADS * HEAD_DIM)
        .astype(jnp.bfloat16)
    )
    query_grad = contract_rows(hidden_attn, query_grad_low)
    key_grad = contract_rows(hidden_attn, key_grad_low)
    value_grad = contract_rows(hidden_attn, value_grad_low)
    grad_hidden_attn = (
        contract_cols(query_grad_low, full_query)
        + contract_cols(key_grad_low, full_key)
        + contract_cols(value_grad_low, full_value)
    )
    gain_attn_grad = jnp.sum(grad_hidden_attn * normed_attn, axis=0)
    grad_inputs = grad_residual + norm_back(grad_hidden_attn, normed_attn, scale_attn, gain_attn)
    attn_sums = lax.psum_scatter(
        jnp.concatenate(
            [query_grad, key_grad, value_grad, as_column(gain_attn_grad)], axis=1
        ).astype(jnp.bfloat16),
        EVERY,
        scatter_dimension=0,
        tiled=True,
    ).astype(jnp.float32)
    clip_limit = threshold[0].astype(jnp.float32)
    shrink_factor = clip_limit / jnp.maximum(largest, clip_limit)
    query_scale = jnp.repeat(jnp.sqrt(shrink_factor), HEAD_DIM)
    key_shrink = jnp.repeat(
        jnp.sqrt(jnp.min(shrink_factor.reshape(KEY_VALUE_HEADS, query_per_key), axis=1)), HEAD_DIM
    )
    clipped_query = (w_query.astype(jnp.float32) * query_scale[None, :]).astype(jnp.bfloat16)
    clipped_key = (key_weight.astype(jnp.float32) * key_shrink[None, :]).astype(jnp.bfloat16)
    return (
        out[None],
        grad_inputs.astype(jnp.bfloat16)[None],
        attn_sums[:, query_width + 2 * key_width],
        attn_sums[:, :query_width],
        attn_sums[:, query_width : query_width + key_width],
        attn_sums[:, query_width + key_width : query_width + 2 * key_width],
        late_sums[:, :query_width],
        late_sums[:, query_width + expert_count],
        late_sums[:, query_width : query_width + expert_count],
        grad_in_shard,
        grad_out_shard,
        largest,
        clipped_query,
        clipped_key,
    )


def solution(mesh):
    return jax.shard_map(
        on_device,
        mesh=mesh,
        in_specs=(
            P(("expert", "shard"), "dp", None),
            P(("expert", "shard"), "dp", None),
            P(),
            P("shard", None),
            P("shard", None),
            P("shard", None),
            P("shard", None),
            P(),
            P(),
            P(("expert", "shard"), None, None),
            P(("expert", "shard"), None, None),
            P(("expert", "shard"), "dp", None),
            P(("expert", "shard"), "dp"),
            P(),
        ),
        out_specs=(
            P(("expert", "shard"), "dp", None),
            P(("expert", "shard"), "dp", None),
            P(("dp", "expert", "shard")),
            P(("dp", "expert", "shard"), None),
            P(("dp", "expert", "shard"), None),
            P(("dp", "expert", "shard"), None),
            P(("dp", "expert", "shard"), None),
            P(("dp", "expert", "shard")),
            P(("dp", "expert", "shard"), None),
            P(("expert", "shard"), "dp", None),
            P(("expert", "shard"), "dp", None),
            P(),
            P("shard", None),
            P("shard", None),
        ),
        check_vma=False,
    )
```

```python
import functools
import math

import jax
import jax.numpy as jnp
from jax import lax
from jax.experimental import pallas as pl
from jax.experimental.pallas import tpu as pltpu
from jax.sharding import PartitionSpec as P

QUERY_HEADS = 24
KEY_VALUE_HEADS = 8
HEAD_DIM = 64
TOP = 8
GROUP = ("expert", "shard")
EVERY = ("dp", "expert", "shard")

EPSILON = 1e-06
EXCLUDED = -1e30


def rope_tables(positions, head_size):
    half_size = head_size // 2
    frequency = jnp.exp(
        jnp.arange(half_size).astype(jnp.float32) * (-2.0 * math.log(10000.0) / head_size)
    )
    angles = positions.astype(jnp.float32)[:, None] * frequency[None, :]
    return (jnp.cos(angles), jnp.sin(angles))


def apply_rotary(values, cosine_lookup, sine_lookup):
    half_size = values.shape[-1] // 2
    first_half = values[..., :half_size]
    second = values[..., half_size:]
    cosine_b = cosine_lookup[:, None, :]
    sine_b = sine_lookup[:, None, :]
    return jnp.concatenate(
        [first_half * cosine_b - second * sine_b, second * cosine_b + first_half * sine_b], axis=-1
    )


def rms_scale(values):
    return lax.rsqrt(jnp.mean(values * values, axis=-1, keepdims=True) + EPSILON)


def norm_back(grad_normed, normed, inv_rms, gain_vector):
    scaled = grad_normed * gain_vector
    return inv_rms * (scaled - normed * jnp.mean(scaled * normed, axis=-1, keepdims=True))


def contract_rows(left_side, right_side):
    return lax.dot_general(
        left_side, right_side, (((0,), (0,)), ((), ())), preferred_element_type=jnp.float32
    )


def contract_cols(left_side, right_side):
    return lax.dot_general(
        left_side, right_side, (((1,), (1,)), ((), ())), preferred_element_type=jnp.float32
    )


def as_column(vector, before=0):
    return jnp.pad(vector[:, None], ((0, 0), (0, 127 - before)))


def masked_softmax(logits, picked):
    kept = jnp.where(picked, logits, EXCLUDED)
    exponent = jnp.exp(kept - jnp.max(kept, axis=-1, keepdims=True))
    return exponent / jnp.sum(exponent, axis=-1, keepdims=True)


def max_dp(values):
    if lax.axis_size("dp") != 2:
        return lax.pmax(values, "dp")
    return jnp.maximum(values, lax.ppermute(values, "dp", [(0, 1), (1, 0)]))


def allowed_bias(position_ref, docs_all_ref, docs_own_ref):
    keys, rows = docs_all_ref.shape[0], docs_own_ref.shape[1]
    key_at = lax.broadcasted_iota(jnp.int32, (keys, rows), 0)
    row_at = lax.broadcasted_iota(jnp.int32, (keys, rows), 1) + position_ref[0]
    allowed = (key_at <= row_at) & (docs_all_ref[...] == docs_own_ref[...])
    return jnp.where(allowed, 0.0, EXCLUDED)


def attend_kernel(
    position_ref, docs_all_ref, docs_own_ref, query_ref, key_ref, value_ref,
    mix_ref, log_ref, top_ref, bias,
):
    @pl.when(pl.program_id(0) == 0)
    def _():
        bias[...] = allowed_bias(position_ref, docs_all_ref, docs_own_ref)

    rows = query_ref.shape[0]
    mixes, logs, tops = [], [], []
    for head in range(query_ref.shape[1] // HEAD_DIM):
        group = head * key_ref.shape[1] // query_ref.shape[1] * HEAD_DIM
        query = query_ref[:, head * HEAD_DIM : (head + 1) * HEAD_DIM]
        key = key_ref[:, group : group + HEAD_DIM]
        value = value_ref[:, group : group + HEAD_DIM]
        scores = contract_cols(key, query) + bias[...]
        top = jnp.max(scores, axis=0, keepdims=True)
        exponent = jnp.exp(scores - top)
        totals = jnp.sum(exponent, axis=0, keepdims=True)
        probs = (exponent * (1.0 / totals)).astype(jnp.bfloat16)
        mixes.append(contract_rows(value, probs))
        logs.append(top + jnp.log(totals))
        tops.append(top)
    mix_ref[...] = jnp.concatenate(mixes, axis=0).T.astype(jnp.bfloat16)
    blank = [jnp.zeros((8 - len(logs), rows), jnp.float32)]
    log_ref[0] = jnp.concatenate(logs + blank, axis=0)
    top_ref[0] = jnp.broadcast_to(
        jnp.max(jnp.concatenate(tops + blank, axis=0), axis=1, keepdims=True), (8, 128)
    )


def attend_back_kernel(
    position_ref, docs_all_ref, docs_own_ref, query_ref, key_ref, value_ref, mix_grad_ref, log_ref,
    query_grad_ref, key_grad_ref, value_grad_ref, bias,
):
    @pl.when(pl.program_id(0) == 0)
    def _():
        bias[...] = allowed_bias(position_ref, docs_all_ref, docs_own_ref)

    query_grads, key_grads, value_grads = [], {}, {}
    for head in range(query_ref.shape[1] // HEAD_DIM):
        group = head * key_ref.shape[1] // query_ref.shape[1] * HEAD_DIM
        query = query_ref[:, head * HEAD_DIM : (head + 1) * HEAD_DIM]
        mix_grad = mix_grad_ref[:, head * HEAD_DIM : (head + 1) * HEAD_DIM]
        key = key_ref[:, group : group + HEAD_DIM]
        value = value_ref[:, group : group + HEAD_DIM]
        scores = contract_cols(key, query) + bias[...]
        probs = jnp.exp(scores - log_ref[0, head : head + 1, :])
        prob_grads = contract_cols(value, mix_grad)
        centre = jnp.sum(probs * prob_grads, axis=0, keepdims=True)
        score_grads = (probs * (prob_grads - centre)).astype(jnp.bfloat16)
        query_grads.append(contract_rows(key, score_grads))
        key_term = jnp.dot(score_grads, query, preferred_element_type=jnp.float32)
        value_term = jnp.dot(
            probs.astype(jnp.bfloat16), mix_grad, preferred_element_type=jnp.float32
        )
        key_grads[group] = key_grads[group] + key_term if group in key_grads else key_term
        value_grads[group] = value_grads[group] + value_term if group in value_grads else value_term
    query_grad_ref[...] = jnp.concatenate(query_grads, axis=0).T
    for group in key_grads:
        key_grad_ref[:, group : group + HEAD_DIM] = key_grads[group]
        value_grad_ref[:, group : group + HEAD_DIM] = value_grads[group]


def attention_specs(rows, keys, query_width, key_width):
    whole = lambda shape: pl.BlockSpec(shape, lambda i: (0, 0))
    by_head = lambda count, width: pl.BlockSpec((count, width), lambda i: (0, i))
    steps = key_width // 128
    in_specs = [
        pl.BlockSpec(memory_space=pltpu.SMEM),
        whole((keys, 1)),
        whole((1, rows)),
        by_head(rows, query_width // steps),
        by_head(keys, 128),
        by_head(keys, 128),
    ]
    return steps, in_specs, by_head, pl.BlockSpec((1, 8, rows), lambda i: (i, 0, 0))


def attend(position, docs_all, docs_own, query, key, value):
    rows, query_width = query.shape
    keys, key_width = key.shape
    steps, in_specs, by_head, by_log = attention_specs(rows, keys, query_width, key_width)
    mix, logs, tops = pl.pallas_call(
        attend_kernel,
        grid=(steps,),
        in_specs=in_specs,
        out_specs=(
            by_head(rows, query_width // steps), by_log, pl.BlockSpec((1, 8, 128), lambda i: (i, 0, 0))
        ),
        out_shape=(
            jax.ShapeDtypeStruct((rows, query_width), jnp.bfloat16),
            jax.ShapeDtypeStruct((steps, 8, rows), jnp.float32),
            jax.ShapeDtypeStruct((steps, 8, 128), jnp.float32),
        ),
        scratch_shapes=[pltpu.VMEM((keys, rows), jnp.float32)],
        compiler_params=pltpu.CompilerParams(vmem_limit_bytes=50 * 2**20),
    )(position, docs_all[:, None], docs_own[None, :], query, key, value)
    return mix, logs, tops[:, : QUERY_HEADS // steps, 0].reshape(QUERY_HEADS)


def attend_back(position, docs_all, docs_own, query, key, value, mix_grad, logs):
    rows, query_width = query.shape
    keys, key_width = key.shape
    steps, in_specs, by_head, by_log = attention_specs(rows, keys, query_width, key_width)
    wide = query_width // steps
    return pl.pallas_call(
        attend_back_kernel,
        grid=(steps,),
        in_specs=in_specs + [by_head(rows, wide), by_log],
        out_specs=(by_head(rows, wide), by_head(keys, 128), by_head(keys, 128)),
        out_shape=(
            jax.ShapeDtypeStruct((rows, query_width), jnp.float32),
            jax.ShapeDtypeStruct((keys, key_width), jnp.float32),
            jax.ShapeDtypeStruct((keys, key_width), jnp.float32),
        ),
        scratch_shapes=[pltpu.VMEM((keys, rows), jnp.float32)],
        compiler_params=pltpu.CompilerParams(vmem_limit_bytes=50 * 2**20),
    )(position, docs_all[:, None], docs_own[None, :], query, key, value, mix_grad, logs)


def scatter_kernel(
    whole_ref, total_ref, from_core, pair_sum, first_x, first_y, mid, last_x, last_y, sums, from_line,
    core_send, core_recv, x_send, x_recv, y_send, y_recv, z_send, z_recv,
):
    half, expert, depth = lax.axis_index("dp"), lax.axis_index("expert"), lax.axis_index("shard")
    side, core = expert // 2, expert % 2
    partner = {"dp": 1 - half}
    opposite = {"expert": 2 * ((side + 1) % 2) + core}
    sibling = {"expert": 2 * side + (core + 1) % 2}
    cols = whole_ref.shape[2] // 2
    left, right = pl.ds(0, cols), pl.ds(cols, cols)

    def along(distance):
        return {"shard": (depth + distance) % 4}

    barrier = pltpu.get_barrier_semaphore()
    for peer in (partner, opposite, sibling, along(1), along(2), along(3)):
        pl.semaphore_signal(barrier, inc=1, device_id=peer, device_id_type=pl.DeviceIdType.MESH)
    pl.semaphore_wait(barrier, 6)

    def remote(src, dst, send, recv, to):
        return pltpu.make_async_remote_copy(
            src_ref=src, dst_ref=dst, send_sem=send, recv_sem=recv, device_id=to,
            device_id_type=pl.DeviceIdType.MESH,
        )

    def added(a, b):
        return (a.astype(jnp.float32) + b.astype(jnp.float32)).astype(jnp.bfloat16)

    def chunk(j, other_core):
        return 4 * ((half + j // 2) % 2) + 2 * ((side + j % 2) % 2) + (core + other_core) % 2

    def to_core(j):
        return remote(
            whole_ref.at[chunk(j, 1)], from_core.at[j], core_send.at[j], core_recv.at[j], sibling
        )

    def to_x(k):
        return remote(
            pair_sum.at[2 + k, :, left], first_x.at[k], x_send.at[k], x_recv.at[k], partner
        )

    def to_y(k):
        return remote(
            pair_sum.at[2 * k + 1, :, right], first_y.at[k], y_send.at[k], y_recv.at[k], opposite
        )

    def then_y():
        return remote(mid.at[0], last_y, y_send.at[2], y_recv.at[2], opposite)

    def then_x():
        return remote(mid.at[1], last_x, x_send.at[2], x_recv.at[2], partner)

    def to_line(zi, part):
        return remote(
            sums.at[part, (depth + zi) % 4], from_line.at[zi, part], z_send.at[zi, part],
            z_recv.at[zi, part], along(zi),
        )

    order = (3, 2, 1, 0)
    for j in order:
        to_core(j).start()
    for j in order:
        to_core(j).wait_recv()
        pair_sum[j] = added(whole_ref[chunk(j, 0)], from_core[j])
        if j == 3:
            to_x(1).start()
            to_y(1).start()
        if j == 2:
            to_x(0).start()
        if j == 1:
            to_y(0).start()
    to_x(1).wait_recv()
    mid[0] = added(pair_sum[1, :, left], first_x[1])
    then_y().start()
    to_y(1).wait_recv()
    mid[1] = added(pair_sum[2, :, right], first_y[1])
    then_x().start()
    share = sums.shape[2]
    for part, first, last, last_ref, own in (
        (0, to_x(0), then_y(), last_y, left), (1, to_y(0), then_x(), last_x, right)
    ):
        first.wait_recv()
        last.wait_recv()
        near = (first_x if part == 0 else first_y)[0]
        full = (
            pair_sum[0, :, own].astype(jnp.float32)
            + near.astype(jnp.float32)
            + last_ref[...].astype(jnp.float32)
        ).astype(jnp.bfloat16)
        for z in range(4):
            sums[part, z] = full[z * share : (z + 1) * share]
        for zi in (2, 1, 3):
            to_line(zi, part).start()
    for part, own in ((0, left), (1, right)):
        result = sums[part, depth].astype(jnp.float32)
        for zi in (1, 3, 2):
            to_line(zi, part).wait_recv()
            result = result + from_line[zi, part].astype(jnp.float32)
        total_ref[:, own] = result
    for j in order:
        to_core(j).wait_send()
    for k in range(2):
        to_x(k).wait_send()
        to_y(k).wait_send()
    then_x().wait_send()
    then_y().wait_send()
    for zi in range(1, 4):
        for part in range(2):
            to_line(zi, part).wait_send()


def scatter_every(whole):
    if lax.axis_size("dp") != 2:
        return lax.psum_scatter(whole, EVERY, scatter_dimension=0, tiled=True).astype(jnp.float32)
    rows, width = whole.shape[0] // 8, whole.shape[1]
    cols, low, dma = width // 2, whole.dtype, pltpu.SemaphoreType.DMA
    return pl.pallas_call(
        scatter_kernel,
        out_shape=jax.ShapeDtypeStruct((rows // 4, width), jnp.float32),
        in_specs=[pl.BlockSpec(memory_space=pltpu.VMEM)],
        out_specs=pl.BlockSpec(memory_space=pltpu.VMEM),
        scratch_shapes=[
            pltpu.VMEM((4, rows, width), low),
            pltpu.VMEM((4, rows, width), low),
            pltpu.VMEM((2, rows, cols), low),
            pltpu.VMEM((2, rows, cols), low),
            pltpu.VMEM((2, rows, cols), low),
            pltpu.VMEM((rows, cols), low),
            pltpu.VMEM((rows, cols), low),
            pltpu.VMEM((2, 4, rows // 4, cols), low),
            pltpu.VMEM((4, 2, rows // 4, cols), low),
            dma((4,)), dma((4,)), dma((3,)), dma((3,)), dma((3,)), dma((3,)), dma((4, 2)), dma((4, 2)),
        ],
        compiler_params=pltpu.CompilerParams(
            collective_id=2, has_side_effects=True, vmem_limit_bytes=44 * 2**20
        ),
    )(whole.reshape(8, rows, width))


def gather_dp(rows):
    if lax.axis_size("dp") != 2:
        return lax.all_gather(rows, "dp", axis=0, tiled=True)
    other = lax.ppermute(rows, "dp", [(0, 1), (1, 0)])
    early = lax.axis_index("dp") == 0
    return jnp.concatenate(
        [jnp.where(early, rows, other), jnp.where(early, other, rows)], axis=0
    )


def scatter_dp(whole, dim):
    if lax.axis_size("dp") != 2:
        return lax.psum_scatter(
            whole.astype(jnp.bfloat16), "dp", scatter_dimension=dim, tiled=True
        ).astype(jnp.float32)
    size, at = whole.shape[dim] // 2, lax.axis_index("dp")
    given = lax.dynamic_slice_in_dim(whole, (1 - at) * size, size, dim).astype(jnp.bfloat16)
    taken = lax.ppermute(given, "dp", [(0, 1), (1, 0)])
    kept = lax.dynamic_slice_in_dim(whole, at * size, size, dim)
    return kept.astype(jnp.float32) + taken.astype(jnp.float32)


def weights_kernel(first_ref, second_ref, first_full, second_full, own_sem, send_sem, recv_sem):
    pair, expert, depth = lax.axis_index("dp"), lax.axis_index("expert"), lax.axis_index("shard")
    side, core = expert // 2, expert % 2
    half = pair % 2
    partner = {"dp": pair + 1 - 2 * half}
    opposite = {"expert": 2 * ((side + 1) % 2) + core}
    sibling = {"expert": 2 * side + (core + 1) % 2}
    rows = first_ref.shape[0]
    part = rows // 8
    arrays = ((first_ref, first_full), (second_ref, second_full))

    def along(distance):
        return {"shard": (depth + distance) % 4}

    barrier = pltpu.get_barrier_semaphore()
    for peer in (partner, opposite, sibling, along(1), along(2), along(3)):
        pl.semaphore_signal(barrier, inc=1, device_id=peer, device_id_type=pl.DeviceIdType.MESH)
    pl.semaphore_wait(barrier, 6)

    def eighth(px, pa, pc):
        return 4 * ((half + px) % 2) + 2 * ((side + pa) % 2) + (core + pc) % 2

    def place(full, zi, px, pa, pc):
        start = ((depth + zi) % 4) * rows + eighth(px, pa, pc) * part
        return full.at[pl.ds(pl.multiple_of(start, part), part)]

    def copy(which, zi, source, hop, to):
        px, pa, pc = source
        full = arrays[which][1]
        there = 4 * (px ^ hop[0]) + 2 * (pa ^ hop[1]) + (pc ^ hop[2])
        return pltpu.make_async_remote_copy(
            src_ref=place(full, zi, px, pa, pc),
            dst_ref=place(full, zi, px, pa, pc),
            send_sem=send_sem.at[which, zi, there],
            recv_sem=recv_sem.at[which, zi, there],
            device_id=to,
            device_id_type=pl.DeviceIdType.MESH,
        )

    def along_line(which, zi):
        own, full = arrays[which]
        start = eighth(0, 0, 0) * part
        return pltpu.make_async_remote_copy(
            src_ref=own.at[pl.ds(pl.multiple_of(start, part), part)],
            dst_ref=full.at[pl.ds(pl.multiple_of(depth * rows + start, part), part)],
            send_sem=send_sem.at[which, zi, 0],
            recv_sem=recv_sem.at[which, zi, 0],
            device_id=along(4 - zi),
            device_id_type=pl.DeviceIdType.MESH,
        )

    own_copies = [
        pltpu.make_async_copy(
            own, full.at[pl.ds(pl.multiple_of(depth * rows, rows), rows)], own_sem.at[which]
        )
        for which, (own, full) in enumerate(arrays)
    ]
    near, over, by = (1, 0, 0), (0, 1, 0), (0, 0, 1)
    for which in range(2):
        for zi in (1, 3, 2):
            along_line(which, zi).start()
    for own_copy in own_copies:
        own_copy.start()
    for which in range(2):
        for zi in (1, 3, 2):
            along_line(which, zi).wait_recv()
            copy(which, zi, (0, 0, 0), near, partner).start()
            copy(which, zi, (0, 0, 0), over, opposite).start()
            copy(which, zi, (0, 0, 0), by, sibling).start()
        for zi in (1, 3, 2):
            copy(which, zi, (0, 0, 0), near, partner).wait_recv()
            copy(which, zi, (1, 0, 0), by, sibling).start()

            @pl.when(core == 0)
            def _():
                copy(which, zi, (1, 0, 0), over, opposite).start()

            copy(which, zi, (0, 0, 0), over, opposite).wait_recv()
            copy(which, zi, (0, 1, 0), by, sibling).start()

            @pl.when(core == 1)
            def _():
                copy(which, zi, (0, 1, 0), near, partner).start()

    for which in range(2):
        for zi in (1, 3, 2):
            copy(which, zi, (1, 0, 0), over, opposite).wait_recv()
            copy(which, zi, (1, 1, 0), by, sibling).start()
    for which in range(2):
        for zi in (1, 3, 2):
            for px, pa in ((0, 0), (1, 0), (0, 1), (1, 1)):
                copy(which, zi, (px, pa, 0), by, sibling).wait()
            along_line(which, zi).wait_send()
            copy(which, zi, (0, 0, 0), near, partner).wait_send()
            copy(which, zi, (0, 0, 0), over, opposite).wait_send()

            @pl.when(core == 0)
            def _():
                copy(which, zi, (1, 0, 0), over, opposite).wait_send()

            @pl.when(core == 1)
            def _():
                copy(which, zi, (0, 1, 0), near, partner).wait_send()

    for own_copy in own_copies:
        own_copy.wait()


def gather_weights(first, second):
    anywhere = pl.BlockSpec(memory_space=pl.ANY)
    dma = pltpu.SemaphoreType.DMA
    return pl.pallas_call(
        weights_kernel,
        out_shape=tuple(
            jax.ShapeDtypeStruct((4 * part.shape[0], part.shape[1]), part.dtype)
            for part in (first, second)
        ),
        in_specs=[anywhere] * 2,
        out_specs=(anywhere,) * 2,
        scratch_shapes=[dma((2,)), dma((2, 4, 8)), dma((2, 4, 8))],
        compiler_params=pltpu.CompilerParams(collective_id=1, has_side_effects=True),
    )(first, second)


def experts_kernel(
    in_pairs, hidden_ref, cot_ref, router_ref, win_ref, wout_ref,
    rows_ref, kept_ref, core_ref, across_ref, line_ref, stage_ref, dwin_ref, dwout_ref, taken_in, taken_out,
    acc_in, acc_out, win, wout, router, row_tile, cot_tile, made, parts,
    load_sem, tile_sem, row_recv, core_send, across_send, line_send,
    made_sem, part_sem, core_recv, across_recv, line_recv, stage_sem, stage_send, store_sem, given_sem, taken_sem,
):
    own_count, width = wout_ref.shape[0], wout_ref.shape[1]
    rows_own, model = hidden_ref.shape[0] - 16, hidden_ref.shape[1]
    tile = rows_own // 2
    expert, depth = lax.axis_index("expert"), lax.axis_index("shard")
    side, core = expert // 2, expert % 2
    sibling = {"expert": 2 * side + (core + 1) % 2}
    opposite = {"expert": 2 * ((side + 1) % 2) + core}

    def along(distance):
        return {"shard": (depth + distance) % 4}

    def remote(src, dst, send, recv, to):
        return pltpu.make_async_remote_copy(
            src_ref=src, dst_ref=dst, send_sem=send, recv_sem=recv, device_id=to,
            device_id_type=pl.DeviceIdType.MESH,
        )

    barrier = pltpu.get_barrier_semaphore()
    half = lax.axis_index("dp")
    partner = {"dp": 1 - half}
    peers = [sibling, opposite, along(1), along(2), along(3)] + [partner] * in_pairs
    for peer in peers:
        pl.semaphore_signal(barrier, inc=1, device_id=peer, device_id_type=pl.DeviceIdType.MESH)
    pl.semaphore_wait(barrier, len(peers))

    loads = [
        pltpu.make_async_copy(win_ref, win, load_sem.at[0]),
        pltpu.make_async_copy(wout_ref, wout, load_sem.at[1]),
        pltpu.make_async_copy(router_ref, router, load_sem.at[2]),
    ]

    def to_sibling(src, r):
        return remote(src, rows_ref.at[r + 1], core_send.at[r // 2], row_recv.at[r + 1], sibling)

    def to_opposite(src, r):
        return remote(src, rows_ref.at[r + 2], across_send.at[r // 4], row_recv.at[r + 2], opposite)

    def to_line(zi):
        return remote(
            hidden_ref, rows_ref.at[4 * zi], line_send.at[zi], row_recv.at[4 * zi], along(4 - zi)
        )

    def own_rows():
        return pltpu.make_async_copy(hidden_ref, rows_ref.at[0], row_recv.at[0])

    to_sibling(hidden_ref, 0).start()
    to_opposite(hidden_ref, 0).start()
    for zi in range(1, 4):
        to_line(zi).start()
    own_rows().start()
    for load in loads:
        load.start()

    def arrive(r):
        @pl.when(r == 0)
        def _():
            own_rows().wait()

        @pl.when(r > 0)
        def _():
            remote(
                rows_ref.at[r], rows_ref.at[r], core_send.at[0], row_recv.at[r], sibling
            ).wait_recv()

            @pl.when(r % 2 == 0)
            def _():
                to_sibling(rows_ref.at[r], r).start()

            @pl.when(r % 4 == 0)
            def _():
                to_opposite(rows_ref.at[r], r).start()

    def block_at(step):
        turn = (step // 2 + 1) // 2
        place = (turn + 7) % 8
        return 4 * ((place + place // 4) % 4) + 2 * (1 - place // 4) + (step // 2 + 1) % 2

    def tiles(step):
        r, sub, slot = block_at(step), step % 2, step % 2
        other = 2 * ((side + (r % 4) // 2) % 2) + (core + r) % 2
        start = (other * 4 + (depth + r // 4) % 4) * rows_own + sub * tile
        start = pl.multiple_of(start, tile)
        return (
            pltpu.make_async_copy(
                rows_ref.at[r, pl.ds(pl.multiple_of(sub * tile, tile), tile)],
                row_tile.at[slot], tile_sem.at[0, slot],
            ),
            pltpu.make_async_copy(
                cot_ref.at[pl.ds(start, tile)], cot_tile.at[slot], tile_sem.at[1, slot]
            ),
        )

    acc_in[...] = jnp.zeros_like(acc_in)
    acc_out[...] = jnp.zeros_like(acc_out)
    arrive(1)
    for copy in tiles(0):
        copy.start()
    for load in loads:
        load.wait()

    def send_made(step):
        r, sub, slot = block_at(step), step % 2, step % 2
        return remote(
            made.at[slot], core_ref.at[r // 2, sub], made_sem.at[slot],
            core_recv.at[r // 2, sub], sibling,
        )

    def keep_made(step):
        r, sub, slot = block_at(step), step % 2, step % 2
        return pltpu.make_async_copy(made.at[slot], kept_ref.at[r // 2, sub], made_sem.at[slot])

    def made_done(step):
        away = (step // 2 + 1) % 2

        @pl.when(away == 1)
        def _():
            send_made(step).wait_send()

        @pl.when(away == 0)
        def _():
            keep_made(step).wait()

    def send_y(zi, sub):
        return remote(
            stage_ref.at[zi, sub], across_ref.at[zi, sub], stage_send.at[zi, sub],
            across_recv.at[zi, sub], opposite,
        )

    def send_z(zi, sub):
        return remote(
            stage_ref.at[3 + zi, sub], line_ref.at[zi, sub], stage_send.at[3 + zi, sub],
            line_recv.at[zi, sub], along(zi),
        )

    def staged(place, sub):
        return pltpu.make_async_copy(parts.at[0], stage_ref.at[place, sub], stage_sem.at[0])

    def load_kept(pair, sub):
        return pltpu.make_async_copy(kept_ref.at[pair, sub], parts.at[0], part_sem.at[0])

    def load_core(pair, sub):
        return pltpu.make_async_copy(core_ref.at[pair, sub], parts.at[1], part_sem.at[1])

    def load_across(zi, sub):
        return pltpu.make_async_copy(across_ref.at[zi, sub], parts.at[2], part_sem.at[2])

    def core_arrived(pair, sub):
        remote(
            made.at[0], core_ref.at[pair, sub], made_sem.at[0], core_recv.at[pair, sub], sibling
        ).wait_recv()

    def begin_y(zi, sub):
        core_arrived(2 * zi + 1, sub)
        load_kept(2 * zi + 1, sub).start()
        load_core(2 * zi + 1, sub).start()

    def end_y(zi, sub):
        load_kept(2 * zi + 1, sub).wait()
        load_core(2 * zi + 1, sub).wait()
        parts[0] = (parts[0].astype(jnp.float32) + parts[1].astype(jnp.float32)).astype(
            jnp.bfloat16
        )
        staged(zi, sub).start()

    def begin_z(zi, sub):
        core_arrived(2 * zi, sub)
        send_y(zi, sub).wait_recv()
        load_kept(2 * zi, sub).start()
        load_core(2 * zi, sub).start()
        load_across(zi, sub).start()

    def end_z(zi, sub):
        load_kept(2 * zi, sub).wait()
        load_core(2 * zi, sub).wait()
        load_across(zi, sub).wait()
        parts[0] = (
            parts[0].astype(jnp.float32) + parts[1].astype(jnp.float32) + parts[2].astype(jnp.float32)
        ).astype(jnp.bfloat16)
        staged(3 + zi, sub).start()

    first = (expert * 4 + depth) * own_count

    def body(step, carry):
        slot, sub = step % 2, step % 2
        stage_y = (step >= 10) & (step < 24) & (step % 4 >= 2)
        zi_y = (step // 4 - 1) % 4
        stage_z = (step == 24) | (step == 25) | (step >= 30)
        zi_z = 1 + (step - 24) // 6
        for copy in tiles(step):
            copy.wait()

        @pl.when(step < 31)
        def _():
            after = block_at(step + 1)

            @pl.when((step % 2 == 1) & ((after % 4 != 0) | (after == 0)))
            def _():
                arrive(after)

            for early, r in ((2, 4), (6, 8), (10, 12)):
                @pl.when(step == early)
                def _():
                    arrive(jnp.int32(r))

            for copy in tiles(step + 1):
                copy.start()

        before_y = (step >= 11) & (step < 25) & ((step - 1) % 4 >= 2)
        before_z = (step == 25) | (step == 26) | (step == 31)

        @pl.when(before_y)
        def _():
            zi = ((step - 1) // 4 - 1) % 4
            staged(zi, 1 - sub).wait()
            send_y(zi, 1 - sub).start()

        @pl.when(before_z)
        def _():
            zi = 1 + (step - 25) // 6
            staged(3 + zi, 1 - sub).wait()
            send_z(zi, 1 - sub).start()

        @pl.when(stage_y)
        def _():
            begin_y(zi_y, sub)

        @pl.when(stage_z)
        def _():
            begin_z(zi_z, sub)

        @pl.when(step >= 2)
        def _():
            made_done(step - 2)

        rows, cot = row_tile[slot], cot_tile[slot, :, :model]
        logits = jnp.dot(rows, router[...], preferred_element_type=jnp.float32)
        lanes = lax.broadcasted_iota(jnp.int32, logits.shape, 1)
        routes = cot_tile[slot, :, model:].astype(jnp.float32).astype(jnp.int32)
        picked = lanes == routes[:, 0:1]
        for k in range(1, TOP):
            picked = picked | (lanes == routes[:, k : k + 1])
        gates = masked_softmax(logits, picked)
        out_sum = grad_sum = None
        gate_lanes = lax.broadcasted_iota(jnp.int32, (tile, 128), 1)
        gate_grads = jnp.zeros((tile, 128), jnp.float32)
        for e in range(own_count):
            gate = jnp.sum(jnp.where(lanes == first + e, gates, 0.0), axis=1, keepdims=True)
            both = jnp.dot(rows, win[e], preferred_element_type=jnp.float32)
            gate_part, up_part = both[:, :width], both[:, width:]
            sig = jax.nn.sigmoid(gate_part)
            activated = gate_part * sig
            hidden = (activated * up_part).astype(jnp.bfloat16).astype(jnp.float32)
            gated = (gate * hidden).astype(jnp.bfloat16)
            term = jnp.dot(gated, wout[e], preferred_element_type=jnp.float32)
            out_sum = term if out_sum is None else out_sum + term
            plain = contract_cols(cot, wout[e])
            own_grad = jnp.sum(plain * hidden, axis=1, keepdims=True)
            high = own_grad.astype(jnp.bfloat16).astype(jnp.float32)
            gate_grads = jnp.where(gate_lanes == first + e, high, gate_grads)
            gate_grads = jnp.where(gate_lanes == 64 + first + e, own_grad - high, gate_grads)
            back = gate * plain
            d_gate = back * up_part * sig * (1.0 + gate_part * (1.0 - sig))
            d_up = back * activated
            d_both = jnp.concatenate([d_gate, d_up], axis=1).astype(jnp.bfloat16)
            term = contract_cols(d_both, win[e])
            grad_sum = term if grad_sum is None else grad_sum + term
            acc_in[e] += contract_rows(rows, d_both)
            acc_out[e] += contract_rows(gated, cot)
        made[slot, :, :model] = grad_sum.astype(jnp.bfloat16)
        made[slot, :, model : 2 * model] = out_sum.astype(jnp.bfloat16)
        made[slot, :, 2 * model :] = gate_grads.astype(jnp.bfloat16)

        away = (step // 2 + 1) % 2

        @pl.when(away == 1)
        def _():
            send_made(step).start()

        @pl.when(away == 0)
        def _():
            keep_made(step).start()

        @pl.when(stage_y)
        def _():
            end_y(zi_y, sub)

        @pl.when(stage_z)
        def _():
            end_z(zi_z, sub)

        return carry

    lax.fori_loop(0, 32, body, 0)
    win[...] = acc_in[...].astype(jnp.bfloat16)
    wout[...] = acc_out[...].astype(jnp.bfloat16)
    grads = ((acc_in, win, taken_in, dwin_ref), (acc_out, wout, taken_out, dwout_ref))

    def half_rows(ref, at):
        size = ref.shape[1] // 2
        return ref.at[:, pl.ds(pl.multiple_of(at * size, size), size)]

    def give(which):
        _, sent, taken, _ = grads[which]
        return remote(
            half_rows(sent, 1 - half), taken, given_sem.at[which], taken_sem.at[which], partner
        )

    def store(which):
        total, sent, _, result = grads[which]
        return pltpu.make_async_copy(
            half_rows(total, half) if in_pairs else sent, result, store_sem.at[which]
        )

    for which in range(2):
        give(which).start() if in_pairs else store(which).start()
    staged(5, 1).wait()
    send_z(2, 1).start()
    for sub in range(2):
        begin_z(3, sub)
        end_z(3, sub)
        staged(6, sub).wait()
        send_z(3, sub).start()
    made_done(30)
    made_done(31)
    for sub in range(2):
        core_arrived(0, sub)
        send_y(0, sub).wait_recv()
        for zi in range(4):
            send_y(zi, sub).wait_send()
        for zi in range(1, 4):
            send_z(zi, sub).wait_send()
            send_z(zi, sub).wait_recv()
    for r in range(0, 16, 2):
        to_sibling(hidden_ref, r).wait_send()
    for r in range(0, 16, 4):
        to_opposite(hidden_ref, r).wait_send()
    for zi in range(1, 4):
        to_line(zi).wait_send()
    if in_pairs:
        for which in range(2):
            total, sent, taken, _ = grads[which]
            give(which).wait_recv()
            fetch = pltpu.make_async_copy(taken, half_rows(sent, half), load_sem.at[which])
            fetch.start()
            fetch.wait()
            size = total.shape[1] // 2
            rows = pl.ds(pl.multiple_of(half * size, size), size)
            total[:, rows] += sent[:, rows].astype(jnp.float32)
            store(which).start()
            give(which).wait_send()
    for which in range(2):
        store(which).wait()


def experts_pass(hidden, cotangent, w_router, expert_in, expert_out):
    rows_own, model = hidden.shape[0] - 16, hidden.shape[1]
    tile = rows_own // 2
    wide = 2 * model + 128
    anywhere = pl.BlockSpec(memory_space=pl.ANY)
    low = jnp.bfloat16
    kept = jax.ShapeDtypeStruct((8, 2, tile, wide), low)
    quarter = jax.ShapeDtypeStruct((4, 2, tile, wide), low)
    dma = pltpu.SemaphoreType.DMA
    in_pairs = lax.axis_size("dp") == 2
    share = lambda w: (w.shape[0], w.shape[1] // 2 if in_pairs else w.shape[1], w.shape[2])
    results = pl.pallas_call(
        functools.partial(experts_kernel, in_pairs),
        out_shape=(
            jax.ShapeDtypeStruct((16, rows_own + 16, model), low),
            kept,
            kept,
            quarter,
            quarter,
            jax.ShapeDtypeStruct((7, 2, tile, wide), low),
            jax.ShapeDtypeStruct(share(expert_in), jnp.float32 if in_pairs else low),
            jax.ShapeDtypeStruct(share(expert_out), jnp.float32 if in_pairs else low),
            jax.ShapeDtypeStruct(share(expert_in), low),
            jax.ShapeDtypeStruct(share(expert_out), low),
        ),
        in_specs=[anywhere] * 5,
        out_specs=(anywhere,) * 10,
        scratch_shapes=[
            pltpu.VMEM(expert_in.shape, jnp.float32),
            pltpu.VMEM(expert_out.shape, jnp.float32),
            pltpu.VMEM(expert_in.shape, low),
            pltpu.VMEM(expert_out.shape, low),
            pltpu.VMEM(w_router.shape, low),
            pltpu.VMEM((2, tile, model), low),
            pltpu.VMEM((2, tile, cotangent.shape[1]), low),
            pltpu.VMEM((2, tile, wide), low),
            pltpu.VMEM((3, tile, wide), low),
            dma((3,)), dma((2, 2)), dma((16,)), dma((8,)), dma((4,)), dma((4,)),
            dma((2,)), dma((3,)), dma((8, 2)), dma((4, 2)), dma((4, 2)), dma((1,)), dma((7, 2)), dma((2,)), dma((2,)), dma((2,)),
        ],
        compiler_params=pltpu.CompilerParams(
            collective_id=0, has_side_effects=True, vmem_limit_bytes=60 * 2**20
        ),
    )(hidden, cotangent, w_router, expert_in, expert_out)
    rows, kept, core, across, line, _, weight_in_grad, weight_out_grad, _, _ = results
    total = kept[0].astype(jnp.float32) + core[0].astype(jnp.float32)
    total = total + across[0].astype(jnp.float32)
    for zi in range(1, 4):
        total = total + line[zi].astype(jnp.float32)
    if not in_pairs:
        weight_in_grad = scatter_dp(weight_in_grad, 1)
        weight_out_grad = scatter_dp(weight_out_grad, 1)
    return total.reshape(rows_own, wide), rows[:, rows_own, :128], weight_in_grad, weight_out_grad


def on_device(
    tokens,
    cotangent,
    gain_attn,
    w_query,
    key_weight,
    value_weight,
    w_output,
    gain_ffn,
    w_router,
    expert_in,
    expert_out,
    routes,
    doc_ids,
    threshold,
):
    inputs = tokens[0].astype(jnp.float32)
    token_matrix, model_width = inputs.shape
    query_per_key = QUERY_HEADS // KEY_VALUE_HEADS
    query_width, key_width = w_query.shape[1], key_weight.shape[1]
    route_columns = jnp.pad(routes[0].astype(jnp.bfloat16), ((0, 0), (0, 128 - TOP)))
    all_cotangent = lax.all_gather(
        jnp.concatenate([cotangent[0], route_columns], axis=1), GROUP, axis=0, tiled=True
    )
    scale_attn = rms_scale(inputs)
    normed_attn = inputs * scale_attn
    hidden_attn = (normed_attn * gain_attn).astype(jnp.bfloat16)
    full_qkv, full_output = gather_weights(
        jnp.concatenate([w_query, key_weight, value_weight], axis=1), w_output
    )
    full_query = full_qkv[:, :query_width]
    full_key = full_qkv[:, query_width : query_width + key_width]
    full_value = full_qkv[:, query_width + key_width :]
    own_positions = lax.axis_index("dp") * token_matrix + jnp.arange(token_matrix)
    local_cosine, local_sine = rope_tables(own_positions, HEAD_DIM)
    projected = jnp.dot(hidden_attn, full_qkv, preferred_element_type=jnp.float32)
    query_proj = projected[:, :query_width]
    key_projected = projected[:, query_width : query_width + key_width]
    value_proj = projected[:, query_width + key_width :]
    query_rotated = (
        apply_rotary(
            query_proj.reshape(token_matrix, QUERY_HEADS, HEAD_DIM), local_cosine, local_sine
        )
        * 0.125
    ).astype(jnp.bfloat16)
    key_rotated = (
        apply_rotary(
            key_projected.reshape(token_matrix, KEY_VALUE_HEADS, HEAD_DIM), local_cosine, local_sine
        )
        .astype(jnp.bfloat16)
        .reshape(token_matrix, KEY_VALUE_HEADS * HEAD_DIM)
    )
    value_low = value_proj.astype(jnp.bfloat16)
    own_docs = doc_ids[0]
    both_gathered = gather_dp(jnp.concatenate([key_rotated, value_low], axis=1))
    gathered_keys, gathered_values = both_gathered[:, :key_width], both_gathered[:, key_width:]
    docs_all = lax.all_gather(own_docs, "dp", axis=0, tiled=True)
    attn_low, log_totals, head_max = attend(
        own_positions[:1], docs_all, own_docs, query_rotated.reshape(token_matrix, query_width),
        gathered_keys, gathered_values,
    )
    branch_attn = contract_cols(attn_low, full_output)
    residual = inputs + branch_attn
    scale_ffn = rms_scale(residual)
    normed_ffn = residual * scale_ffn
    hidden_ffn = (normed_ffn * gain_ffn).astype(jnp.bfloat16)
    expert_count = w_router.shape[1]
    router_logits = jnp.dot(hidden_ffn, w_router, preferred_element_type=jnp.float32)
    route_ids = routes[0]
    picked = (route_ids[:, :, None] == jnp.arange(expert_count)[None, None, :]).any(axis=1)
    gate_weights = masked_softmax(router_logits, picked)
    grad_out = cotangent[0].astype(jnp.float32)
    high = lax.reduce_precision(head_max, 8, 7)
    middle = lax.reduce_precision(head_max - high, 8, 7)
    in_three = jnp.concatenate([high, middle, head_max - high - middle]).astype(jnp.bfloat16)
    extra = jnp.broadcast_to(
        jnp.pad(in_three, (0, hidden_ffn.shape[1] - in_three.shape[0])), (16, hidden_ffn.shape[1])
    )
    summed, maxima, grad_in_shard, grad_out_shard = experts_pass(
        jnp.concatenate([hidden_ffn, extra], axis=0), all_cotangent, w_router, expert_in, expert_out
    )
    model = hidden_ffn.shape[1]
    maxima = maxima.astype(jnp.float32)
    largest = jnp.max(
        maxima[:, :QUERY_HEADS]
        + maxima[:, QUERY_HEADS : 2 * QUERY_HEADS]
        + maxima[:, 2 * QUERY_HEADS : 3 * QUERY_HEADS],
        axis=0,
    )
    largest = max_dp(largest)
    grad_hidden_ffn = summed[:, :model]
    out = (residual + summed[:, model : 2 * model]).astype(jnp.bfloat16)
    gate_cols = summed[:, 2 * model :]
    grad_gates = gate_cols[:, :expert_count] + gate_cols[:, 64 : 64 + expert_count]
    weighted = gate_weights * jnp.where(picked, grad_gates, 0.0)
    grad_logits = (
        weighted - gate_weights * jnp.sum(weighted, axis=-1, keepdims=True)
    ).astype(jnp.bfloat16)
    router_grad = contract_rows(hidden_ffn, grad_logits)
    grad_hidden_ffn = grad_hidden_ffn + contract_cols(grad_logits, w_router)
    gain_ffn_grad = jnp.sum(grad_hidden_ffn * normed_ffn, axis=0)
    grad_residual = grad_out + norm_back(grad_hidden_ffn, normed_ffn, scale_ffn, gain_ffn)
    grad_branch = grad_residual.astype(jnp.bfloat16)
    output_grad = contract_rows(grad_branch, attn_low)
    late_sums = lax.psum_scatter(
        jnp.concatenate(
            [output_grad, router_grad, as_column(gain_ffn_grad, expert_count)], axis=1
        ).astype(jnp.bfloat16),
        EVERY,
        scatter_dimension=0,
        tiled=True,
    ).astype(jnp.float32)
    attention_gradient = jnp.dot(
        grad_branch, full_output, preferred_element_type=jnp.float32
    ).astype(jnp.bfloat16)
    grad_query_rows, key_gradient, value_gradient = attend_back(
        own_positions[:1], docs_all, own_docs, query_rotated.reshape(token_matrix, query_width),
        gathered_keys, gathered_values, attention_gradient, log_totals,
    )
    both_own = scatter_dp(
        jnp.concatenate([key_gradient, value_gradient], axis=1), 0
    )
    local_key_gradient, value_grad_own = both_own[:, :key_width], both_own[:, key_width:]
    key_grad_low = (
        apply_rotary(
            local_key_gradient.reshape(token_matrix, KEY_VALUE_HEADS, HEAD_DIM),
            local_cosine,
            -local_sine,
        )
        .reshape(token_matrix, KEY_VALUE_HEADS * HEAD_DIM)
        .astype(jnp.bfloat16)
    )
    value_grad_low = value_grad_own.astype(jnp.bfloat16)
    query_grad_rows = grad_query_rows.reshape(token_matrix, QUERY_HEADS, HEAD_DIM)
    query_grad_low = (
        (apply_rotary(query_grad_rows, local_cosine, -local_sine) * 0.125)
        .reshape(token_matrix, QUERY_HEADS * HEAD_DIM)
        .astype(jnp.bfloat16)
    )
    all_grad_low = jnp.concatenate([query_grad_low, key_grad_low, value_grad_low], axis=1)
    attn_sums = scatter_every(contract_rows(hidden_attn, all_grad_low).astype(jnp.bfloat16))
    grad_hidden_attn = contract_cols(all_grad_low, full_qkv)
    grad_inputs = grad_residual + norm_back(grad_hidden_attn, normed_attn, scale_attn, gain_attn)
    share = attn_sums.shape[0]
    first_row = (
        (lax.axis_index("dp") * lax.axis_size("expert") + lax.axis_index("expert"))
        * lax.axis_size("shard")
        + lax.axis_index("shard")
    ) * share
    own_rows = lax.dynamic_slice_in_dim(full_qkv, first_row, share, 0)
    own_gain = lax.dynamic_slice_in_dim(gain_attn, first_row, share, 0)
    gain_attn_grad = jnp.sum(own_rows.astype(jnp.float32) * attn_sums, axis=1) / own_gain
    clip_limit = threshold[0].astype(jnp.float32)
    shrink_factor = clip_limit / jnp.maximum(largest, clip_limit)
    query_scale = jnp.repeat(jnp.sqrt(shrink_factor), HEAD_DIM)
    key_shrink = jnp.repeat(
        jnp.sqrt(jnp.min(shrink_factor.reshape(KEY_VALUE_HEADS, query_per_key), axis=1)), HEAD_DIM
    )
    clipped_query = (w_query.astype(jnp.float32) * query_scale[None, :]).astype(jnp.bfloat16)
    clipped_key = (key_weight.astype(jnp.float32) * key_shrink[None, :]).astype(jnp.bfloat16)
    return (
        out[None],
        grad_inputs.astype(jnp.bfloat16)[None],
        gain_attn_grad,
        attn_sums[:, :query_width],
        attn_sums[:, query_width : query_width + key_width],
        attn_sums[:, query_width + key_width : query_width + 2 * key_width],
        late_sums[:, :query_width],
        late_sums[:, query_width + expert_count],
        late_sums[:, query_width : query_width + expert_count],
        grad_in_shard,
        grad_out_shard,
        largest,
        clipped_query,
        clipped_key,
    )


def solution(mesh):
    return jax.shard_map(
        on_device,
        mesh=mesh,
        in_specs=(
            P(("expert", "shard"), "dp", None),
            P(("expert", "shard"), "dp", None),
            P(),
            P("shard", None),
            P("shard", None),
            P("shard", None),
            P("shard", None),
            P(),
            P(),
            P(("expert", "shard"), None, None),
            P(("expert", "shard"), None, None),
            P(("expert", "shard"), "dp", None),
            P(("expert", "shard"), "dp"),
            P(),
        ),
        out_specs=(
            P(("expert", "shard"), "dp", None),
            P(("expert", "shard"), "dp", None),
            P(("dp", "expert", "shard")),
            P(("dp", "expert", "shard"), None),
            P(("dp", "expert", "shard"), None),
            P(("dp", "expert", "shard"), None),
            P(("dp", "expert", "shard"), None),
            P(("dp", "expert", "shard")),
            P(("dp", "expert", "shard"), None),
            P(("expert", "shard"), "dp", None),
            P(("expert", "shard"), "dp", None),
            P(),
            P("shard", None),
            P("shard", None),
        ),
        check_vma=False,
    )
```

```python
import functools
import math

import jax
import jax.numpy as jnp
from jax import lax
from jax.experimental import pallas as pl
from jax.experimental.pallas import tpu as pltpu
from jax.sharding import PartitionSpec as P

QUERY_HEADS = 24
KEY_VALUE_HEADS = 8
HEAD_DIM = 64
TOP = 8
GROUP = ("expert", "shard")
EVERY = ("dp", "expert", "shard")

EPSILON = 1e-06
EXCLUDED = -1e30


def rope_tables(positions, head_size):
    half_size = head_size // 2
    frequency = jnp.exp(
        jnp.arange(half_size).astype(jnp.float32) * (-2.0 * math.log(10000.0) / head_size)
    )
    angles = positions.astype(jnp.float32)[:, None] * frequency[None, :]
    return (jnp.cos(angles), jnp.sin(angles))


def apply_rotary(values, cosine_lookup, sine_lookup):
    half_size = values.shape[-1] // 2
    first_half = values[..., :half_size]
    second = values[..., half_size:]
    cosine_b = cosine_lookup[:, None, :]
    sine_b = sine_lookup[:, None, :]
    return jnp.concatenate(
        [first_half * cosine_b - second * sine_b, second * cosine_b + first_half * sine_b], axis=-1
    )


def rms_scale(values):
    return lax.rsqrt(jnp.mean(values * values, axis=-1, keepdims=True) + EPSILON)


def norm_back(grad_normed, normed, inv_rms, gain_vector):
    scaled = grad_normed * gain_vector
    return inv_rms * (scaled - normed * jnp.mean(scaled * normed, axis=-1, keepdims=True))


def contract_rows(left_side, right_side):
    return lax.dot_general(
        left_side, right_side, (((0,), (0,)), ((), ())), preferred_element_type=jnp.float32
    )


def contract_cols(left_side, right_side):
    return lax.dot_general(
        left_side, right_side, (((1,), (1,)), ((), ())), preferred_element_type=jnp.float32
    )


def as_column(vector, before=0):
    return jnp.pad(vector[:, None], ((0, 0), (0, 127 - before)))


def masked_softmax(logits, picked):
    kept = jnp.where(picked, logits, EXCLUDED)
    exponent = jnp.exp(kept - jnp.max(kept, axis=-1, keepdims=True))
    return exponent / jnp.sum(exponent, axis=-1, keepdims=True)


def max_dp(values):
    if lax.axis_size("dp") != 2:
        return lax.pmax(values, "dp")
    return jnp.maximum(values, lax.ppermute(values, "dp", [(0, 1), (1, 0)]))


def allowed_bias(position_ref, docs_all_ref, docs_own_ref):
    keys, rows = docs_all_ref.shape[0], docs_own_ref.shape[1]
    key_at = lax.broadcasted_iota(jnp.int32, (keys, rows), 0)
    row_at = lax.broadcasted_iota(jnp.int32, (keys, rows), 1) + position_ref[0]
    allowed = (key_at <= row_at) & (docs_all_ref[...] == docs_own_ref[...])
    return jnp.where(allowed, 0.0, EXCLUDED)


def attend_kernel(
    position_ref, docs_all_ref, docs_own_ref, query_ref, key_ref, value_ref,
    mix_ref, log_ref, top_ref, bias,
):
    @pl.when(pl.program_id(0) == 0)
    def _():
        bias[...] = allowed_bias(position_ref, docs_all_ref, docs_own_ref)

    rows = query_ref.shape[0]
    mixes, logs, tops = [], [], []
    for head in range(query_ref.shape[1] // HEAD_DIM):
        group = head * key_ref.shape[1] // query_ref.shape[1] * HEAD_DIM
        query = query_ref[:, head * HEAD_DIM : (head + 1) * HEAD_DIM]
        key = key_ref[:, group : group + HEAD_DIM]
        value = value_ref[:, group : group + HEAD_DIM]
        scores = contract_cols(key, query) + bias[...]
        top = jnp.max(scores, axis=0, keepdims=True)
        exponent = jnp.exp(scores - top)
        totals = jnp.sum(exponent, axis=0, keepdims=True)
        probs = (exponent * (1.0 / totals)).astype(jnp.bfloat16)
        mixes.append(contract_rows(value, probs))
        logs.append(top + jnp.log(totals))
        tops.append(top)
    mix_ref[...] = jnp.concatenate(mixes, axis=0).T.astype(jnp.bfloat16)
    blank = [jnp.zeros((8 - len(logs), rows), jnp.float32)]
    log_ref[0] = jnp.concatenate(logs + blank, axis=0)
    top_ref[0] = jnp.broadcast_to(
        jnp.max(jnp.concatenate(tops + blank, axis=0), axis=1, keepdims=True), (8, 128)
    )


def attend_back_kernel(
    position_ref, docs_all_ref, docs_own_ref, query_ref, key_ref, value_ref, mix_grad_ref, log_ref,
    query_grad_ref, key_grad_ref, value_grad_ref, bias,
):
    @pl.when(pl.program_id(0) == 0)
    def _():
        bias[...] = allowed_bias(position_ref, docs_all_ref, docs_own_ref)

    query_grads, key_grads, value_grads = [], {}, {}
    for head in range(query_ref.shape[1] // HEAD_DIM):
        group = head * key_ref.shape[1] // query_ref.shape[1] * HEAD_DIM
        query = query_ref[:, head * HEAD_DIM : (head + 1) * HEAD_DIM]
        mix_grad = mix_grad_ref[:, head * HEAD_DIM : (head + 1) * HEAD_DIM]
        key = key_ref[:, group : group + HEAD_DIM]
        value = value_ref[:, group : group + HEAD_DIM]
        scores = contract_cols(key, query) + bias[...]
        probs = jnp.exp(scores - log_ref[0, head : head + 1, :])
        prob_grads = contract_cols(value, mix_grad)
        centre = jnp.sum(probs * prob_grads, axis=0, keepdims=True)
        score_grads = (probs * (prob_grads - centre)).astype(jnp.bfloat16)
        query_grads.append(contract_rows(key, score_grads))
        key_term = jnp.dot(score_grads, query, preferred_element_type=jnp.float32)
        value_term = jnp.dot(
            probs.astype(jnp.bfloat16), mix_grad, preferred_element_type=jnp.float32
        )
        key_grads[group] = key_grads[group] + key_term if group in key_grads else key_term
        value_grads[group] = value_grads[group] + value_term if group in value_grads else value_term
    query_grad_ref[...] = jnp.concatenate(query_grads, axis=0).T
    for group in key_grads:
        key_grad_ref[:, group : group + HEAD_DIM] = key_grads[group]
        value_grad_ref[:, group : group + HEAD_DIM] = value_grads[group]


def attention_specs(rows, keys, query_width, key_width):
    whole = lambda shape: pl.BlockSpec(shape, lambda i: (0, 0))
    by_head = lambda count, width: pl.BlockSpec((count, width), lambda i: (0, i))
    steps = key_width // 128
    in_specs = [
        pl.BlockSpec(memory_space=pltpu.SMEM),
        whole((keys, 1)),
        whole((1, rows)),
        by_head(rows, query_width // steps),
        by_head(keys, 128),
        by_head(keys, 128),
    ]
    return steps, in_specs, by_head, pl.BlockSpec((1, 8, rows), lambda i: (i, 0, 0))


def attend(position, docs_all, docs_own, query, key, value):
    rows, query_width = query.shape
    keys, key_width = key.shape
    steps, in_specs, by_head, by_log = attention_specs(rows, keys, query_width, key_width)
    mix, logs, tops = pl.pallas_call(
        attend_kernel,
        grid=(steps,),
        in_specs=in_specs,
        out_specs=(
            by_head(rows, query_width // steps), by_log, pl.BlockSpec((1, 8, 128), lambda i: (i, 0, 0))
        ),
        out_shape=(
            jax.ShapeDtypeStruct((rows, query_width), jnp.bfloat16),
            jax.ShapeDtypeStruct((steps, 8, rows), jnp.float32),
            jax.ShapeDtypeStruct((steps, 8, 128), jnp.float32),
        ),
        scratch_shapes=[pltpu.VMEM((keys, rows), jnp.float32)],
        cost_estimate=pl.CostEstimate(
            flops=16 * rows * keys * query_width, bytes_accessed=8 * 2**20,
            transcendentals=rows * keys * QUERY_HEADS,
        ),
        compiler_params=pltpu.CompilerParams(vmem_limit_bytes=50 * 2**20),
    )(position, docs_all[:, None], docs_own[None, :], query, key, value)
    return mix, logs, tops[:, : QUERY_HEADS // steps, 0].reshape(QUERY_HEADS)


def attend_back(position, docs_all, docs_own, query, key, value, mix_grad, logs):
    rows, query_width = query.shape
    keys, key_width = key.shape
    steps, in_specs, by_head, by_log = attention_specs(rows, keys, query_width, key_width)
    wide = query_width // steps
    return pl.pallas_call(
        attend_back_kernel,
        grid=(steps,),
        in_specs=in_specs + [by_head(rows, wide), by_log],
        out_specs=(by_head(rows, wide), by_head(keys, 128), by_head(keys, 128)),
        out_shape=(
            jax.ShapeDtypeStruct((rows, query_width), jnp.float32),
            jax.ShapeDtypeStruct((keys, key_width), jnp.float32),
            jax.ShapeDtypeStruct((keys, key_width), jnp.float32),
        ),
        scratch_shapes=[pltpu.VMEM((keys, rows), jnp.float32)],
        cost_estimate=pl.CostEstimate(
            flops=40 * rows * keys * query_width, bytes_accessed=16 * 2**20,
            transcendentals=rows * keys * QUERY_HEADS,
        ),
        compiler_params=pltpu.CompilerParams(vmem_limit_bytes=50 * 2**20),
    )(position, docs_all[:, None], docs_own[None, :], query, key, value, mix_grad, logs)


def scatter_kernel(
    whole_a, whole_b, total_a, total_b, core_a, core_b, pair_a, pair_b, first_a, first_b, mid_a, mid_b,
    last_a, last_b, sums_a, sums_b, line_a, line_b,
    core_send, core_recv, first_send, first_recv, last_send, last_recv, line_send, line_recv,
):
    half, expert, depth = lax.axis_index("dp"), lax.axis_index("expert"), lax.axis_index("shard")
    side, core = expert // 2, expert % 2
    partner = {"dp": 1 - half}
    opposite = {"expert": 2 * ((side + 1) % 2) + core}
    sibling = {"expert": 2 * side + (core + 1) % 2}
    whole, total, from_core, pair_sum = (
        (whole_a, whole_b), (total_a, total_b), (core_a, core_b), (pair_a, pair_b)
    )
    first, mid, last, sums, from_line = (
        (first_a, first_b), (mid_a, mid_b), (last_a, last_b), (sums_a, sums_b), (line_a, line_b)
    )

    def along(distance):
        return {"shard": (depth + distance) % 4}

    barrier = pltpu.get_barrier_semaphore()
    for peer in (partner, opposite, sibling, along(1), along(2), along(3)):
        pl.semaphore_signal(barrier, inc=1, device_id=peer, device_id_type=pl.DeviceIdType.MESH)
    pl.semaphore_wait(barrier, 6)

    def remote(src, dst, send, recv, to):
        return pltpu.make_async_remote_copy(
            src_ref=src, dst_ref=dst, send_sem=send, recv_sem=recv, device_id=to,
            device_id_type=pl.DeviceIdType.MESH,
        )

    def added(a, b):
        return (a.astype(jnp.float32) + b.astype(jnp.float32)).astype(jnp.bfloat16)

    def chunk(j, other_core):
        return 4 * ((half + j // 2) % 2) + 2 * ((side + j % 2) % 2) + (core + other_core) % 2

    def to_core(w, j):
        return remote(
            whole[w].at[chunk(j, 1)], from_core[w].at[j], core_send.at[w, j], core_recv.at[w, j], sibling
        )

    def to_first(w, k):
        j = 2 + k if w == 0 else 2 * k + 1
        return remote(
            pair_sum[w].at[j], first[w].at[k], first_send.at[w, k], first_recv.at[w, k],
            (partner, opposite)[w],
        )

    def to_last(w):
        return remote(mid[w], last[w], last_send.at[w], last_recv.at[w], (opposite, partner)[w])

    def to_line(w, zi):
        return remote(
            sums[w].at[(depth + zi) % 4], from_line[w].at[zi], line_send.at[w, zi],
            line_recv.at[w, zi], along(zi),
        )

    for j in (3, 2, 1, 0):
        for w in range(2):
            to_core(w, j).start()
    for j in (3, 2, 1, 0):
        for w in range(2):
            to_core(w, j).wait_recv()
            pair_sum[w][j] = added(whole[w][chunk(j, 0)], from_core[w][j])
            if j == 3:
                to_first(w, 1).start()
            if j == 2 - w:
                to_first(w, 0).start()
    for w in range(2):
        to_first(w, 1).wait_recv()
        mid[w][...] = added(pair_sum[w][1 + w], first[w][1])
        to_last(w).start()
    share = sums_a.shape[1]
    for w in range(2):
        to_first(w, 0).wait_recv()
        to_last(w).wait_recv()
        full = (
            pair_sum[w][0].astype(jnp.float32)
            + first[w][0].astype(jnp.float32)
            + last[w][...].astype(jnp.float32)
        ).astype(jnp.bfloat16)
        for z in range(4):
            sums[w][z] = full[z * share : (z + 1) * share]
        for zi in (2, 1, 3):
            to_line(w, zi).start()
    for w in range(2):
        result = sums[w][depth].astype(jnp.float32)
        for zi in (1, 3, 2):
            to_line(w, zi).wait_recv()
            result = result + from_line[w][zi].astype(jnp.float32)
        total[w][...] = result
    for w in range(2):
        for j in range(4):
            to_core(w, j).wait_send()
        for k in range(2):
            to_first(w, k).wait_send()
        to_last(w).wait_send()
        for zi in range(1, 4):
            to_line(w, zi).wait_send()


def scatter_every(*arrays):
    if lax.axis_size("dp") != 2:
        return [
            lax.psum_scatter(a, EVERY, scatter_dimension=0, tiled=True).astype(jnp.float32)
            for a in arrays
        ]
    rows, low, dma = arrays[0].shape[0] // 8, arrays[0].dtype, pltpu.SemaphoreType.DMA
    widths = [a.shape[1] for a in arrays]
    both = lambda *shape: [pltpu.VMEM((*shape, w), low) for w in widths]
    in_vmem = pl.BlockSpec(memory_space=pltpu.VMEM)
    return pl.pallas_call(
        scatter_kernel,
        out_shape=tuple(jax.ShapeDtypeStruct((rows // 4, w), jnp.float32) for w in widths),
        in_specs=[in_vmem] * 2,
        out_specs=(in_vmem,) * 2,
        scratch_shapes=[
            *both(4, rows), *both(4, rows), *both(2, rows), *both(rows), *both(rows),
            *both(4, rows // 4), *both(4, rows // 4),
            dma((2, 4)), dma((2, 4)), dma((2, 2)), dma((2, 2)), dma((2,)), dma((2,)),
            dma((2, 4)), dma((2, 4)),
        ],
        compiler_params=pltpu.CompilerParams(
            collective_id=2, has_side_effects=True, vmem_limit_bytes=50 * 2**20
        ),
    )(*[a.reshape(8, rows, a.shape[1]) for a in arrays])


def gather_dp(rows):
    if lax.axis_size("dp") != 2:
        return lax.all_gather(rows, "dp", axis=0, tiled=True)
    other = lax.ppermute(rows, "dp", [(0, 1), (1, 0)])
    early = lax.axis_index("dp") == 0
    return jnp.concatenate(
        [jnp.where(early, rows, other), jnp.where(early, other, rows)], axis=0
    )


def scatter_dp(whole, dim):
    if lax.axis_size("dp") != 2:
        return lax.psum_scatter(
            whole.astype(jnp.bfloat16), "dp", scatter_dimension=dim, tiled=True
        ).astype(jnp.float32)
    size, at = whole.shape[dim] // 2, lax.axis_index("dp")
    given = lax.dynamic_slice_in_dim(whole, (1 - at) * size, size, dim).astype(jnp.bfloat16)
    taken = lax.ppermute(given, "dp", [(0, 1), (1, 0)])
    kept = lax.dynamic_slice_in_dim(whole, at * size, size, dim)
    return kept.astype(jnp.float32) + taken.astype(jnp.float32)


def weights_kernel(first_ref, second_ref, first_full, second_full, own_sem, send_sem, recv_sem):
    pair, expert, depth = lax.axis_index("dp"), lax.axis_index("expert"), lax.axis_index("shard")
    side, core = expert // 2, expert % 2
    half = pair % 2
    partner = {"dp": pair + 1 - 2 * half}
    opposite = {"expert": 2 * ((side + 1) % 2) + core}
    sibling = {"expert": 2 * side + (core + 1) % 2}
    rows = first_ref.shape[0]
    part = rows // 8
    arrays = ((first_ref, first_full), (second_ref, second_full))

    def along(distance):
        return {"shard": (depth + distance) % 4}

    barrier = pltpu.get_barrier_semaphore()
    for peer in (partner, opposite, sibling, along(1), along(2), along(3)):
        pl.semaphore_signal(barrier, inc=1, device_id=peer, device_id_type=pl.DeviceIdType.MESH)
    pl.semaphore_wait(barrier, 6)

    def eighth(px, pa, pc):
        return 4 * ((half + px) % 2) + 2 * ((side + pa) % 2) + (core + pc) % 2

    def place(full, zi, px, pa, pc):
        start = ((depth + zi) % 4) * rows + eighth(px, pa, pc) * part
        return full.at[pl.ds(pl.multiple_of(start, part), part)]

    def copy(which, zi, source, hop, to):
        px, pa, pc = source
        full = arrays[which][1]
        there = 4 * (px ^ hop[0]) + 2 * (pa ^ hop[1]) + (pc ^ hop[2])
        return pltpu.make_async_remote_copy(
            src_ref=place(full, zi, px, pa, pc),
            dst_ref=place(full, zi, px, pa, pc),
            send_sem=send_sem.at[which, zi, there],
            recv_sem=recv_sem.at[which, zi, there],
            device_id=to,
            device_id_type=pl.DeviceIdType.MESH,
        )

    def along_line(which, zi):
        own, full = arrays[which]
        start = eighth(0, 0, 0) * part
        return pltpu.make_async_remote_copy(
            src_ref=own.at[pl.ds(pl.multiple_of(start, part), part)],
            dst_ref=full.at[pl.ds(pl.multiple_of(depth * rows + start, part), part)],
            send_sem=send_sem.at[which, zi, 0],
            recv_sem=recv_sem.at[which, zi, 0],
            device_id=along(4 - zi),
            device_id_type=pl.DeviceIdType.MESH,
        )

    own_copies = [
        pltpu.make_async_copy(
            own, full.at[pl.ds(pl.multiple_of(depth * rows, rows), rows)], own_sem.at[which]
        )
        for which, (own, full) in enumerate(arrays)
    ]
    near, over, by = (1, 0, 0), (0, 1, 0), (0, 0, 1)
    for which in range(2):
        for zi in (1, 3, 2):
            along_line(which, zi).start()
    for own_copy in own_copies:
        own_copy.start()
    for which in range(2):
        for zi in (1, 3, 2):
            along_line(which, zi).wait_recv()
            copy(which, zi, (0, 0, 0), near, partner).start()
            copy(which, zi, (0, 0, 0), over, opposite).start()
            copy(which, zi, (0, 0, 0), by, sibling).start()
        for zi in (1, 3, 2):
            copy(which, zi, (0, 0, 0), near, partner).wait_recv()
            copy(which, zi, (1, 0, 0), by, sibling).start()

            @pl.when(core == 0)
            def _():
                copy(which, zi, (1, 0, 0), over, opposite).start()

            copy(which, zi, (0, 0, 0), over, opposite).wait_recv()
            copy(which, zi, (0, 1, 0), by, sibling).start()

            @pl.when(core == 1)
            def _():
                copy(which, zi, (0, 1, 0), near, partner).start()

    for which in range(2):
        for zi in (1, 3, 2):
            copy(which, zi, (1, 0, 0), over, opposite).wait_recv()
            copy(which, zi, (1, 1, 0), by, sibling).start()
    for which in range(2):
        for zi in (1, 3, 2):
            for px, pa in ((0, 0), (1, 0), (0, 1), (1, 1)):
                copy(which, zi, (px, pa, 0), by, sibling).wait()
            along_line(which, zi).wait_send()
            copy(which, zi, (0, 0, 0), near, partner).wait_send()
            copy(which, zi, (0, 0, 0), over, opposite).wait_send()

            @pl.when(core == 0)
            def _():
                copy(which, zi, (1, 0, 0), over, opposite).wait_send()

            @pl.when(core == 1)
            def _():
                copy(which, zi, (0, 1, 0), near, partner).wait_send()

    for own_copy in own_copies:
        own_copy.wait()


def gather_weights(first, second):
    anywhere = pl.BlockSpec(memory_space=pl.ANY)
    dma = pltpu.SemaphoreType.DMA
    return pl.pallas_call(
        weights_kernel,
        out_shape=tuple(
            jax.ShapeDtypeStruct((4 * part.shape[0], part.shape[1]), part.dtype)
            for part in (first, second)
        ),
        in_specs=[anywhere] * 2,
        out_specs=(anywhere,) * 2,
        scratch_shapes=[dma((2,)), dma((2, 4, 8)), dma((2, 4, 8))],
        compiler_params=pltpu.CompilerParams(collective_id=1, has_side_effects=True),
    )(first, second)


def experts_kernel(
    in_pairs, hidden_ref, cot_ref, router_ref, win_ref, wout_ref,
    rows_ref, kept_ref, core_ref, across_ref, near_ref, far_ref, stage_ref, out_ref, dwin_ref, dwout_ref, given_in, given_out,
    acc_in, acc_out, win, wout, router, row_tile, cot_tile, made, out_tile, parts,
    load_sem, tile_sem, row_recv, core_send, across_send, line_send,
    made_sem, part_sem, core_recv, across_recv, near_recv, far_recv,
    stage_sem, stage_send, store_sem, out_sem,
):
    own_count, width = wout_ref.shape[0], wout_ref.shape[1]
    rows_own, model = hidden_ref.shape[0] - 16, hidden_ref.shape[1]
    tile = rows_own // 2
    expert, depth = lax.axis_index("expert"), lax.axis_index("shard")
    side, core = expert // 2, expert % 2
    sibling = {"expert": 2 * side + (core + 1) % 2}
    opposite = {"expert": 2 * ((side + 1) % 2) + core}

    near = {"shard": depth + 1 - 2 * (depth % 2)}
    far = {"shard": (depth + 2) % 4}

    def remote(src, dst, send, recv, to):
        return pltpu.make_async_remote_copy(
            src_ref=src, dst_ref=dst, send_sem=send, recv_sem=recv, device_id=to,
            device_id_type=pl.DeviceIdType.MESH,
        )

    barrier = pltpu.get_barrier_semaphore()
    half = lax.axis_index("dp")
    peers = [sibling, opposite, near, far]
    for peer in peers:
        pl.semaphore_signal(barrier, inc=1, device_id=peer, device_id_type=pl.DeviceIdType.MESH)
    pl.semaphore_wait(barrier, len(peers))

    loads = [
        pltpu.make_async_copy(win_ref, win, load_sem.at[0]),
        pltpu.make_async_copy(wout_ref, wout, load_sem.at[1]),
        pltpu.make_async_copy(router_ref, router, load_sem.at[2]),
    ]

    def to_sibling(src, r):
        return remote(src, rows_ref.at[r + 1], core_send.at[r // 2], row_recv.at[r + 1], sibling)

    def to_opposite(src, r):
        return remote(src, rows_ref.at[r + 2], across_send.at[r // 4], row_recv.at[r + 2], opposite)

    def to_near():
        return remote(hidden_ref, rows_ref.at[4], line_send.at[0], row_recv.at[4], near)

    def to_far():
        return remote(hidden_ref, rows_ref.at[8], line_send.at[1], row_recv.at[8], far)

    def far_to_near():
        return remote(rows_ref.at[8], rows_ref.at[12], line_send.at[2], row_recv.at[12], near)

    def own_rows():
        return pltpu.make_async_copy(hidden_ref, rows_ref.at[0], row_recv.at[0])

    to_sibling(hidden_ref, 0).start()
    to_opposite(hidden_ref, 0).start()
    to_far().start()
    own_rows().start()
    for load in loads:
        load.start()

    def arrive(r):
        @pl.when(r == 0)
        def _():
            own_rows().wait()

        @pl.when(r > 0)
        def _():
            remote(
                rows_ref.at[r], rows_ref.at[r], core_send.at[0], row_recv.at[r], sibling
            ).wait_recv()

            @pl.when(r % 2 == 0)
            def _():
                to_sibling(rows_ref.at[r], r).start()

            @pl.when(r % 4 == 0)
            def _():
                to_opposite(rows_ref.at[r], r).start()

            @pl.when(r == 8)
            def _():
                far_to_near().start()

    pair_order = (0, 1, 4, 5, 7, 6, 3, 2)

    def block_at(step):
        turn = step // 2
        place = turn // 2
        pair = 0
        for i, value in enumerate(pair_order):
            pair = pair + value * (1 - ((place + 8 - i) % 8 + 7) // 8)
        return 2 * pair + (turn + (7 - place) // 7) % 2

    def first_row(step):
        r, sub = block_at(step), step % 2
        other = 2 * ((side + (r % 4) // 2) % 2) + (core + r) % 2
        plane = 2 * ((depth // 2 + r // 8) % 2) + (depth + r // 4) % 2
        return pl.multiple_of((other * 4 + plane) * rows_own + sub * tile, tile)

    def keep_out(step):
        return pltpu.make_async_copy(
            out_tile.at[step % 2], out_ref.at[pl.ds(first_row(step), tile)], out_sem.at[step % 2]
        )

    def tiles(step):
        r, sub, slot = block_at(step), step % 2, step % 2
        start = first_row(step)
        return (
            pltpu.make_async_copy(
                rows_ref.at[r, pl.ds(pl.multiple_of(sub * tile, tile), tile)],
                row_tile.at[slot], tile_sem.at[0, slot],
            ),
            pltpu.make_async_copy(
                cot_ref.at[pl.ds(start, tile)], cot_tile.at[slot], tile_sem.at[1, slot]
            ),
        )

    acc_in[...] = jnp.zeros_like(acc_in)
    acc_out[...] = jnp.zeros_like(acc_out)
    arrive(1)
    for copy in tiles(0):
        copy.start()
    for load in loads:
        load.wait()

    def send_made(step):
        r, sub, slot = block_at(step), step % 2, step % 2
        return remote(
            made.at[slot], core_ref.at[r // 2, sub], made_sem.at[slot],
            core_recv.at[r // 2, sub], sibling,
        )

    def keep_made(step):
        r, sub, slot = block_at(step), step % 2, step % 2
        return pltpu.make_async_copy(made.at[slot], kept_ref.at[r // 2, sub], made_sem.at[slot])

    def made_done(step):
        away = block_at(step) % 2

        @pl.when(away == 1)
        def _():
            send_made(step).wait_send()

        @pl.when(away == 0)
        def _():
            keep_made(step).wait()

    def send_across(zi, slot, sub):
        return remote(
            stage_ref.at[slot, sub], across_ref.at[zi, sub], stage_send.at[slot, sub],
            across_recv.at[zi, sub], opposite,
        )

    def send_near(zi, slot, sub):
        return remote(
            stage_ref.at[slot, sub], near_ref.at[zi // 2, sub], stage_send.at[slot, sub],
            near_recv.at[zi // 2, sub], near,
        )

    def send_far(sub):
        return remote(
            stage_ref.at[5, sub], far_ref.at[sub], stage_send.at[5, sub], far_recv.at[sub], far
        )

    def staged(slot, sub):
        return pltpu.make_async_copy(parts.at[0], stage_ref.at[slot, sub], stage_sem.at[0])

    def core_arrived(pair, sub):
        remote(
            made.at[0], core_ref.at[pair, sub], made_sem.at[0], core_recv.at[pair, sub], sibling
        ).wait_recv()

    def fetch(source, place):
        return pltpu.make_async_copy(source, parts.at[place], part_sem.at[place])

    def begin_one(kind, zi, sub):
        pair = 2 * zi + (1 if kind == "y" else 0)
        core_arrived(pair, sub)
        fetch(kept_ref.at[pair, sub], 0).start()
        fetch(core_ref.at[pair, sub], 1).start()
        if kind != "y":
            send_across(zi, 0, sub).wait_recv()
            fetch(across_ref.at[zi, sub], 2).start()
        if kind == "d":
            send_near(zi, 0, sub).wait_recv()
            fetch(near_ref.at[zi // 2, sub], 3).start()

    def end_one(kind, zi, slot, sub):
        pair = 2 * zi + (1 if kind == "y" else 0)
        fetch(kept_ref.at[pair, sub], 0).wait()
        fetch(core_ref.at[pair, sub], 1).wait()
        total = parts[0].astype(jnp.float32) + parts[1].astype(jnp.float32)
        if kind != "y":
            fetch(across_ref.at[zi, sub], 2).wait()
            total = total + parts[2].astype(jnp.float32)
        if kind == "d":
            fetch(near_ref.at[zi // 2, sub], 3).wait()
            total = total + parts[3].astype(jnp.float32)
        parts[0] = total.astype(jnp.bfloat16)
        staged(slot, sub).start()

    def send_one(kind, zi, slot, sub):
        staged(slot, sub).wait()
        if kind == "y":
            send_across(zi, slot, sub).start()
        if kind == "c":
            send_near(zi, slot, sub).start()
        if kind == "d":
            send_far(sub).start()

    between = (("y", 16, 2, 1), ("y", 20, 3, 0), ("y", 24, 0, 4), ("c", 26, 3, 2), ("y", 28, 1, 3))
    after_all = (("d", 2, 5), ("c", 1, 6))

    def at_stage(step, act):
        for kind, begin, zi, slot in between:
            @pl.when((step == begin) | (step == begin + 1))
            def _():
                act(kind, zi, slot)

    first = (expert * 4 + depth) * own_count

    def body(step, carry):
        slot, sub = step % 2, step % 2
        for copy in tiles(step):
            copy.wait()

        @pl.when(step < 31)
        def _():
            after = block_at(step + 1)

            @pl.when((step % 2 == 1) & ((after % 4 != 0) | (after == 0)))
            def _():
                arrive(after)

            @pl.when(step == 10)
            def _():
                to_near().start()

            for early, r in ((7, 8), (11, 12), (16, 4)):
                @pl.when(step == early)
                def _():
                    arrive(jnp.int32(r))

            for copy in tiles(step + 1):
                copy.start()

        at_stage(step - 1, lambda kind, zi, slot: send_one(kind, zi, slot, 1 - sub))
        at_stage(step, lambda kind, zi, slot: begin_one(kind, zi, sub))

        @pl.when(step >= 2)
        def _():
            made_done(step - 2)
            keep_out(step - 2).wait()

        rows, cot = row_tile[slot], cot_tile[slot, :, :model]
        logits = jnp.dot(rows, router[...], preferred_element_type=jnp.float32)
        lanes = lax.broadcasted_iota(jnp.int32, logits.shape, 1)
        routes = cot_tile[slot, :, model:].astype(jnp.float32).astype(jnp.int32)
        picked = lanes == routes[:, 0:1]
        for k in range(1, TOP):
            picked = picked | (lanes == routes[:, k : k + 1])
        gates = masked_softmax(logits, picked)
        out_sum = grad_sum = None
        gate_lanes = lax.broadcasted_iota(jnp.int32, (tile, 128), 1)
        gate_grads = jnp.zeros((tile, 128), jnp.float32)
        for e in range(own_count):
            gate = jnp.sum(jnp.where(lanes == first + e, gates, 0.0), axis=1, keepdims=True)
            both = jnp.dot(rows, win[e], preferred_element_type=jnp.float32)
            gate_part, up_part = both[:, :width], both[:, width:]
            sig = jax.nn.sigmoid(gate_part)
            activated = gate_part * sig
            hidden = (activated * up_part).astype(jnp.bfloat16).astype(jnp.float32)
            gated = (gate * hidden).astype(jnp.bfloat16)
            term = jnp.dot(gated, wout[e], preferred_element_type=jnp.float32)
            out_sum = term if out_sum is None else out_sum + term
            plain = contract_cols(cot, wout[e])
            own_grad = jnp.sum(plain * hidden, axis=1, keepdims=True)
            high = own_grad.astype(jnp.bfloat16).astype(jnp.float32)
            gate_grads = jnp.where(gate_lanes == first + e, high, gate_grads)
            gate_grads = jnp.where(gate_lanes == 64 + first + e, own_grad - high, gate_grads)
            back = gate * plain
            d_gate = back * up_part * sig * (1.0 + gate_part * (1.0 - sig))
            d_up = back * activated
            d_both = jnp.concatenate([d_gate, d_up], axis=1).astype(jnp.bfloat16)
            term = contract_cols(d_both, win[e])
            grad_sum = term if grad_sum is None else grad_sum + term
            acc_in[e] += contract_rows(rows, d_both)
            acc_out[e] += contract_rows(gated, cot)
        made[slot, :, :model] = grad_sum.astype(jnp.bfloat16)
        made[slot, :, model:] = gate_grads.astype(jnp.bfloat16)
        out_tile[slot] = out_sum.astype(jnp.bfloat16)
        keep_out(step).start()

        away = block_at(step) % 2

        @pl.when(away == 1)
        def _():
            send_made(step).start()

        @pl.when(away == 0)
        def _():
            keep_made(step).start()

        at_stage(step, lambda kind, zi, slot: end_one(kind, zi, slot, sub))
        return carry

    lax.fori_loop(0, 32, body, 0)
    win[...] = acc_in[...].astype(jnp.bfloat16)
    wout[...] = acc_out[...].astype(jnp.bfloat16)
    grads = ((acc_in, win, dwin_ref, given_in), (acc_out, wout, dwout_ref, given_out))

    def half_rows(ref, at):
        size = ref.shape[1] // 2
        return ref.at[:, pl.ds(pl.multiple_of(at * size, size), size)]

    stores = []
    for which, (total, low, result, given) in enumerate(grads):
        if in_pairs:
            stores.append(
                pltpu.make_async_copy(half_rows(low, 1 - half), given, store_sem.at[which, 0])
            )
            stores.append(
                pltpu.make_async_copy(half_rows(total, half), result, store_sem.at[which, 1])
            )
        else:
            stores.append(pltpu.make_async_copy(low, result, store_sem.at[which, 0]))
    for store in stores:
        store.start()
    for kind, zi, slot in after_all:
        for sub in range(2):
            begin_one(kind, zi, sub)
            end_one(kind, zi, slot, sub)
            send_one(kind, zi, slot, sub)
    made_done(30)
    made_done(31)
    keep_out(30).wait()
    keep_out(31).wait()
    for sub in range(2):
        core_arrived(0, sub)
        send_across(0, 4, sub).wait()
        send_near(0, 0, sub).wait_recv()
        send_far(sub).wait()
        for zi, slot in ((2, 1), (3, 0), (1, 3)):
            send_across(zi, slot, sub).wait_send()
        send_near(3, 2, sub).wait_send()
        send_near(1, 6, sub).wait_send()
    for r in range(0, 16, 2):
        to_sibling(hidden_ref, r).wait_send()
    for r in range(0, 16, 4):
        to_opposite(hidden_ref, r).wait_send()
    to_near().wait_send()
    to_far().wait_send()
    far_to_near().wait_send()
    for store in stores:
        store.wait()


def experts_pass(hidden, cotangent, w_router, expert_in, expert_out):
    rows_own, model = hidden.shape[0] - 16, hidden.shape[1]
    tile = rows_own // 2
    wide = model + 128
    anywhere = pl.BlockSpec(memory_space=pl.ANY)
    low = jnp.bfloat16
    kept = jax.ShapeDtypeStruct((8, 2, tile, wide), low)
    quarter = jax.ShapeDtypeStruct((4, 2, tile, wide), low)
    dma = pltpu.SemaphoreType.DMA
    in_pairs = lax.axis_size("dp") == 2
    share = lambda w: (w.shape[0], w.shape[1] // 2 if in_pairs else w.shape[1], w.shape[2])
    results = pl.pallas_call(
        functools.partial(experts_kernel, in_pairs),
        out_shape=(
            jax.ShapeDtypeStruct((16, rows_own + 16, model), low),
            kept,
            kept,
            quarter,
            jax.ShapeDtypeStruct((2, 2, tile, wide), low),
            jax.ShapeDtypeStruct((2, tile, wide), low),
            jax.ShapeDtypeStruct((7, 2, tile, wide), low),
            jax.ShapeDtypeStruct((16 * rows_own, model), low),
            jax.ShapeDtypeStruct(share(expert_in), jnp.float32 if in_pairs else low),
            jax.ShapeDtypeStruct(share(expert_out), jnp.float32 if in_pairs else low),
            jax.ShapeDtypeStruct(share(expert_in), low),
            jax.ShapeDtypeStruct(share(expert_out), low),
        ),
        in_specs=[anywhere] * 5,
        out_specs=(anywhere,) * 12,
        scratch_shapes=[
            pltpu.VMEM(expert_in.shape, jnp.float32),
            pltpu.VMEM(expert_out.shape, jnp.float32),
            pltpu.VMEM(expert_in.shape, low),
            pltpu.VMEM(expert_out.shape, low),
            pltpu.VMEM(w_router.shape, low),
            pltpu.VMEM((2, tile, model), low),
            pltpu.VMEM((2, tile, cotangent.shape[1]), low),
            pltpu.VMEM((2, tile, wide), low),
            pltpu.VMEM((2, tile, model), low),
            pltpu.VMEM((4, tile, wide), low),
            dma((3,)), dma((2, 2)), dma((16,)), dma((8,)), dma((4,)), dma((3,)),
            dma((2,)), dma((4,)), dma((8, 2)), dma((4, 2)), dma((2, 2)), dma((2,)),
            dma((1,)), dma((7, 2)), dma((2, 2)), dma((2,)),
        ],
        compiler_params=pltpu.CompilerParams(
            collective_id=0, has_side_effects=True, vmem_limit_bytes=60 * 2**20
        ),
    )(hidden, cotangent, w_router, expert_in, expert_out)
    rows, kept, core, across, near, far, _, partial_out, *grads = results
    total = kept[0].astype(jnp.float32) + core[0].astype(jnp.float32)
    total = total + across[0].astype(jnp.float32)
    total = total + near[0].astype(jnp.float32) + far.astype(jnp.float32)
    if in_pairs:
        swap = lambda given: lax.ppermute(given, "dp", [(0, 1), (1, 0)])
        weight_in_grad, weight_out_grad = (grads[0], swap(grads[2])), (grads[1], swap(grads[3]))
    else:
        weight_in_grad, weight_out_grad = (scatter_dp(grads[0], 1),), (scatter_dp(grads[1], 1),)
    branch = lax.psum_scatter(partial_out, GROUP, scatter_dimension=0, tiled=True)
    summed = total.reshape(rows_own, wide)
    return summed, branch, rows[:, rows_own, :128], weight_in_grad, weight_out_grad


def on_device(
    tokens,
    cotangent,
    gain_attn,
    w_query,
    key_weight,
    value_weight,
    w_output,
    gain_ffn,
    w_router,
    expert_in,
    expert_out,
    routes,
    doc_ids,
    threshold,
):
    inputs = tokens[0].astype(jnp.float32)
    token_matrix, model_width = inputs.shape
    query_per_key = QUERY_HEADS // KEY_VALUE_HEADS
    query_width, key_width = w_query.shape[1], key_weight.shape[1]
    route_columns = jnp.pad(routes[0].astype(jnp.bfloat16), ((0, 0), (0, 128 - TOP)))
    all_cotangent = lax.all_gather(
        jnp.concatenate([cotangent[0], route_columns], axis=1), GROUP, axis=0, tiled=True
    )
    scale_attn = rms_scale(inputs)
    normed_attn = inputs * scale_attn
    hidden_attn = (normed_attn * gain_attn).astype(jnp.bfloat16)
    full_qkv, full_output = gather_weights(
        jnp.concatenate([w_query, key_weight, value_weight], axis=1), w_output
    )
    full_query = full_qkv[:, :query_width]
    full_key = full_qkv[:, query_width : query_width + key_width]
    full_value = full_qkv[:, query_width + key_width :]
    own_positions = lax.axis_index("dp") * token_matrix + jnp.arange(token_matrix)
    local_cosine, local_sine = rope_tables(own_positions, HEAD_DIM)
    projected = jnp.dot(hidden_attn, full_qkv, preferred_element_type=jnp.float32)
    query_proj = projected[:, :query_width]
    key_projected = projected[:, query_width : query_width + key_width]
    value_proj = projected[:, query_width + key_width :]
    query_rotated = (
        apply_rotary(
            query_proj.reshape(token_matrix, QUERY_HEADS, HEAD_DIM), local_cosine, local_sine
        )
        * 0.125
    ).astype(jnp.bfloat16)
    key_rotated = (
        apply_rotary(
            key_projected.reshape(token_matrix, KEY_VALUE_HEADS, HEAD_DIM), local_cosine, local_sine
        )
        .astype(jnp.bfloat16)
        .reshape(token_matrix, KEY_VALUE_HEADS * HEAD_DIM)
    )
    value_low = value_proj.astype(jnp.bfloat16)
    own_docs = doc_ids[0]
    both_gathered = gather_dp(jnp.concatenate([key_rotated, value_low], axis=1))
    gathered_keys, gathered_values = both_gathered[:, :key_width], both_gathered[:, key_width:]
    docs_all = lax.all_gather(own_docs, "dp", axis=0, tiled=True)
    attn_low, log_totals, head_max = attend(
        own_positions[:1], docs_all, own_docs, query_rotated.reshape(token_matrix, query_width),
        gathered_keys, gathered_values,
    )
    branch_attn = contract_cols(attn_low, full_output)
    residual = inputs + branch_attn
    scale_ffn = rms_scale(residual)
    normed_ffn = residual * scale_ffn
    hidden_ffn = (normed_ffn * gain_ffn).astype(jnp.bfloat16)
    expert_count = w_router.shape[1]
    router_logits = jnp.dot(hidden_ffn, w_router, preferred_element_type=jnp.float32)
    route_ids = routes[0]
    picked = (route_ids[:, :, None] == jnp.arange(expert_count)[None, None, :]).any(axis=1)
    gate_weights = masked_softmax(router_logits, picked)
    grad_out = cotangent[0].astype(jnp.float32)
    high = lax.reduce_precision(head_max, 8, 7)
    middle = lax.reduce_precision(head_max - high, 8, 7)
    in_three = jnp.concatenate([high, middle, head_max - high - middle]).astype(jnp.bfloat16)
    extra = jnp.broadcast_to(
        jnp.pad(in_three, (0, hidden_ffn.shape[1] - in_three.shape[0])), (16, hidden_ffn.shape[1])
    )
    summed, branch_ffn, maxima, in_parts, out_parts = experts_pass(
        jnp.concatenate([hidden_ffn, extra], axis=0), all_cotangent, w_router, expert_in, expert_out
    )
    model = hidden_ffn.shape[1]
    maxima = maxima.astype(jnp.float32)
    largest = jnp.max(
        maxima[:, :QUERY_HEADS]
        + maxima[:, QUERY_HEADS : 2 * QUERY_HEADS]
        + maxima[:, 2 * QUERY_HEADS : 3 * QUERY_HEADS],
        axis=0,
    )
    largest = max_dp(largest)
    grad_hidden_ffn = summed[:, :model]
    gate_cols = summed[:, model:]
    grad_gates = gate_cols[:, :expert_count] + gate_cols[:, 64 : 64 + expert_count]
    weighted = gate_weights * jnp.where(picked, grad_gates, 0.0)
    grad_logits = (
        weighted - gate_weights * jnp.sum(weighted, axis=-1, keepdims=True)
    ).astype(jnp.bfloat16)
    router_grad = contract_rows(hidden_ffn, grad_logits)
    grad_hidden_ffn = grad_hidden_ffn + contract_cols(grad_logits, w_router)
    gain_ffn_grad = jnp.sum(grad_hidden_ffn * normed_ffn, axis=0)
    grad_residual = grad_out + norm_back(grad_hidden_ffn, normed_ffn, scale_ffn, gain_ffn)
    grad_branch = grad_residual.astype(jnp.bfloat16)
    output_grad = contract_rows(grad_branch, attn_low)
    late_grads = jnp.concatenate(
        [output_grad, router_grad, as_column(gain_ffn_grad, expert_count)], axis=1
    ).astype(jnp.bfloat16)
    attention_gradient = jnp.dot(
        grad_branch, full_output, preferred_element_type=jnp.float32
    ).astype(jnp.bfloat16)
    grad_query_rows, key_gradient, value_gradient = attend_back(
        own_positions[:1], docs_all, own_docs, query_rotated.reshape(token_matrix, query_width),
        gathered_keys, gathered_values, attention_gradient, log_totals,
    )
    both_own = scatter_dp(
        jnp.concatenate([key_gradient, value_gradient], axis=1), 0
    )
    local_key_gradient, value_grad_own = both_own[:, :key_width], both_own[:, key_width:]
    key_grad_low = (
        apply_rotary(
            local_key_gradient.reshape(token_matrix, KEY_VALUE_HEADS, HEAD_DIM),
            local_cosine,
            -local_sine,
        )
        .reshape(token_matrix, KEY_VALUE_HEADS * HEAD_DIM)
        .astype(jnp.bfloat16)
    )
    value_grad_low = value_grad_own.astype(jnp.bfloat16)
    query_grad_rows = grad_query_rows.reshape(token_matrix, QUERY_HEADS, HEAD_DIM)
    query_grad_low = (
        (apply_rotary(query_grad_rows, local_cosine, -local_sine) * 0.125)
        .reshape(token_matrix, QUERY_HEADS * HEAD_DIM)
        .astype(jnp.bfloat16)
    )
    all_grad_low = jnp.concatenate([query_grad_low, key_grad_low, value_grad_low], axis=1)
    attn_sums, late_sums = scatter_every(
        contract_rows(hidden_attn, all_grad_low).astype(jnp.bfloat16), late_grads
    )
    attn_sums, late_sums, branch_ffn, in_parts, out_parts = lax.optimization_barrier(
        (attn_sums, late_sums, branch_ffn, in_parts, out_parts)
    )
    out = (residual + branch_ffn.astype(jnp.float32)).astype(jnp.bfloat16)
    grad_in_shard = sum(p.astype(jnp.float32) for p in in_parts)
    grad_out_shard = sum(p.astype(jnp.float32) for p in out_parts)
    grad_hidden_attn = contract_cols(all_grad_low, full_qkv)
    grad_inputs = grad_residual + norm_back(grad_hidden_attn, normed_attn, scale_attn, gain_attn)
    share = attn_sums.shape[0]
    first_row = (
        (lax.axis_index("dp") * lax.axis_size("expert") + lax.axis_index("expert"))
        * lax.axis_size("shard")
        + lax.axis_index("shard")
    ) * share
    own_rows = lax.dynamic_slice_in_dim(full_qkv, first_row, share, 0)
    own_gain = lax.dynamic_slice_in_dim(gain_attn, first_row, share, 0)
    gain_attn_grad = jnp.sum(own_rows.astype(jnp.float32) * attn_sums, axis=1) / own_gain
    clip_limit = threshold[0].astype(jnp.float32)
    shrink_factor = clip_limit / jnp.maximum(largest, clip_limit)
    query_scale = jnp.repeat(jnp.sqrt(shrink_factor), HEAD_DIM)
    key_shrink = jnp.repeat(
        jnp.sqrt(jnp.min(shrink_factor.reshape(KEY_VALUE_HEADS, query_per_key), axis=1)), HEAD_DIM
    )
    clipped_query = (w_query.astype(jnp.float32) * query_scale[None, :]).astype(jnp.bfloat16)
    clipped_key = (key_weight.astype(jnp.float32) * key_shrink[None, :]).astype(jnp.bfloat16)
    return (
        out[None],
        grad_inputs.astype(jnp.bfloat16)[None],
        gain_attn_grad,
        attn_sums[:, :query_width],
        attn_sums[:, query_width : query_width + key_width],
        attn_sums[:, query_width + key_width : query_width + 2 * key_width],
        late_sums[:, :query_width],
        late_sums[:, query_width + expert_count],
        late_sums[:, query_width : query_width + expert_count],
        grad_in_shard,
        grad_out_shard,
        largest,
        clipped_query,
        clipped_key,
    )


def solution(mesh):
    return jax.shard_map(
        on_device,
        mesh=mesh,
        in_specs=(
            P(("expert", "shard"), "dp", None),
            P(("expert", "shard"), "dp", None),
            P(),
            P("shard", None),
            P("shard", None),
            P("shard", None),
            P("shard", None),
            P(),
            P(),
            P(("expert", "shard"), None, None),
            P(("expert", "shard"), None, None),
            P(("expert", "shard"), "dp", None),
            P(("expert", "shard"), "dp"),
            P(),
        ),
        out_specs=(
            P(("expert", "shard"), "dp", None),
            P(("expert", "shard"), "dp", None),
            P(("dp", "expert", "shard")),
            P(("dp", "expert", "shard"), None),
            P(("dp", "expert", "shard"), None),
            P(("dp", "expert", "shard"), None),
            P(("dp", "expert", "shard"), None),
            P(("dp", "expert", "shard")),
            P(("dp", "expert", "shard"), None),
            P(("expert", "shard"), "dp", None),
            P(("expert", "shard"), "dp", None),
            P(),
            P("shard", None),
            P("shard", None),
        ),
        check_vma=False,
    )
```

```python
import functools
import math

import jax
import jax.numpy as jnp
from jax import lax
from jax.experimental import pallas as pl
from jax.experimental.pallas import tpu as pltpu
from jax.sharding import PartitionSpec as P

QUERY_HEADS = 24
KEY_VALUE_HEADS = 8
HEAD_DIM = 64
TOP = 8
GROUP = ("expert", "shard")
EVERY = ("dp", "expert", "shard")

EPSILON = 1e-06
EXCLUDED = -1e30


def rope_tables(positions, head_size):
    half_size = head_size // 2
    frequency = jnp.exp(
        jnp.arange(half_size).astype(jnp.float32) * (-2.0 * math.log(10000.0) / head_size)
    )
    angles = positions.astype(jnp.float32)[:, None] * frequency[None, :]
    return (jnp.cos(angles), jnp.sin(angles))


def apply_rotary(values, cosine_lookup, sine_lookup):
    half_size = values.shape[-1] // 2
    first_half = values[..., :half_size]
    second = values[..., half_size:]
    cosine_b = cosine_lookup[:, None, :]
    sine_b = sine_lookup[:, None, :]
    return jnp.concatenate(
        [first_half * cosine_b - second * sine_b, second * cosine_b + first_half * sine_b], axis=-1
    )


def rms_scale(values):
    return lax.rsqrt(jnp.mean(values * values, axis=-1, keepdims=True) + EPSILON)


def norm_back(grad_normed, normed, inv_rms, gain_vector):
    scaled = grad_normed * gain_vector
    return inv_rms * (scaled - normed * jnp.mean(scaled * normed, axis=-1, keepdims=True))


def contract_rows(left_side, right_side):
    return lax.dot_general(
        left_side, right_side, (((0,), (0,)), ((), ())), preferred_element_type=jnp.float32
    )


def contract_cols(left_side, right_side):
    return lax.dot_general(
        left_side, right_side, (((1,), (1,)), ((), ())), preferred_element_type=jnp.float32
    )


def as_column(vector, before=0):
    return jnp.pad(vector[:, None], ((0, 0), (0, 127 - before)))


def masked_softmax(logits, picked):
    kept = jnp.where(picked, logits, EXCLUDED)
    exponent = jnp.exp(kept - jnp.max(kept, axis=-1, keepdims=True))
    return exponent / jnp.sum(exponent, axis=-1, keepdims=True)


def max_dp(values):
    if lax.axis_size("dp") != 2:
        return lax.pmax(values, "dp")
    return jnp.maximum(values, lax.ppermute(values, "dp", [(0, 1), (1, 0)]))


def allowed_bias(position_ref, docs_all_ref, docs_own_ref):
    keys, rows = docs_all_ref.shape[0], docs_own_ref.shape[1]
    key_at = lax.broadcasted_iota(jnp.int32, (keys, rows), 0)
    row_at = lax.broadcasted_iota(jnp.int32, (keys, rows), 1) + position_ref[0]
    allowed = (key_at <= row_at) & (docs_all_ref[...] == docs_own_ref[...])
    return jnp.where(allowed, 0.0, EXCLUDED)


def attend_kernel(
    position_ref, docs_all_ref, docs_own_ref, query_ref, key_ref, value_ref,
    mix_ref, log_ref, top_ref, bias,
):
    @pl.when(pl.program_id(0) == 0)
    def _():
        bias[...] = allowed_bias(position_ref, docs_all_ref, docs_own_ref)

    rows = query_ref.shape[0]
    mixes, logs, tops = [], [], []
    for head in range(query_ref.shape[1] // HEAD_DIM):
        group = head * key_ref.shape[1] // query_ref.shape[1] * HEAD_DIM
        query = query_ref[:, head * HEAD_DIM : (head + 1) * HEAD_DIM]
        key = key_ref[:, group : group + HEAD_DIM]
        value = value_ref[:, group : group + HEAD_DIM]
        scores = contract_cols(key, query) + bias[...]
        top = jnp.max(scores, axis=0, keepdims=True)
        exponent = jnp.exp(scores - top)
        totals = jnp.sum(exponent, axis=0, keepdims=True)
        probs = (exponent * (1.0 / totals)).astype(jnp.bfloat16)
        mixes.append(contract_rows(value, probs))
        logs.append(top + jnp.log(totals))
        tops.append(top)
    mix_ref[...] = jnp.concatenate(mixes, axis=0).T.astype(jnp.bfloat16)
    blank = [jnp.zeros((8 - len(logs), rows), jnp.float32)]
    log_ref[0] = jnp.concatenate(logs + blank, axis=0)
    top_ref[0] = jnp.broadcast_to(
        jnp.max(jnp.concatenate(tops + blank, axis=0), axis=1, keepdims=True), (8, 128)
    )


def attend_back_kernel(
    position_ref, docs_all_ref, docs_own_ref, query_ref, key_ref, value_ref, mix_grad_ref, log_ref,
    query_grad_ref, key_grad_ref, value_grad_ref, bias,
):
    @pl.when(pl.program_id(0) == 0)
    def _():
        bias[...] = allowed_bias(position_ref, docs_all_ref, docs_own_ref)

    query_grads, key_grads, value_grads = [], {}, {}
    for head in range(query_ref.shape[1] // HEAD_DIM):
        group = head * key_ref.shape[1] // query_ref.shape[1] * HEAD_DIM
        query = query_ref[:, head * HEAD_DIM : (head + 1) * HEAD_DIM]
        mix_grad = mix_grad_ref[:, head * HEAD_DIM : (head + 1) * HEAD_DIM]
        key = key_ref[:, group : group + HEAD_DIM]
        value = value_ref[:, group : group + HEAD_DIM]
        scores = contract_cols(key, query) + bias[...]
        probs = jnp.exp(scores - log_ref[0, head : head + 1, :])
        prob_grads = contract_cols(value, mix_grad)
        centre = jnp.sum(probs * prob_grads, axis=0, keepdims=True)
        score_grads = (probs * (prob_grads - centre)).astype(jnp.bfloat16)
        query_grads.append(contract_rows(key, score_grads))
        key_term = jnp.dot(score_grads, query, preferred_element_type=jnp.float32)
        value_term = jnp.dot(
            probs.astype(jnp.bfloat16), mix_grad, preferred_element_type=jnp.float32
        )
        key_grads[group] = key_grads[group] + key_term if group in key_grads else key_term
        value_grads[group] = value_grads[group] + value_term if group in value_grads else value_term
    query_grad_ref[...] = jnp.concatenate(query_grads, axis=0).T
    for group in key_grads:
        key_grad_ref[:, group : group + HEAD_DIM] = key_grads[group]
        value_grad_ref[:, group : group + HEAD_DIM] = value_grads[group]


def attention_specs(rows, keys, query_width, key_width):
    whole = lambda shape: pl.BlockSpec(shape, lambda i: (0, 0))
    by_head = lambda count, width: pl.BlockSpec((count, width), lambda i: (0, i))
    steps = key_width // 128
    in_specs = [
        pl.BlockSpec(memory_space=pltpu.SMEM),
        whole((keys, 1)),
        whole((1, rows)),
        by_head(rows, query_width // steps),
        by_head(keys, 128),
        by_head(keys, 128),
    ]
    return steps, in_specs, by_head, pl.BlockSpec((1, 8, rows), lambda i: (i, 0, 0))


def attend(position, docs_all, docs_own, query, key, value):
    rows, query_width = query.shape
    keys, key_width = key.shape
    steps, in_specs, by_head, by_log = attention_specs(rows, keys, query_width, key_width)
    mix, logs, tops = pl.pallas_call(
        attend_kernel,
        grid=(steps,),
        in_specs=in_specs,
        out_specs=(
            by_head(rows, query_width // steps), by_log, pl.BlockSpec((1, 8, 128), lambda i: (i, 0, 0))
        ),
        out_shape=(
            jax.ShapeDtypeStruct((rows, query_width), jnp.bfloat16),
            jax.ShapeDtypeStruct((steps, 8, rows), jnp.float32),
            jax.ShapeDtypeStruct((steps, 8, 128), jnp.float32),
        ),
        scratch_shapes=[pltpu.VMEM((keys, rows), jnp.float32)],
        cost_estimate=pl.CostEstimate(
            flops=16 * rows * keys * query_width, bytes_accessed=8 * 2**20,
            transcendentals=rows * keys * QUERY_HEADS,
        ),
        compiler_params=pltpu.CompilerParams(vmem_limit_bytes=50 * 2**20),
    )(position, docs_all[:, None], docs_own[None, :], query, key, value)
    return mix, logs, tops[:, : QUERY_HEADS // steps, 0].reshape(QUERY_HEADS)


def attend_back(position, docs_all, docs_own, query, key, value, mix_grad, logs):
    rows, query_width = query.shape
    keys, key_width = key.shape
    steps, in_specs, by_head, by_log = attention_specs(rows, keys, query_width, key_width)
    wide = query_width // steps
    return pl.pallas_call(
        attend_back_kernel,
        grid=(steps,),
        in_specs=in_specs + [by_head(rows, wide), by_log],
        out_specs=(by_head(rows, wide), by_head(keys, 128), by_head(keys, 128)),
        out_shape=(
            jax.ShapeDtypeStruct((rows, query_width), jnp.float32),
            jax.ShapeDtypeStruct((keys, key_width), jnp.float32),
            jax.ShapeDtypeStruct((keys, key_width), jnp.float32),
        ),
        scratch_shapes=[pltpu.VMEM((keys, rows), jnp.float32)],
        cost_estimate=pl.CostEstimate(
            flops=40 * rows * keys * query_width, bytes_accessed=16 * 2**20,
            transcendentals=rows * keys * QUERY_HEADS,
        ),
        compiler_params=pltpu.CompilerParams(vmem_limit_bytes=50 * 2**20),
    )(position, docs_all[:, None], docs_own[None, :], query, key, value, mix_grad, logs)


def scatter_kernel(
    whole_a, whole_b, grads_ref, weights_ref, total_a, total_b, product, grads, weights, core_a, core_b, pair_a, pair_b, first_a, first_b, mid_a, mid_b,
    last_a, last_b, sums_a, sums_b, line_a, line_b,
    core_send, core_recv, first_send, first_recv, last_send, last_recv, line_send, line_recv, load_sem,
):
    half, expert, depth = lax.axis_index("dp"), lax.axis_index("expert"), lax.axis_index("shard")
    side, core = expert // 2, expert % 2
    partner = {"dp": 1 - half}
    opposite = {"expert": 2 * ((side + 1) % 2) + core}
    sibling = {"expert": 2 * side + (core + 1) % 2}
    whole, total, from_core, pair_sum = (
        (whole_a, whole_b), (total_a, total_b), (core_a, core_b), (pair_a, pair_b)
    )
    first, mid, last, sums, from_line = (
        (first_a, first_b), (mid_a, mid_b), (last_a, last_b), (sums_a, sums_b), (line_a, line_b)
    )

    def along(distance):
        return {"shard": (depth + distance) % 4}

    barrier = pltpu.get_barrier_semaphore()
    for peer in (partner, opposite, sibling, along(1), along(2), along(3)):
        pl.semaphore_signal(barrier, inc=1, device_id=peer, device_id_type=pl.DeviceIdType.MESH)
    pl.semaphore_wait(barrier, 6)

    def remote(src, dst, send, recv, to):
        return pltpu.make_async_remote_copy(
            src_ref=src, dst_ref=dst, send_sem=send, recv_sem=recv, device_id=to,
            device_id_type=pl.DeviceIdType.MESH,
        )

    def added(a, b):
        return (a.astype(jnp.float32) + b.astype(jnp.float32)).astype(jnp.bfloat16)

    def chunk(j, other_core):
        return 4 * ((half + j // 2) % 2) + 2 * ((side + j % 2) % 2) + (core + other_core) % 2

    def to_core(w, j):
        return remote(
            whole[w].at[chunk(j, 1)], from_core[w].at[j], core_send.at[w, j], core_recv.at[w, j], sibling
        )

    def to_first(w, k):
        j = 2 + k if w == 0 else 2 * k + 1
        return remote(
            pair_sum[w].at[j], first[w].at[k], first_send.at[w, k], first_recv.at[w, k],
            (partner, opposite)[w],
        )

    def to_last(w):
        return remote(mid[w], last[w], last_send.at[w], last_recv.at[w], (opposite, partner)[w])

    def to_line(w, zi):
        return remote(
            sums[w].at[(depth + zi) % 4], from_line[w].at[zi], line_send.at[w, zi],
            line_recv.at[w, zi], along(zi),
        )

    for j in (3, 2, 1, 0):
        for w in range(2):
            to_core(w, j).start()
    loads = [
        pltpu.make_async_copy(grads_ref, grads, load_sem.at[0]),
        pltpu.make_async_copy(weights_ref, weights, load_sem.at[1]),
    ]
    for load in loads:
        load.start()
    for j in (3, 2, 1, 0):
        for w in range(2):
            to_core(w, j).wait_recv()
            pair_sum[w][j] = added(whole[w][chunk(j, 0)], from_core[w][j])
            if j == 3:
                to_first(w, 1).start()
            if j == 2 - w:
                to_first(w, 0).start()
    for load in loads:
        load.wait()

    def columns(i, carry):
        own = pl.ds(pl.multiple_of(i * 256, 256), 256)
        product[:, own] = contract_cols(grads[...], weights[own])
        return carry

    lax.fori_loop(0, weights.shape[0] // 256, columns, 0)
    for w in range(2):
        to_first(w, 1).wait_recv()
        mid[w][...] = added(pair_sum[w][1 + w], first[w][1])
        to_last(w).start()
    share = sums_a.shape[1]
    for w in range(2):
        to_first(w, 0).wait_recv()
        to_last(w).wait_recv()
        full = (
            pair_sum[w][0].astype(jnp.float32)
            + first[w][0].astype(jnp.float32)
            + last[w][...].astype(jnp.float32)
        ).astype(jnp.bfloat16)
        for z in range(4):
            sums[w][z] = full[z * share : (z + 1) * share]
        for zi in (2, 1, 3):
            to_line(w, zi).start()
    for w in range(2):
        result = sums[w][depth].astype(jnp.float32)
        for zi in (1, 3, 2):
            to_line(w, zi).wait_recv()
            result = result + from_line[w][zi].astype(jnp.float32)
        total[w][...] = result
    for w in range(2):
        for j in range(4):
            to_core(w, j).wait_send()
        for k in range(2):
            to_first(w, k).wait_send()
        to_last(w).wait_send()
        for zi in range(1, 4):
            to_line(w, zi).wait_send()


def scatter_every(grads, weights, *arrays):
    if lax.axis_size("dp") != 2:
        return [
            lax.psum_scatter(a, EVERY, scatter_dimension=0, tiled=True).astype(jnp.float32)
            for a in arrays
        ] + [contract_cols(grads, weights)]
    rows, low, dma = arrays[0].shape[0] // 8, arrays[0].dtype, pltpu.SemaphoreType.DMA
    widths = [a.shape[1] for a in arrays]
    both = lambda *shape: [pltpu.VMEM((*shape, w), low) for w in widths]
    in_vmem = pl.BlockSpec(memory_space=pltpu.VMEM)
    return pl.pallas_call(
        scatter_kernel,
        out_shape=tuple(jax.ShapeDtypeStruct((rows // 4, w), jnp.float32) for w in widths)
        + (jax.ShapeDtypeStruct((grads.shape[0], weights.shape[0]), jnp.float32),),
        in_specs=[in_vmem] * 2 + [pl.BlockSpec(memory_space=pl.ANY)] * 2,
        out_specs=(in_vmem,) * 3,
        scratch_shapes=[
            pltpu.VMEM(grads.shape, low),
            pltpu.VMEM(weights.shape, low),
            *both(4, rows), *both(4, rows), *both(2, rows), *both(rows), *both(rows),
            *both(4, rows // 4), *both(4, rows // 4),
            dma((2, 4)), dma((2, 4)), dma((2, 2)), dma((2, 2)), dma((2,)), dma((2,)),
            dma((2, 4)), dma((2, 4)), dma((2,)),
        ],
        compiler_params=pltpu.CompilerParams(
            collective_id=2, has_side_effects=True, vmem_limit_bytes=58 * 2**20
        ),
    )(*[a.reshape(8, rows, a.shape[1]) for a in arrays], grads, weights)


def gather_dp(rows):
    if lax.axis_size("dp") != 2:
        return lax.all_gather(rows, "dp", axis=0, tiled=True)
    other = lax.ppermute(rows, "dp", [(0, 1), (1, 0)])
    early = lax.axis_index("dp") == 0
    return jnp.concatenate(
        [jnp.where(early, rows, other), jnp.where(early, other, rows)], axis=0
    )


def scatter_dp(whole, dim):
    if lax.axis_size("dp") != 2:
        return lax.psum_scatter(
            whole.astype(jnp.bfloat16), "dp", scatter_dimension=dim, tiled=True
        ).astype(jnp.float32)
    size, at = whole.shape[dim] // 2, lax.axis_index("dp")
    given = lax.dynamic_slice_in_dim(whole, (1 - at) * size, size, dim).astype(jnp.bfloat16)
    taken = lax.ppermute(given, "dp", [(0, 1), (1, 0)])
    kept = lax.dynamic_slice_in_dim(whole, at * size, size, dim)
    return kept.astype(jnp.float32) + taken.astype(jnp.float32)


def weights_kernel(first_ref, second_ref, first_full, second_full, own_sem, send_sem, recv_sem):
    pair, expert, depth = lax.axis_index("dp"), lax.axis_index("expert"), lax.axis_index("shard")
    side, core = expert // 2, expert % 2
    half = pair % 2
    partner = {"dp": pair + 1 - 2 * half}
    opposite = {"expert": 2 * ((side + 1) % 2) + core}
    sibling = {"expert": 2 * side + (core + 1) % 2}
    rows = first_ref.shape[0]
    part = rows // 8
    arrays = ((first_ref, first_full), (second_ref, second_full))

    def along(distance):
        return {"shard": (depth + distance) % 4}

    barrier = pltpu.get_barrier_semaphore()
    for peer in (partner, opposite, sibling, along(1), along(2), along(3)):
        pl.semaphore_signal(barrier, inc=1, device_id=peer, device_id_type=pl.DeviceIdType.MESH)
    pl.semaphore_wait(barrier, 6)

    def eighth(px, pa, pc):
        return 4 * ((half + px) % 2) + 2 * ((side + pa) % 2) + (core + pc) % 2

    def place(full, zi, px, pa, pc):
        start = ((depth + zi) % 4) * rows + eighth(px, pa, pc) * part
        return full.at[pl.ds(pl.multiple_of(start, part), part)]

    def copy(which, zi, source, hop, to):
        px, pa, pc = source
        full = arrays[which][1]
        there = 4 * (px ^ hop[0]) + 2 * (pa ^ hop[1]) + (pc ^ hop[2])
        return pltpu.make_async_remote_copy(
            src_ref=place(full, zi, px, pa, pc),
            dst_ref=place(full, zi, px, pa, pc),
            send_sem=send_sem.at[which, zi, there],
            recv_sem=recv_sem.at[which, zi, there],
            device_id=to,
            device_id_type=pl.DeviceIdType.MESH,
        )

    def along_line(which, zi):
        own, full = arrays[which]
        start = eighth(0, 0, 0) * part
        return pltpu.make_async_remote_copy(
            src_ref=own.at[pl.ds(pl.multiple_of(start, part), part)],
            dst_ref=full.at[pl.ds(pl.multiple_of(depth * rows + start, part), part)],
            send_sem=send_sem.at[which, zi, 0],
            recv_sem=recv_sem.at[which, zi, 0],
            device_id=along(4 - zi),
            device_id_type=pl.DeviceIdType.MESH,
        )

    own_copies = [
        pltpu.make_async_copy(
            own, full.at[pl.ds(pl.multiple_of(depth * rows, rows), rows)], own_sem.at[which]
        )
        for which, (own, full) in enumerate(arrays)
    ]
    near, over, by = (1, 0, 0), (0, 1, 0), (0, 0, 1)
    for which in range(2):
        for zi in (1, 3, 2):
            along_line(which, zi).start()
    for own_copy in own_copies:
        own_copy.start()
    for which in range(2):
        for zi in (1, 3, 2):
            along_line(which, zi).wait_recv()
            copy(which, zi, (0, 0, 0), near, partner).start()
            copy(which, zi, (0, 0, 0), over, opposite).start()
            copy(which, zi, (0, 0, 0), by, sibling).start()
        for zi in (1, 3, 2):
            copy(which, zi, (0, 0, 0), near, partner).wait_recv()
            copy(which, zi, (1, 0, 0), by, sibling).start()

            @pl.when(core == 0)
            def _():
                copy(which, zi, (1, 0, 0), over, opposite).start()

            copy(which, zi, (0, 0, 0), over, opposite).wait_recv()
            copy(which, zi, (0, 1, 0), by, sibling).start()

            @pl.when(core == 1)
            def _():
                copy(which, zi, (0, 1, 0), near, partner).start()

    for which in range(2):
        for zi in (1, 3, 2):
            copy(which, zi, (1, 0, 0), over, opposite).wait_recv()
            copy(which, zi, (1, 1, 0), by, sibling).start()
    for which in range(2):
        for zi in (1, 3, 2):
            for px, pa in ((0, 0), (1, 0), (0, 1), (1, 1)):
                copy(which, zi, (px, pa, 0), by, sibling).wait()
            along_line(which, zi).wait_send()
            copy(which, zi, (0, 0, 0), near, partner).wait_send()
            copy(which, zi, (0, 0, 0), over, opposite).wait_send()

            @pl.when(core == 0)
            def _():
                copy(which, zi, (1, 0, 0), over, opposite).wait_send()

            @pl.when(core == 1)
            def _():
                copy(which, zi, (0, 1, 0), near, partner).wait_send()

    for own_copy in own_copies:
        own_copy.wait()


def gather_weights(first, second):
    anywhere = pl.BlockSpec(memory_space=pl.ANY)
    dma = pltpu.SemaphoreType.DMA
    return pl.pallas_call(
        weights_kernel,
        out_shape=tuple(
            jax.ShapeDtypeStruct((4 * part.shape[0], part.shape[1]), part.dtype)
            for part in (first, second)
        ),
        in_specs=[anywhere] * 2,
        out_specs=(anywhere,) * 2,
        scratch_shapes=[dma((2,)), dma((2, 4, 8)), dma((2, 4, 8))],
        compiler_params=pltpu.CompilerParams(collective_id=1, has_side_effects=True),
    )(first, second)


def experts_kernel(
    in_pairs, hidden_ref, cot_ref, router_ref, win_ref, wout_ref,
    rows_ref, kept_ref, core_ref, across_ref, near_ref, far_ref, stage_ref, out_ref, dwin_ref, dwout_ref, taken_in, taken_out,
    acc_in, acc_out, win, wout, router, row_tile, cot_tile, made, out_tile, parts,
    load_sem, tile_sem, row_recv, core_send, across_send, line_send,
    made_sem, part_sem, core_recv, across_recv, near_recv, far_recv,
    stage_sem, stage_send, store_sem, out_sem, given_sem, taken_sem,
):
    own_count, width = wout_ref.shape[0], wout_ref.shape[1]
    rows_own, model = hidden_ref.shape[0] - 16, hidden_ref.shape[1]
    tile = rows_own // 2
    expert, depth = lax.axis_index("expert"), lax.axis_index("shard")
    side, core = expert // 2, expert % 2
    sibling = {"expert": 2 * side + (core + 1) % 2}
    opposite = {"expert": 2 * ((side + 1) % 2) + core}

    near = {"shard": depth + 1 - 2 * (depth % 2)}
    far = {"shard": (depth + 2) % 4}

    def remote(src, dst, send, recv, to):
        return pltpu.make_async_remote_copy(
            src_ref=src, dst_ref=dst, send_sem=send, recv_sem=recv, device_id=to,
            device_id_type=pl.DeviceIdType.MESH,
        )

    barrier = pltpu.get_barrier_semaphore()
    half = lax.axis_index("dp")
    partner = {"dp": 1 - half}
    peers = [sibling, opposite, near, far] + [partner] * in_pairs
    for peer in peers:
        pl.semaphore_signal(barrier, inc=1, device_id=peer, device_id_type=pl.DeviceIdType.MESH)
    pl.semaphore_wait(barrier, len(peers))

    loads = [
        pltpu.make_async_copy(win_ref, win, load_sem.at[0]),
        pltpu.make_async_copy(wout_ref, wout, load_sem.at[1]),
        pltpu.make_async_copy(router_ref, router, load_sem.at[2]),
    ]

    def to_sibling(src, r):
        return remote(src, rows_ref.at[r + 1], core_send.at[r // 2], row_recv.at[r + 1], sibling)

    def to_opposite(src, r):
        return remote(src, rows_ref.at[r + 2], across_send.at[r // 4], row_recv.at[r + 2], opposite)

    def to_near():
        return remote(hidden_ref, rows_ref.at[4], line_send.at[0], row_recv.at[4], near)

    def to_far():
        return remote(hidden_ref, rows_ref.at[8], line_send.at[1], row_recv.at[8], far)

    def far_to_near():
        return remote(rows_ref.at[8], rows_ref.at[12], line_send.at[2], row_recv.at[12], near)

    def own_rows():
        return pltpu.make_async_copy(hidden_ref, rows_ref.at[0], row_recv.at[0])

    to_sibling(hidden_ref, 0).start()
    to_opposite(hidden_ref, 0).start()
    to_far().start()
    own_rows().start()
    for load in loads:
        load.start()

    def arrive(r):
        @pl.when(r == 0)
        def _():
            own_rows().wait()

        @pl.when(r > 0)
        def _():
            remote(
                rows_ref.at[r], rows_ref.at[r], core_send.at[0], row_recv.at[r], sibling
            ).wait_recv()

            @pl.when(r % 2 == 0)
            def _():
                to_sibling(rows_ref.at[r], r).start()

            @pl.when(r % 4 == 0)
            def _():
                to_opposite(rows_ref.at[r], r).start()

            @pl.when(r == 8)
            def _():
                far_to_near().start()

    pair_order = (0, 1, 4, 5, 7, 6, 3, 2)

    def block_at(step):
        turn = step // 2
        place = turn // 2
        pair = 0
        for i, value in enumerate(pair_order):
            pair = pair + value * (1 - ((place + 8 - i) % 8 + 7) // 8)
        return 2 * pair + (turn + (7 - place) // 7) % 2

    def first_row(step):
        r, sub = block_at(step), step % 2
        other = 2 * ((side + (r % 4) // 2) % 2) + (core + r) % 2
        plane = 2 * ((depth // 2 + r // 8) % 2) + (depth + r // 4) % 2
        return pl.multiple_of((other * 4 + plane) * rows_own + sub * tile, tile)

    def keep_out(step):
        return pltpu.make_async_copy(
            out_tile.at[step % 2], out_ref.at[pl.ds(first_row(step), tile)], out_sem.at[step % 2]
        )

    def tiles(step):
        r, sub, slot = block_at(step), step % 2, step % 2
        start = first_row(step)
        return (
            pltpu.make_async_copy(
                rows_ref.at[r, pl.ds(pl.multiple_of(sub * tile, tile), tile)],
                row_tile.at[slot], tile_sem.at[0, slot],
            ),
            pltpu.make_async_copy(
                cot_ref.at[pl.ds(start, tile)], cot_tile.at[slot], tile_sem.at[1, slot]
            ),
        )

    acc_in[...] = jnp.zeros_like(acc_in)
    acc_out[...] = jnp.zeros_like(acc_out)
    arrive(1)
    for copy in tiles(0):
        copy.start()
    for load in loads:
        load.wait()

    def send_made(step):
        r, sub, slot = block_at(step), step % 2, step % 2
        return remote(
            made.at[slot], core_ref.at[r // 2, sub], made_sem.at[slot],
            core_recv.at[r // 2, sub], sibling,
        )

    def keep_made(step):
        r, sub, slot = block_at(step), step % 2, step % 2
        return pltpu.make_async_copy(made.at[slot], kept_ref.at[r // 2, sub], made_sem.at[slot])

    def made_done(step):
        away = block_at(step) % 2

        @pl.when(away == 1)
        def _():
            send_made(step).wait_send()

        @pl.when(away == 0)
        def _():
            keep_made(step).wait()

    def send_across(zi, slot, sub):
        return remote(
            stage_ref.at[slot, sub], across_ref.at[zi, sub], stage_send.at[slot, sub],
            across_recv.at[zi, sub], opposite,
        )

    def send_near(zi, slot, sub):
        return remote(
            stage_ref.at[slot, sub], near_ref.at[zi // 2, sub], stage_send.at[slot, sub],
            near_recv.at[zi // 2, sub], near,
        )

    def send_far(sub):
        return remote(
            stage_ref.at[5, sub], far_ref.at[sub], stage_send.at[5, sub], far_recv.at[sub], far
        )

    def staged(slot, sub):
        return pltpu.make_async_copy(parts.at[0], stage_ref.at[slot, sub], stage_sem.at[0])

    def core_arrived(pair, sub):
        remote(
            made.at[0], core_ref.at[pair, sub], made_sem.at[0], core_recv.at[pair, sub], sibling
        ).wait_recv()

    def fetch(source, place):
        return pltpu.make_async_copy(source, parts.at[place], part_sem.at[place])

    def begin_one(kind, zi, sub):
        pair = 2 * zi + (1 if kind == "y" else 0)
        core_arrived(pair, sub)
        fetch(kept_ref.at[pair, sub], 0).start()
        fetch(core_ref.at[pair, sub], 1).start()
        if kind != "y":
            send_across(zi, 0, sub).wait_recv()
            fetch(across_ref.at[zi, sub], 2).start()
        if kind == "d":
            send_near(zi, 0, sub).wait_recv()
            fetch(near_ref.at[zi // 2, sub], 3).start()

    def end_one(kind, zi, slot, sub):
        pair = 2 * zi + (1 if kind == "y" else 0)
        fetch(kept_ref.at[pair, sub], 0).wait()
        fetch(core_ref.at[pair, sub], 1).wait()
        total = parts[0].astype(jnp.float32) + parts[1].astype(jnp.float32)
        if kind != "y":
            fetch(across_ref.at[zi, sub], 2).wait()
            total = total + parts[2].astype(jnp.float32)
        if kind == "d":
            fetch(near_ref.at[zi // 2, sub], 3).wait()
            total = total + parts[3].astype(jnp.float32)
        parts[0] = total.astype(jnp.bfloat16)
        staged(slot, sub).start()

    def send_one(kind, zi, slot, sub):
        staged(slot, sub).wait()
        if kind == "y":
            send_across(zi, slot, sub).start()
        if kind == "c":
            send_near(zi, slot, sub).start()
        if kind == "d":
            send_far(sub).start()

    between = (("y", 16, 2, 1), ("y", 20, 3, 0), ("y", 22, 0, 4), ("c", 26, 3, 2), ("y", 28, 1, 3), ("d", 30, 2, 5))
    after_all = (("c", 1, 6),)

    def at_stage(step, act):
        for kind, begin, zi, slot in between:
            @pl.when((step == begin) | (step == begin + 1))
            def _():
                act(kind, zi, slot)

    first = (expert * 4 + depth) * own_count

    def body(step, carry):
        slot, sub = step % 2, step % 2
        for copy in tiles(step):
            copy.wait()

        @pl.when(step < 31)
        def _():
            after = block_at(step + 1)

            @pl.when((step % 2 == 1) & ((after % 4 != 0) | (after == 0)))
            def _():
                arrive(after)

            @pl.when(step == 10)
            def _():
                to_near().start()

            for early, r in ((7, 8), (11, 12), (16, 4)):
                @pl.when(step == early)
                def _():
                    arrive(jnp.int32(r))

            for copy in tiles(step + 1):
                copy.start()

        at_stage(step - 1, lambda kind, zi, slot: send_one(kind, zi, slot, 1 - sub))
        at_stage(step, lambda kind, zi, slot: begin_one(kind, zi, sub))

        @pl.when(step >= 2)
        def _():
            made_done(step - 2)
            keep_out(step - 2).wait()

        rows, cot = row_tile[slot], cot_tile[slot, :, :model]
        logits = jnp.dot(rows, router[...], preferred_element_type=jnp.float32)
        lanes = lax.broadcasted_iota(jnp.int32, logits.shape, 1)
        routes = cot_tile[slot, :, model:].astype(jnp.float32).astype(jnp.int32)
        picked = lanes == routes[:, 0:1]
        for k in range(1, TOP):
            picked = picked | (lanes == routes[:, k : k + 1])
        gates = masked_softmax(logits, picked)
        out_sum = grad_sum = None
        gate_lanes = lax.broadcasted_iota(jnp.int32, (tile, 128), 1)
        gate_grads = jnp.zeros((tile, 128), jnp.float32)
        for e in range(own_count):
            gate = jnp.sum(jnp.where(lanes == first + e, gates, 0.0), axis=1, keepdims=True)
            both = jnp.dot(rows, win[e], preferred_element_type=jnp.float32)
            gate_part, up_part = both[:, :width], both[:, width:]
            sig = jax.nn.sigmoid(gate_part)
            activated = gate_part * sig
            hidden = (activated * up_part).astype(jnp.bfloat16).astype(jnp.float32)
            gated = (gate * hidden).astype(jnp.bfloat16)
            term = jnp.dot(gated, wout[e], preferred_element_type=jnp.float32)
            out_sum = term if out_sum is None else out_sum + term
            plain = contract_cols(cot, wout[e])
            own_grad = jnp.sum(plain * hidden, axis=1, keepdims=True)
            high = own_grad.astype(jnp.bfloat16).astype(jnp.float32)
            gate_grads = jnp.where(gate_lanes == first + e, high, gate_grads)
            gate_grads = jnp.where(gate_lanes == 64 + first + e, own_grad - high, gate_grads)
            back = gate * plain
            d_gate = back * up_part * sig * (1.0 + gate_part * (1.0 - sig))
            d_up = back * activated
            d_both = jnp.concatenate([d_gate, d_up], axis=1).astype(jnp.bfloat16)
            term = contract_cols(d_both, win[e])
            grad_sum = term if grad_sum is None else grad_sum + term
            acc_in[e] += contract_rows(rows, d_both)
            acc_out[e] += contract_rows(gated, cot)
        made[slot, :, :model] = grad_sum.astype(jnp.bfloat16)
        made[slot, :, model:] = gate_grads.astype(jnp.bfloat16)
        out_tile[slot] = out_sum.astype(jnp.bfloat16)
        keep_out(step).start()

        away = block_at(step) % 2

        @pl.when(away == 1)
        def _():
            send_made(step).start()

        @pl.when(away == 0)
        def _():
            keep_made(step).start()

        at_stage(step, lambda kind, zi, slot: end_one(kind, zi, slot, sub))
        return carry

    lax.fori_loop(0, 32, body, 0)
    win[...] = acc_in[...].astype(jnp.bfloat16)
    wout[...] = acc_out[...].astype(jnp.bfloat16)
    grads = ((acc_in, win, taken_in, dwin_ref), (acc_out, wout, taken_out, dwout_ref))

    def half_rows(ref, at):
        size = ref.shape[1] // 2
        return ref.at[:, pl.ds(pl.multiple_of(at * size, size), size)]

    def give(which):
        _, sent, taken, _ = grads[which]
        return remote(
            half_rows(sent, 1 - half), taken, given_sem.at[which], taken_sem.at[which], partner
        )

    def store(which):
        total, sent, _, result = grads[which]
        return pltpu.make_async_copy(
            half_rows(total, half) if in_pairs else sent, result, store_sem.at[which, 0]
        )

    for which in range(2):
        give(which).start() if in_pairs else store(which).start()
    send_one("d", 2, 5, 1)
    for kind, zi, slot in after_all:
        for sub in range(2):
            begin_one(kind, zi, sub)
            end_one(kind, zi, slot, sub)
            send_one(kind, zi, slot, sub)
    made_done(30)
    made_done(31)
    keep_out(30).wait()
    keep_out(31).wait()
    for sub in range(2):
        core_arrived(0, sub)
        send_across(0, 4, sub).wait()
        send_near(0, 0, sub).wait_recv()
        send_far(sub).wait()
        for zi, slot in ((2, 1), (3, 0), (1, 3)):
            send_across(zi, slot, sub).wait_send()
        send_near(3, 2, sub).wait_send()
        send_near(1, 6, sub).wait_send()
    for r in range(0, 16, 2):
        to_sibling(hidden_ref, r).wait_send()
    for r in range(0, 16, 4):
        to_opposite(hidden_ref, r).wait_send()
    to_near().wait_send()
    to_far().wait_send()
    far_to_near().wait_send()
    if in_pairs:
        for which in range(2):
            total, sent, taken, _ = grads[which]
            give(which).wait_recv()
            fetch = pltpu.make_async_copy(taken, half_rows(sent, half), load_sem.at[which])
            fetch.start()
            fetch.wait()
            size = total.shape[1] // 2
            rows = pl.ds(pl.multiple_of(half * size, size), size)
            total[:, rows] += sent[:, rows].astype(jnp.float32)
            store(which).start()
            give(which).wait_send()
    for which in range(2):
        store(which).wait()


def experts_pass(hidden, cotangent, w_router, expert_in, expert_out):
    rows_own, model = hidden.shape[0] - 16, hidden.shape[1]
    tile = rows_own // 2
    wide = model + 128
    anywhere = pl.BlockSpec(memory_space=pl.ANY)
    low = jnp.bfloat16
    kept = jax.ShapeDtypeStruct((8, 2, tile, wide), low)
    quarter = jax.ShapeDtypeStruct((4, 2, tile, wide), low)
    dma = pltpu.SemaphoreType.DMA
    in_pairs = lax.axis_size("dp") == 2
    share = lambda w: (w.shape[0], w.shape[1] // 2 if in_pairs else w.shape[1], w.shape[2])
    results = pl.pallas_call(
        functools.partial(experts_kernel, in_pairs),
        out_shape=(
            jax.ShapeDtypeStruct((16, rows_own + 16, model), low),
            kept,
            kept,
            quarter,
            jax.ShapeDtypeStruct((2, 2, tile, wide), low),
            jax.ShapeDtypeStruct((2, tile, wide), low),
            jax.ShapeDtypeStruct((7, 2, tile, wide), low),
            jax.ShapeDtypeStruct((16 * rows_own, model), low),
            jax.ShapeDtypeStruct(share(expert_in), jnp.float32 if in_pairs else low),
            jax.ShapeDtypeStruct(share(expert_out), jnp.float32 if in_pairs else low),
            jax.ShapeDtypeStruct(share(expert_in), low),
            jax.ShapeDtypeStruct(share(expert_out), low),
        ),
        in_specs=[anywhere] * 5,
        out_specs=(anywhere,) * 12,
        scratch_shapes=[
            pltpu.VMEM(expert_in.shape, jnp.float32),
            pltpu.VMEM(expert_out.shape, jnp.float32),
            pltpu.VMEM(expert_in.shape, low),
            pltpu.VMEM(expert_out.shape, low),
            pltpu.VMEM(w_router.shape, low),
            pltpu.VMEM((2, tile, model), low),
            pltpu.VMEM((2, tile, cotangent.shape[1]), low),
            pltpu.VMEM((2, tile, wide), low),
            pltpu.VMEM((2, tile, model), low),
            pltpu.VMEM((4, tile, wide), low),
            dma((3,)), dma((2, 2)), dma((16,)), dma((8,)), dma((4,)), dma((3,)),
            dma((2,)), dma((4,)), dma((8, 2)), dma((4, 2)), dma((2, 2)), dma((2,)),
            dma((1,)), dma((7, 2)), dma((2, 2)), dma((2,)), dma((2,)), dma((2,)),
        ],
        compiler_params=pltpu.CompilerParams(
            collective_id=0, has_side_effects=True, vmem_limit_bytes=60 * 2**20
        ),
    )(hidden, cotangent, w_router, expert_in, expert_out)
    rows, kept, core, across, near, far, _, partial_out, *grads = results
    total = kept[0].astype(jnp.float32) + core[0].astype(jnp.float32)
    total = total + across[0].astype(jnp.float32)
    total = total + near[0].astype(jnp.float32) + far.astype(jnp.float32)
    if in_pairs:
        weight_in_grad, weight_out_grad = (grads[0],), (grads[1],)
    else:
        weight_in_grad, weight_out_grad = (scatter_dp(grads[0], 1),), (scatter_dp(grads[1], 1),)
    branch = lax.psum_scatter(partial_out, GROUP, scatter_dimension=0, tiled=True)
    summed = total.reshape(rows_own, wide)
    return summed, branch, rows[:, rows_own, :128], weight_in_grad, weight_out_grad


def on_device(
    tokens,
    cotangent,
    gain_attn,
    w_query,
    key_weight,
    value_weight,
    w_output,
    gain_ffn,
    w_router,
    expert_in,
    expert_out,
    routes,
    doc_ids,
    threshold,
):
    inputs = tokens[0].astype(jnp.float32)
    token_matrix, model_width = inputs.shape
    query_per_key = QUERY_HEADS // KEY_VALUE_HEADS
    query_width, key_width = w_query.shape[1], key_weight.shape[1]
    route_columns = jnp.pad(routes[0].astype(jnp.bfloat16), ((0, 0), (0, 128 - TOP)))
    all_cotangent = lax.all_gather(
        jnp.concatenate([cotangent[0], route_columns], axis=1), GROUP, axis=0, tiled=True
    )
    scale_attn = rms_scale(inputs)
    normed_attn = inputs * scale_attn
    hidden_attn = (normed_attn * gain_attn).astype(jnp.bfloat16)
    full_qkv, full_output = gather_weights(
        jnp.concatenate([w_query, key_weight, value_weight], axis=1), w_output
    )
    full_query = full_qkv[:, :query_width]
    full_key = full_qkv[:, query_width : query_width + key_width]
    full_value = full_qkv[:, query_width + key_width :]
    own_positions = lax.axis_index("dp") * token_matrix + jnp.arange(token_matrix)
    local_cosine, local_sine = rope_tables(own_positions, HEAD_DIM)
    projected = jnp.dot(hidden_attn, full_qkv, preferred_element_type=jnp.float32)
    query_proj = projected[:, :query_width]
    key_projected = projected[:, query_width : query_width + key_width]
    value_proj = projected[:, query_width + key_width :]
    query_rotated = (
        apply_rotary(
            query_proj.reshape(token_matrix, QUERY_HEADS, HEAD_DIM), local_cosine, local_sine
        )
        * 0.125
    ).astype(jnp.bfloat16)
    key_rotated = (
        apply_rotary(
            key_projected.reshape(token_matrix, KEY_VALUE_HEADS, HEAD_DIM), local_cosine, local_sine
        )
        .astype(jnp.bfloat16)
        .reshape(token_matrix, KEY_VALUE_HEADS * HEAD_DIM)
    )
    value_low = value_proj.astype(jnp.bfloat16)
    own_docs = doc_ids[0]
    both_gathered = gather_dp(jnp.concatenate([key_rotated, value_low], axis=1))
    gathered_keys, gathered_values = both_gathered[:, :key_width], both_gathered[:, key_width:]
    docs_all = lax.all_gather(own_docs, "dp", axis=0, tiled=True)
    attn_low, log_totals, head_max = attend(
        own_positions[:1], docs_all, own_docs, query_rotated.reshape(token_matrix, query_width),
        gathered_keys, gathered_values,
    )
    branch_attn = contract_cols(attn_low, full_output)
    residual = inputs + branch_attn
    scale_ffn = rms_scale(residual)
    normed_ffn = residual * scale_ffn
    hidden_ffn = (normed_ffn * gain_ffn).astype(jnp.bfloat16)
    expert_count = w_router.shape[1]
    router_logits = jnp.dot(hidden_ffn, w_router, preferred_element_type=jnp.float32)
    route_ids = routes[0]
    picked = (route_ids[:, :, None] == jnp.arange(expert_count)[None, None, :]).any(axis=1)
    gate_weights = masked_softmax(router_logits, picked)
    grad_out = cotangent[0].astype(jnp.float32)
    high = lax.reduce_precision(head_max, 8, 7)
    middle = lax.reduce_precision(head_max - high, 8, 7)
    in_three = jnp.concatenate([high, middle, head_max - high - middle]).astype(jnp.bfloat16)
    extra = jnp.broadcast_to(
        jnp.pad(in_three, (0, hidden_ffn.shape[1] - in_three.shape[0])), (16, hidden_ffn.shape[1])
    )
    summed, branch_ffn, maxima, in_parts, out_parts = experts_pass(
        jnp.concatenate([hidden_ffn, extra], axis=0), all_cotangent, w_router, expert_in, expert_out
    )
    model = hidden_ffn.shape[1]
    maxima = maxima.astype(jnp.float32)
    largest = jnp.max(
        maxima[:, :QUERY_HEADS]
        + maxima[:, QUERY_HEADS : 2 * QUERY_HEADS]
        + maxima[:, 2 * QUERY_HEADS : 3 * QUERY_HEADS],
        axis=0,
    )
    largest = max_dp(largest)
    grad_hidden_ffn = summed[:, :model]
    gate_cols = summed[:, model:]
    grad_gates = gate_cols[:, :expert_count] + gate_cols[:, 64 : 64 + expert_count]
    weighted = gate_weights * jnp.where(picked, grad_gates, 0.0)
    grad_logits = (
        weighted - gate_weights * jnp.sum(weighted, axis=-1, keepdims=True)
    ).astype(jnp.bfloat16)
    router_grad = contract_rows(hidden_ffn, grad_logits)
    grad_hidden_ffn = grad_hidden_ffn + contract_cols(grad_logits, w_router)
    gain_ffn_grad = jnp.sum(grad_hidden_ffn * normed_ffn, axis=0)
    grad_residual = grad_out + norm_back(grad_hidden_ffn, normed_ffn, scale_ffn, gain_ffn)
    grad_branch = grad_residual.astype(jnp.bfloat16)
    output_grad = contract_rows(grad_branch, attn_low)
    late_grads = jnp.concatenate(
        [output_grad, router_grad, as_column(gain_ffn_grad, expert_count)], axis=1
    ).astype(jnp.bfloat16)
    attention_gradient = jnp.dot(
        grad_branch, full_output, preferred_element_type=jnp.float32
    ).astype(jnp.bfloat16)
    grad_query_rows, key_gradient, value_gradient = attend_back(
        own_positions[:1], docs_all, own_docs, query_rotated.reshape(token_matrix, query_width),
        gathered_keys, gathered_values, attention_gradient, log_totals,
    )
    both_own = scatter_dp(
        jnp.concatenate([key_gradient, value_gradient], axis=1), 0
    )
    local_key_gradient, value_grad_own = both_own[:, :key_width], both_own[:, key_width:]
    key_grad_low = (
        apply_rotary(
            local_key_gradient.reshape(token_matrix, KEY_VALUE_HEADS, HEAD_DIM),
            local_cosine,
            -local_sine,
        )
        .reshape(token_matrix, KEY_VALUE_HEADS * HEAD_DIM)
        .astype(jnp.bfloat16)
    )
    value_grad_low = value_grad_own.astype(jnp.bfloat16)
    query_grad_rows = grad_query_rows.reshape(token_matrix, QUERY_HEADS, HEAD_DIM)
    query_grad_low = (
        (apply_rotary(query_grad_rows, local_cosine, -local_sine) * 0.125)
        .reshape(token_matrix, QUERY_HEADS * HEAD_DIM)
        .astype(jnp.bfloat16)
    )
    all_grad_low = jnp.concatenate([query_grad_low, key_grad_low, value_grad_low], axis=1)
    attn_sums, late_sums, grad_hidden_attn = scatter_every(
        all_grad_low, full_qkv, contract_rows(hidden_attn, all_grad_low).astype(jnp.bfloat16), late_grads
    )
    attn_sums, late_sums, branch_ffn, in_parts, out_parts = lax.optimization_barrier(
        (attn_sums, late_sums, branch_ffn, in_parts, out_parts)
    )
    out = (residual + branch_ffn.astype(jnp.float32)).astype(jnp.bfloat16)
    grad_in_shard = sum(p.astype(jnp.float32) for p in in_parts)
    grad_out_shard = sum(p.astype(jnp.float32) for p in out_parts)
    grad_inputs = grad_residual + norm_back(grad_hidden_attn, normed_attn, scale_attn, gain_attn)
    share = attn_sums.shape[0]
    first_row = (
        (lax.axis_index("dp") * lax.axis_size("expert") + lax.axis_index("expert"))
        * lax.axis_size("shard")
        + lax.axis_index("shard")
    ) * share
    own_rows = lax.dynamic_slice_in_dim(full_qkv, first_row, share, 0)
    own_gain = lax.dynamic_slice_in_dim(gain_attn, first_row, share, 0)
    gain_attn_grad = jnp.sum(own_rows.astype(jnp.float32) * attn_sums, axis=1) / own_gain
    clip_limit = threshold[0].astype(jnp.float32)
    shrink_factor = clip_limit / jnp.maximum(largest, clip_limit)
    query_scale = jnp.repeat(jnp.sqrt(shrink_factor), HEAD_DIM)
    key_shrink = jnp.repeat(
        jnp.sqrt(jnp.min(shrink_factor.reshape(KEY_VALUE_HEADS, query_per_key), axis=1)), HEAD_DIM
    )
    clipped_query = (w_query.astype(jnp.float32) * query_scale[None, :]).astype(jnp.bfloat16)
    clipped_key = (key_weight.astype(jnp.float32) * key_shrink[None, :]).astype(jnp.bfloat16)
    return (
        out[None],
        grad_inputs.astype(jnp.bfloat16)[None],
        gain_attn_grad,
        attn_sums[:, :query_width],
        attn_sums[:, query_width : query_width + key_width],
        attn_sums[:, query_width + key_width : query_width + 2 * key_width],
        late_sums[:, :query_width],
        late_sums[:, query_width + expert_count],
        late_sums[:, query_width : query_width + expert_count],
        grad_in_shard,
        grad_out_shard,
        largest,
        clipped_query,
        clipped_key,
    )


def solution(mesh):
    return jax.shard_map(
        on_device,
        mesh=mesh,
        in_specs=(
            P(("expert", "shard"), "dp", None),
            P(("expert", "shard"), "dp", None),
            P(),
            P("shard", None),
            P("shard", None),
            P("shard", None),
            P("shard", None),
            P(),
            P(),
            P(("expert", "shard"), None, None),
            P(("expert", "shard"), None, None),
            P(("expert", "shard"), "dp", None),
            P(("expert", "shard"), "dp"),
            P(),
        ),
        out_specs=(
            P(("expert", "shard"), "dp", None),
            P(("expert", "shard"), "dp", None),
            P(("dp", "expert", "shard")),
            P(("dp", "expert", "shard"), None),
            P(("dp", "expert", "shard"), None),
            P(("dp", "expert", "shard"), None),
            P(("dp", "expert", "shard"), None),
            P(("dp", "expert", "shard")),
            P(("dp", "expert", "shard"), None),
            P(("expert", "shard"), "dp", None),
            P(("expert", "shard"), "dp", None),
            P(),
            P("shard", None),
            P("shard", None),
        ),
        check_vma=False,
    )
```
